32 devices in a mesh: batch: 4 (over y, core), tile: 8 (over z, x).
Axes of the slice: x: 2, y: 2, z: 4, core: 2. Of those that a mesh axis runs over, the one named last changes fastest.
Arguments:
- embed_input: bfloat16 [4, 4, 64, 256, 64], P('batch', None, 'tile'), may hold values from -6 to 6
- piece_image: int32 [4, 4, 8, 2], P('batch'), may hold values from 0 to 63, as said below
- embed_weight: bfloat16 [3, 3, 64, 128], replicated, may hold values from -0.25 to 0.25
- embed_bias: bfloat16 [128], replicated, may hold values from -3 to 3
- embed_gain: bfloat16 [128], replicated, may hold values from 0.099609375 to 1.8984375
- embed_shift: bfloat16 [128], replicated, may hold values from -2 to 2
- first_gain: bfloat16 [128], replicated, may hold values from 0.099609375 to 1.8984375
- first_shift: bfloat16 [128], replicated, may hold values from -2 to 2
- query_weight: bfloat16 [128, 128], replicated, may hold values from -0.75 to 0.75
- query_bias: bfloat16 [128], replicated, may hold values from -2 to 2
- reduce_weight: bfloat16 [4, 4, 128, 128], replicated, may hold values from -0.125 to 0.125
- reduce_bias: bfloat16 [128], replicated, may hold values from -3 to 3
- reduce_gain: bfloat16 [128], replicated, may hold values from 0.099609375 to 1.8984375
- reduce_shift: bfloat16 [128], replicated, may hold values from -2 to 2
- key_weight: bfloat16 [128, 128], replicated, may hold values from -0.5 to 0.5
- value_weight: bfloat16 [128, 128], replicated, may hold values from -0.5 to 0.5
- value_bias: bfloat16 [128], replicated, may hold values from -0.59765625 to 0.59765625
- output_weight: bfloat16 [128, 128], replicated, may hold values from -6 to 6
- output_bias: bfloat16 [128], replicated, may hold values from -2 to 2
- second_gain: bfloat16 [128], replicated, may hold values from 0.099609375 to 1.8984375
- second_shift: bfloat16 [128], replicated, may hold values from -2 to 2
- expand_weight: bfloat16 [128, 1024], replicated, may hold values from -0.5 to 0.5
- expand_bias: bfloat16 [1024], replicated, may hold values from -2 to 2
- depth_weight: bfloat16 [3, 3, 1024], replicated, may hold values from -2 to 2
- depth_bias: bfloat16 [1024], replicated, may hold values from -2 to 2
- shrink_weight: bfloat16 [1024, 128], replicated, may hold values from -0.1875 to 0.1875
- shrink_bias: bfloat16 [128], replicated, may hold values from -2 to 2
- cotangent: bfloat16 [4, 4, 32, 128, 128], P('batch', None, 'tile'), may hold values from -6 to 6
Outputs:
- block_output: bfloat16 [4, 4, 32, 128, 128], P('batch', None, 'tile')
- grad_input: float32 [4, 4, 64, 256, 64], P('batch', None, 'tile')
- grad_embed_weight: float32 [3, 3, 64, 128], replicated
- grad_embed_bias: float32 [128], replicated
- grad_embed_gain: float32 [128], replicated
- grad_embed_shift: float32 [128], replicated
- grad_first_gain: float32 [128], replicated
- grad_first_shift: float32 [128], replicated
- grad_query_weight: float32 [128, 128], replicated
- grad_query_bias: float32 [128], replicated
- grad_reduce_weight: float32 [4, 4, 128, 128], replicated
- grad_reduce_bias: float32 [128], replicated
- grad_reduce_gain: float32 [128], replicated
- grad_reduce_shift: float32 [128], replicated
- grad_key_weight: float32 [128, 128], replicated
- grad_value_weight: float32 [128, 128], replicated
- grad_value_bias: float32 [128], replicated
- grad_output_weight: float32 [128, 128], replicated
- grad_output_bias: float32 [128], replicated
- grad_second_gain: float32 [128], replicated
- grad_second_shift: float32 [128], replicated
- grad_expand_weight: float32 [128, 1024], replicated
- grad_expand_bias: float32 [1024], replicated
- grad_depth_weight: float32 [3, 3, 1024], replicated
- grad_depth_bias: float32 [1024], replicated
- grad_shrink_weight: float32 [1024, 128], replicated
- grad_shrink_bias: float32 [128], replicated
The draws below stay inside these ranges and needn't reach their ends.
Inputs may be any that keep to these rules, and one draw needn't show every extreme that they name: piece_image[g, s, t, h] numbers the image held by half h (the left or right 128/2 section-2 columns) of tile t's 4 rows in slot column s of group g. A slot column holds either one image on all tiles and both halves, or four images: one per half and per upper or lower tiles, the upper ones being tiles 0 to b - 1 for a b from 1 to 7 drawn for that column. Each group has at least one column with one image and at least one with four, at places drawn from the seed. Numbers of different slot columns and groups are distinct, running from 0 to 63.
All inputs are finite; a program needn't handle non-finite values.
Results may differ from the reference program's by a relative error of at most 0.019.
Values may be sent and summed in bfloat16 or wider, within the bound.
No kernel may reach another device: no remote copies, remote signals or barrier semaphores. Data moves between devices by JAX's collectives and lax.ppermute only.
A program may use at most 128 MiB of HBM per device.

```python
import jax
import jax.numpy as jnp
from jax import lax

C0 = 64
D = 128
HEADS = 2
HID = 1024
REDUCE = 4
COLS = 128
SLOTS = 4
ROWS = 32
N_BATCH = 4
N_TILE = 8


def draw_piece_image(key, part):
    key = jax.random.fold_in(key, 7)
    kind_key, quarter_key, whole_key, border_key = jax.random.split(key, 4)
    slot_index = jnp.arange(SLOTS, dtype=jnp.int32)[None, :]
    single = jax.random.randint(kind_key, (N_BATCH, SLOTS), 0, 4) > 0
    quarter_at = jax.random.randint(quarter_key, (N_BATCH, 1), 0, SLOTS)
    whole_at = (quarter_at + 1 + jax.random.randint(whole_key, (N_BATCH, 1), 0, SLOTS - 1)) % SLOTS
    single = (single | (slot_index == whole_at)) & (slot_index != quarter_at)
    border = jax.random.randint(border_key, (N_BATCH, SLOTS), 1, N_TILE)
    base_ids = (jnp.arange(N_BATCH, dtype=jnp.int32)[:, None] * SLOTS + slot_index) * 4
    tile_index = jnp.arange(N_TILE, dtype=jnp.int32)[None, None, :]
    lower_part = (tile_index >= border[:, :, None]).astype(jnp.int32)
    side_index = jnp.arange(2, dtype=jnp.int32)
    quartered = base_ids[:, :, None, None] + side_index[None, None, None, :] + 2 * lower_part[:, :, :, None]
    whole_base = base_ids + 3 * (base_ids > 0).astype(jnp.int32)
    whole_ids = jnp.broadcast_to(whole_base[:, :, None, None], quartered.shape)
    return jnp.where(single[:, :, None, None], whole_ids, quartered).astype(jnp.int32)


def block_scale(own_key, shape, shards, least, largest):
    def one(axis_at, parts):
        heights = jax.random.uniform(jax.random.fold_in(jax.random.fold_in(own_key, 6), axis_at), (parts,), jnp.float32, least / len(shards), largest / len(shards))
        return jnp.repeat(jnp.exp(heights), shape[axis_at] // parts).reshape((-1,) + (1,) * (len(shape) - axis_at - 1))

    factor_of = one(*shards[0])
    for cut in shards[1:]:
        factor_of = factor_of * one(*cut)
    return factor_of


def scatter_about(key, dims, spread, reach, pieces=(), held_as=jnp.bfloat16):
    loudness = block_scale(key, dims, pieces, -0.22, 0.18) if pieces else 1.0
    values = jax.random.normal(key, dims, jnp.float32) * spread * loudness
    return jnp.minimum(jnp.maximum(values, -reach), reach).astype(held_as)


def setup_inputs(seed: int = 0) -> dict:
    arg_keys = jax.random.split(jax.random.key(seed), 29)
    embed_input = scatter_about(arg_keys[0], (N_BATCH, SLOTS, 2 * ROWS, 2 * COLS, C0), 1.0, 6.0, ((0, 4), (2, 8)))
    piece_image = draw_piece_image(jax.random.fold_in(arg_keys[28], 71), 0)
    embed_weight = scatter_about(arg_keys[2], (3, 3, C0, D), (9 * C0) ** -0.5, 0.25)
    embed_bias = scatter_about(arg_keys[3], (D,), 0.5, 3.0)
    embed_gain = jnp.clip(1.0 + 0.18 * jax.random.normal(arg_keys[4], (D,), jnp.float32), 0.099609375, 1.8984375).astype(jnp.bfloat16)
    embed_shift = scatter_about(arg_keys[5], (D,), 0.3, 2.0)
    first_gain = jnp.clip(1.0 + 0.18 * jax.random.normal(arg_keys[6], (D,), jnp.float32), 0.099609375, 1.8984375).astype(jnp.bfloat16)
    first_shift = scatter_about(arg_keys[7], (D,), 0.3, 2.0)
    query_weight = scatter_about(arg_keys[8], (D, D), (D // 2) ** -0.5, 0.75)
    query_bias = scatter_about(arg_keys[9], (D,), 0.3, 2.0)
    reduce_weight = scatter_about(arg_keys[10], (REDUCE, REDUCE, D, D), (REDUCE * REDUCE * D) ** -0.5, 0.125)
    reduce_bias = scatter_about(arg_keys[11], (D,), 0.5, 3.0)
    reduce_gain = jnp.clip(1.0 + 0.18 * jax.random.normal(arg_keys[12], (D,), jnp.float32), 0.099609375, 1.8984375).astype(jnp.bfloat16)
    reduce_shift = scatter_about(arg_keys[13], (D,), 0.3, 2.0)
    key_weight = scatter_about(arg_keys[14], (D, D), D ** -0.5, 0.5)
    value_weight = scatter_about(arg_keys[15], (D, D), D ** -0.5, 0.5)
    value_bias = scatter_about(arg_keys[16], (D,), 0.1, 0.59765625)
    output_weight = scatter_about(arg_keys[17], (D, D), 1.0, 6.0)
    output_bias = scatter_about(arg_keys[18], (D,), 0.3, 2.0)
    second_gain = jnp.clip(1.0 + 0.18 * jax.random.normal(arg_keys[19], (D,), jnp.float32), 0.099609375, 1.8984375).astype(jnp.bfloat16)
    second_shift = scatter_about(arg_keys[20], (D,), 0.3, 2.0)
    expand_weight = scatter_about(arg_keys[21], (D, HID), D ** -0.5, 0.5)
    expand_bias = scatter_about(arg_keys[22], (HID,), 0.3, 2.0)
    depth_weight = scatter_about(arg_keys[23], (3, 3, HID), 9 ** -0.5, 2.0)
    depth_bias = scatter_about(arg_keys[24], (HID,), 0.3, 2.0)
    shrink_weight = scatter_about(arg_keys[25], (HID, D), HID ** -0.5, 0.1875)
    shrink_bias = scatter_about(arg_keys[26], (D,), 0.3, 2.0)
    cotangent = scatter_about(arg_keys[27], (N_BATCH, SLOTS, ROWS, COLS, D), 1.0, 6.0, ((0, 4), (2, 8)))
    return dict(embed_input=embed_input, piece_image=piece_image, embed_weight=embed_weight, embed_bias=embed_bias, embed_gain=embed_gain, embed_shift=embed_shift, first_gain=first_gain, first_shift=first_shift, query_weight=query_weight, query_bias=query_bias, reduce_weight=reduce_weight, reduce_bias=reduce_bias, reduce_gain=reduce_gain, reduce_shift=reduce_shift, key_weight=key_weight, value_weight=value_weight, value_bias=value_bias, output_weight=output_weight, output_bias=output_bias, second_gain=second_gain, second_shift=second_shift, expand_weight=expand_weight, expand_bias=expand_bias, depth_weight=depth_weight, depth_bias=depth_bias, shrink_weight=shrink_weight, shrink_bias=shrink_bias, cotangent=cotangent)


@jax.custom_vjp
def low(v):
    return lax.optimization_barrier(v.astype(jnp.bfloat16)).astype(jnp.float32)

@jax.custom_vjp
def low_back(v):
    return v

def low_keep(v):
    return (low(v), None)

def low_pass(kept, grad):
    return (grad,)

def back_keep(v):
    return (v, None)

def back_low(kept, grad):
    return (low(grad),)
low.defvjp(low_keep, low_pass)
low_back.defvjp(back_keep, back_low)
HIGHEST = lax.Precision.HIGHEST

def layer_norm(values, norm_gain, norm_shift, epsilon):
    row_mean = lax.optimization_barrier(jnp.mean(values, axis=-1, keepdims=True))
    centered = values - row_mean
    variance = lax.optimization_barrier(jnp.mean(centered * centered, axis=-1, keepdims=True))
    return centered * lax.rsqrt(variance + epsilon) * norm_gain + norm_shift

def cell_ids(piece_ids, row_repeat, col_repeat):
    return jnp.repeat(jnp.repeat(piece_ids, row_repeat, axis=0), col_repeat, axis=1)

def attention(queries, key_rows, values, query_ids, key_ids):
    head_size = D // HEADS
    score_scale = head_size ** (-0.5)
    key_heads = key_rows.reshape(-1, HEADS, head_size)
    value_heads = values.reshape(-1, HEADS, head_size)

    def one_block(block_pair):
        query_block, id_block = block_pair
        scores = low_back(jnp.einsum('qhd,khd->hqk', query_block, key_heads, precision=HIGHEST) * score_scale)
        scores = jnp.where((id_block[:, None] == key_ids[None, :])[None], scores, -1e+30)
        row_max = lax.optimization_barrier(jnp.max(scores, axis=-1, keepdims=True))
        weights = jnp.exp(scores - row_max)
        probs = low(weights / lax.optimization_barrier(jnp.sum(weights, axis=-1, keepdims=True)))
        return jnp.einsum('hqk,khd->qhd', probs, value_heads, precision=HIGHEST).reshape(-1, D)
    query_count = queries.shape[0]
    blocked = lax.map(jax.checkpoint(one_block), (queries.reshape(-1, 512, HEADS, head_size), query_ids.reshape(-1, 512)))
    return low(low_back(blocked.reshape(query_count, D)))

def column_forward(params, image, piece_ids):
    embed_weight, embed_bias, embed_gain, embed_shift, first_gain, first_shift, query_weight, query_bias, reduce_weight, reduce_bias, reduce_gain, reduce_shift, key_weight, value_weight, value_bias, output_weight, output_bias, second_gain, second_shift, expand_weight, expand_bias, depth_weight, depth_bias, shrink_weight, shrink_bias = params
    height = REDUCE * N_TILE
    ids_in = jnp.pad(cell_ids(piece_ids, 2 * REDUCE, COLS), 1, constant_values=-1)
    ids_mid = cell_ids(piece_ids, REDUCE, COLS // 2)
    padded = jnp.pad(image, ((1, 1), (1, 1), (0, 0)))
    embed_sum = embed_bias
    for row_tap in range(3):
        for col_tap in range(3):
            window = padded[row_tap:row_tap + 2 * height:2, col_tap:col_tap + 2 * COLS:2]
            inside = ids_in[row_tap:row_tap + 2 * height:2, col_tap:col_tap + 2 * COLS:2] == ids_mid
            embed_sum = embed_sum + jnp.einsum('rci,io->rco', jnp.where(inside[:, :, None], window, 0.0), embed_weight[row_tap, col_tap], precision=HIGHEST)
    embed_sum = low_back(embed_sum)
    stream = layer_norm(embed_sum, embed_gain, embed_shift, 1e-05)
    normed = low(layer_norm(stream, first_gain, first_shift, 1e-06))
    queries = low(low_back(jnp.einsum('rci,io->rco', normed, query_weight, precision=HIGHEST) + query_bias))
    blocks = normed.reshape(height // REDUCE, REDUCE, COLS // REDUCE, REDUCE, D)
    reduced = low_back(jnp.einsum('pacbi,abio->pco', blocks, reduce_weight, precision=HIGHEST) + reduce_bias)
    reduced_norm = low(layer_norm(reduced, reduce_gain, reduce_shift, 1e-06))
    key_rows = low(jnp.einsum('pci,io->pco', reduced_norm, key_weight, precision=HIGHEST))
    values = low(jnp.einsum('pci,io->pco', reduced_norm, value_weight, precision=HIGHEST) + value_bias)
    key_ids = ids_mid[::REDUCE, ::REDUCE].reshape(-1)
    attended = attention(queries.reshape(height * COLS, D), key_rows.reshape(-1, D), values.reshape(-1, D), ids_mid.reshape(-1), key_ids)
    branch = low_back(jnp.dot(attended, output_weight, precision=HIGHEST) + output_bias)
    stream = stream + branch.reshape(height, COLS, D)
    normed_two = low(layer_norm(stream, second_gain, second_shift, 1e-06))
    hidden = low(low_back(jnp.einsum('rci,io->rco', normed_two, expand_weight, precision=HIGHEST) + expand_bias))
    ids_pad = jnp.pad(ids_mid, 1, constant_values=-1)
    hidden_pad = jnp.pad(hidden, ((1, 1), (1, 1), (0, 0)))
    conv_sum = depth_bias
    for row_tap in range(3):
        for col_tap in range(3):
            inside = ids_pad[row_tap:row_tap + height, col_tap:col_tap + COLS] == ids_mid
            conv_sum = conv_sum + jnp.where(inside[:, :, None], hidden_pad[row_tap:row_tap + height, col_tap:col_tap + COLS], 0.0) * depth_weight[row_tap, col_tap]
    active = low(jax.nn.gelu(conv_sum, approximate=False))
    return stream + jnp.einsum('rci,io->rco', active, shrink_weight, precision=HIGHEST) + shrink_bias

def reference(embed_input, piece_image, embed_weight, embed_bias, embed_gain, embed_shift, first_gain, first_shift, query_weight, query_bias, reduce_weight, reduce_bias, reduce_gain, reduce_shift, key_weight, value_weight, value_bias, output_weight, output_bias, second_gain, second_shift, expand_weight, expand_bias, depth_weight, depth_bias, shrink_weight, shrink_bias, cotangent):
    params = tuple((item.astype(jnp.float32) for item in (embed_weight, embed_bias, embed_gain, embed_shift, first_gain, first_shift, query_weight, query_bias, reduce_weight, reduce_bias, reduce_gain, reduce_shift, key_weight, value_weight, value_bias, output_weight, output_bias, second_gain, second_shift, expand_weight, expand_bias, depth_weight, depth_bias, shrink_weight, shrink_bias)))
    images = embed_input.astype(jnp.float32).reshape(N_BATCH * SLOTS, 2 * REDUCE * N_TILE, 2 * COLS, C0)
    columns = piece_image.reshape(N_BATCH * SLOTS, N_TILE, 2).astype(jnp.int32)

    def forward(weights, inputs):

        def single(column_pair):
            return column_forward(weights, column_pair[0], column_pair[1])
        return lax.map(jax.checkpoint(single), (inputs, columns))
    output, pullback = jax.vjp(forward, params, images)
    weight_grads, input_grad = pullback(cotangent.astype(jnp.float32).reshape(output.shape))
    return (output.reshape(cotangent.shape).astype(jnp.bfloat16), input_grad.reshape(embed_input.shape), weight_grads[0], weight_grads[1], weight_grads[2], weight_grads[3], weight_grads[4], weight_grads[5], weight_grads[6], weight_grads[7], weight_grads[8], weight_grads[9], weight_grads[10], weight_grads[11], weight_grads[12], weight_grads[13], weight_grads[14], weight_grads[15], weight_grads[16], weight_grads[17], weight_grads[18], weight_grads[19], weight_grads[20], weight_grads[21], weight_grads[22], weight_grads[23], weight_grads[24])
```

```python
import math
from functools import partial

import jax
import jax.numpy as jnp
from jax import lax
from jax.experimental import pallas as pl
from jax.experimental.pallas import tpu as pltpu
from jax.sharding import PartitionSpec as P

HEADS = 2
REDUCE = 4
F32 = jnp.float32
BF16 = jnp.bfloat16
HIGHEST = lax.Precision.HIGHEST
LOG2E = math.log2(math.e)
VMEM_BYTES = 56 * 1024 * 1024

(
    EMBED_BIAS,
    EMBED_GAIN,
    EMBED_SHIFT,
    FIRST_GAIN,
    FIRST_SHIFT,
    QUERY_BIAS,
    REDUCE_BIAS,
    REDUCE_GAIN,
    REDUCE_SHIFT,
    VALUE_BIAS,
    OUTPUT_BIAS,
    SECOND_GAIN,
    SECOND_SHIFT,
    SHRINK_BIAS,
) = range(14)
VECTORS = 16
HIDDEN_VECTORS = 16

HALF_PAD = 8


def nn(left, right, precision=None):
    return lax.dot_general(
        left, right, (((1,), (0,)), ((), ())), precision=precision, preferred_element_type=F32
    )


def nt(left, right, precision=None):
    return lax.dot_general(
        left, right, (((1,), (1,)), ((), ())), precision=precision, preferred_element_type=F32
    )


def tn(left, right, precision=None):
    return lax.dot_general(
        left, right, (((0,), (0,)), ((), ())), precision=precision, preferred_element_type=F32
    )


def norm_stats(values, epsilon):
    centered = values - jnp.mean(values, axis=-1, keepdims=True)
    scale = lax.rsqrt(jnp.mean(centered * centered, axis=-1, keepdims=True) + epsilon)
    return centered * scale, scale


def norm_back(grad, hat, scale, gain):
    grad_hat = grad * gain
    mean_grad = jnp.mean(grad_hat, axis=-1, keepdims=True)
    mean_dot = jnp.mean(grad_hat * hat, axis=-1, keepdims=True)
    return scale * (grad_hat - mean_grad - hat * mean_dot)


def row_sum(values):
    return jnp.sum(values, axis=0, keepdims=True)


def params(vmem=VMEM_BYTES, axes=1):
    return pltpu.CompilerParams(
        vmem_limit_bytes=vmem, dimension_semantics=("arbitrary",) * axes
    )


def whole(shape):
    rank = len(shape)
    return pl.BlockSpec(tuple(shape), lambda *_: (0,) * rank)


def per_slot(shape):
    rank = len(shape)
    return pl.BlockSpec((1,) + tuple(shape[1:]), lambda s: (s,) + (0,) * (rank - 1))


def smem():
    return pl.BlockSpec(memory_space=pltpu.SMEM)


def slot_call(body, slots, inputs, outputs, scratch=(), name=None):
    kinds = {"slot": per_slot, "whole": whole}

    def spec(shape, kind):
        return smem() if kind == "smem" else kinds[kind](shape)

    return pl.pallas_call(
        body,
        grid=(slots,),
        in_specs=[spec(a.shape, k) for a, k in inputs],
        out_specs=[spec(s, k) for s, _, k in outputs],
        out_shape=[jax.ShapeDtypeStruct(s, d) for s, d, _ in outputs],
        scratch_shapes=list(scratch),
        compiler_params=params(),
        name=name,
    )(*[a for a, _ in inputs])


def embed_body(
    flags, x, top, ew, vec, rw, kw, vw,
    pairs, esum, stream, normed, blocks, reduced, kv,
    rowbuf, zbuf, nbuf, *, cols,
):
    s = pl.program_id(0)
    slots = pl.num_programs(0)
    same_sides = flags[s, 0]
    same_up = flags[s, 1]
    keys = cols // REDUCE
    lane = lax.broadcasted_iota(jnp.int32, (cols, 128), 1)
    half = x.shape[3]
    for r in range(2 * REDUCE + 1):
        row = (top[0] if r == 0 else x[0, r - 1]).astype(F32)
        rowbuf[r, :, :half] = row
        even = rowbuf[r, pl.ds(0, cols, 2), :]
        odd = rowbuf[r, pl.ds(1, cols, 2), :]
        pair = jnp.where(lane < half, even, pltpu.roll(odd, half, 1))
        if r == 0:
            pair = pair * same_up
        pairs[0, r] = pair.astype(BF16)
    total = None
    for a in range(3):
        lhs = jnp.concatenate([pairs[0, 2 * i + a] for i in range(REDUCE)], axis=0)
        main = ew[a, 1:3].reshape(2 * half, 128)
        side = jnp.concatenate([jnp.zeros_like(ew[a, 0]), ew[a, 0]], axis=0)
        part = nn(lhs, jnp.concatenate([main, side], axis=1))
        total = part if total is None else total + part
    zbuf[...] = total
    column = lax.broadcasted_iota(jnp.int32, (cols, 1), 0)
    mask = jnp.where(column == 0, 0.0, jnp.where(column == cols // 2, same_sides, 1.0))
    for i in range(REDUCE):
        z = zbuf[i * cols : (i + 1) * cols, :]
        value = z[:, :128] + pltpu.roll(z[:, 128:], 1, 0) * mask + vec[EMBED_BIAS : EMBED_BIAS + 1]
        esum[0, i * cols : (i + 1) * cols] = value
        hat, _ = norm_stats(value, 1e-05)
        st = hat * vec[EMBED_GAIN : EMBED_GAIN + 1] + vec[EMBED_SHIFT : EMBED_SHIFT + 1]
        stream[0, i * cols : (i + 1) * cols] = st
        hat, _ = norm_stats(st, 1e-06)
        nm = hat * vec[FIRST_GAIN : FIRST_GAIN + 1] + vec[FIRST_SHIFT : FIRST_SHIFT + 1]
        low = nm.astype(BF16)
        normed[0, i * cols : (i + 1) * cols] = low
        nbuf[i * cols : (i + 1) * cols, :] = low.astype(F32)
    for a in range(REDUCE):
        for b in range(REDUCE):
            at = (a * REDUCE + b) * 128
            piece = nbuf[pl.ds(a * cols + b, keys, REDUCE), :]
            blocks[pl.ds(pl.multiple_of(s * keys, keys), keys), at : at + 128] = piece.astype(BF16)

    @pl.when(s == slots - 1)
    def _():
        value = nn(blocks[...], rw[...]) + vec[REDUCE_BIAS : REDUCE_BIAS + 1]
        reduced[...] = value
        hat, _ = norm_stats(value, 1e-06)
        rn = (hat * vec[REDUCE_GAIN : REDUCE_GAIN + 1] + vec[REDUCE_SHIFT : REDUCE_SHIFT + 1]).astype(BF16)
        kv[:, :128] = nn(rn, kw[...]).astype(BF16)
        kv[:, 128:] = (nn(rn, vw[...]) + vec[VALUE_BIAS : VALUE_BIAS + 1]).astype(BF16)


def both_heads(pieces, at):
    rows = jnp.concatenate([p[0][:, at : at + 128] for p in pieces], axis=0)
    lane = lax.broadcasted_iota(jnp.int32, rows.shape, 1)
    zero = jnp.zeros_like(rows)
    return jnp.concatenate(
        [jnp.where(lane < 64, rows, zero), jnp.where(lane < 64, zero, rows)], axis=0
    )


def attend_body(*refs, pieces, cols):
    (normed, bias, stream, vec, qw, ow), refs = refs[:6], refs[6:]
    kvs, refs = refs[:pieces], refs[pieces:]
    queries, probs, attended, stream_two, normed_two, first_row, last_row, sbuf = refs
    q = (nn(normed[0], qw[...]) + vec[QUERY_BIAS : QUERY_BIAS + 1]).astype(BF16)
    queries[0] = q
    sbuf[...] = nt(q, both_heads(kvs, 0))
    keys = sbuf.shape[1] // HEADS
    half = cols // 2
    factor = LOG2E * (128 // HEADS) ** (-0.5)
    for i in range(REDUCE):
        for side in range(2):
            at = i * cols + side * half
            for h in range(HEADS):
                s = sbuf[at : at + half, h * keys : (h + 1) * keys] * factor + bias[0, side : side + 1]
                e = jnp.exp2(s - jnp.max(s, axis=-1, keepdims=True))
                p = e * (1.0 / jnp.sum(e, axis=-1, keepdims=True))
                probs[0, at : at + half, h * keys : (h + 1) * keys] = p.astype(BF16)
    att = nn(probs[0], both_heads(kvs, 128)).astype(BF16)
    attended[0] = att
    sbuf[:, :128] = nn(att, ow[...])
    for i in range(REDUCE):
        rows = slice(i * cols, (i + 1) * cols)
        value = stream[0, rows] + sbuf[rows, :128] + vec[OUTPUT_BIAS : OUTPUT_BIAS + 1]
        stream_two[0, rows] = value
        hat, _ = norm_stats(value, 1e-06)
        low = (hat * vec[SECOND_GAIN : SECOND_GAIN + 1] + vec[SECOND_SHIFT : SECOND_SHIFT + 1]).astype(BF16)
        normed_two[0, rows] = low
        if i == 0:
            first_row[0] = low
        if i == REDUCE - 1:
            last_row[0] = low


ERF_P = 0.3275911 / math.sqrt(2.0)
ERF_C = [0.5 * c for c in (0.254829592, -0.284496736, 1.421413741, -1.453152027, 1.061405429)]
DENSITY = 1.0 / math.sqrt(2.0 * math.pi)


def gelu_pair(x):
    t = 1.0 / (1.0 + ERF_P * jnp.abs(x))
    e = jnp.exp2((x * x) * (-0.5 * LOG2E))
    poly = t * (ERF_C[0] + t * (ERF_C[1] + t * (ERF_C[2] + t * (ERF_C[3] + t * ERF_C[4]))))
    tail = poly * e
    cdf = jnp.where(x >= 0.0, 1.0 - tail, tail)
    return x * cdf, cdf + x * e * DENSITY


def feed_body(
    flags, nt_own, nt_up, nt_down, g, stream_two, vec, hv, ew, sw,
    out, gn_own, gn_up, gn_down, dew, dsw, dhv,
    hbuf, cbuf, gabuf, abuf, ghbuf, outacc, gnacc, ext, ext_t, g_t, dsw_t,
    *, cols, width,
):
    s = pl.program_id(0)
    slots = pl.num_programs(0)
    same_sides = flags[s, 0]
    same_up = flags[s, 1]
    same_down = flags[s, 2]
    half = cols // 2
    half_pitch = half + 2 * HALF_PAD
    pitch = 2 * half_pitch
    tiles = width // 128
    hidden = ew.shape[1]
    rows_out = REDUCE * cols

    @pl.when(s == 0)
    def _():
        hbuf[...] = jnp.zeros_like(hbuf)
        cbuf[...] = jnp.zeros_like(cbuf)
        dew[...] = jnp.zeros_like(dew)
        dsw_t[...] = jnp.zeros_like(dsw_t)
        dhv[...] = jnp.zeros_like(dhv)

    ext[:cols] = nt_up[0]
    ext[cols : cols + rows_out] = nt_own[0]
    ext[cols + rows_out :] = nt_down[0]
    ext_t[...] = ext[...].T
    g_t[...] = g[0].T
    outacc[...] = jnp.zeros_like(outacc)
    gnacc[...] = jnp.zeros_like(gnacc)

    def ghosts(buf, rows):
        for t in range(tiles):
            for r in range(rows):
                base = r * pitch
                left = base + HALF_PAD + half
                right = base + half_pitch + HALF_PAD
                buf[t, left : left + 1] = buf[t, right : right + 1] * same_sides
                buf[t, right - 1 : right] = buf[t, left - 1 : left] * same_sides

    def block(b, carry):
        at = pl.multiple_of(b * width, width)
        ewb = ew[:, pl.ds(at, width)]
        swb = sw[pl.ds(at, width), :]
        hid = nn(ext[...], ewb) + hv[0:1, pl.ds(at, width)]
        for r in range(REDUCE + 2):
            for side in range(2):
                part = hid[r * cols + side * half : r * cols + (side + 1) * half]
                part = part.astype(BF16).astype(F32)
                if r == 0:
                    part = part * same_up
                if r == REDUCE + 1:
                    part = part * same_down
                base = r * pitch + side * half_pitch + HALF_PAD
                for t in range(tiles):
                    hbuf[t, base : base + half] = part[:, t * 128 : (t + 1) * 128]
        ghosts(hbuf, REDUCE + 2)
        gabuf[...] = nt(g[0], swb)

        strip = 16
        per_half = half // strip
        for t in range(tiles):
            lanes = pl.ds(pl.multiple_of(at + t * 128, 128), 128)
            taps = [[hv[2 + 3 * a + c : 3 + 3 * a + c, lanes] for c in range(3)] for a in range(3)]
            depth_bias = hv[1:2, lanes]
            sums = [jnp.zeros((8, 128), F32) for _ in range(10)]
            for k in range(2 * per_half):
                side, col = divmod(k, per_half)
                base = side * half_pitch + HALF_PAD + col * strip
                h = [
                    [hbuf[t, r * pitch + base + d - 1 : r * pitch + base + d - 1 + strip] for d in range(3)]
                    for r in range(REDUCE + 2)
                ]
                for i in range(REDUCE):
                    conv = depth_bias
                    for a in range(3):
                        for c in range(3):
                            conv = conv + h[i + a][c] * taps[a][c]
                    act, slope = gelu_pair(conv)
                    rows = slice(i * cols + side * half + col * strip, i * cols + side * half + (col + 1) * strip)
                    abuf[rows, t * 128 : (t + 1) * 128] = act.astype(BF16)
                    gc = gabuf[rows, t * 128 : (t + 1) * 128] * slope
                    cbuf[t, i * pitch + base : i * pitch + base + strip] = gc
                    for a in range(3):
                        for c in range(3):
                            prod = gc * h[i + a][c]
                            sums[1 + 3 * a + c] = sums[1 + 3 * a + c] + (prod[:8] + prod[8:])
                    sums[0] = sums[0] + (gc[:8] + gc[8:])
            for n in range(10):
                dhv[1 + n : 2 + n, lanes] += row_sum(sums[n])
        ghosts(cbuf, REDUCE)
        for t in range(tiles):
            lanes = pl.ds(pl.multiple_of(at + t * 128, 128), 128)
            taps = [[hv[2 + 3 * a + c : 3 + 3 * a + c, lanes] for c in range(3)] for a in range(3)]
            total = jnp.zeros((8, 128), F32)
            for k in range(2 * per_half):
                side, col = divmod(k, per_half)
                base = side * half_pitch + HALF_PAD + col * strip
                gc = [
                    [cbuf[t, i * pitch + base + d - 1 : i * pitch + base + d - 1 + strip] for d in range(3)]
                    for i in range(REDUCE)
                ]
                for r in range(REDUCE + 2):
                    gh = None
                    for a in range(3):
                        if not 0 <= r - a < REDUCE:
                            continue
                        for c in range(3):
                            term = gc[r - a][2 - c] * taps[a][c]
                            gh = term if gh is None else gh + term
                    if r == 0:
                        gh = gh * same_up
                    if r == REDUCE + 1:
                        gh = gh * same_down
                    total = total + (gh[:8] + gh[8:])
                    rows = slice(r * cols + side * half + col * strip, r * cols + side * half + (col + 1) * strip)
                    ghbuf[rows, t * 128 : (t + 1) * 128] = gh.astype(BF16)
            dhv[0:1, lanes] += row_sum(total)
        outacc[...] += nn(abuf[...], swb)
        gnacc[...] += nt(ghbuf[...], ewb)
        dew[:, pl.ds(at, width)] += nn(ext_t[...], ghbuf[...])
        dsw_t[:, pl.ds(at, width)] += nn(g_t[...], abuf[...])
        return carry

    lax.fori_loop(0, hidden // width, block, 0)
    out[0] = (outacc[...] + stream_two[0] + vec[SHRINK_BIAS : SHRINK_BIAS + 1]).astype(BF16)
    gn_up[0] = gnacc[:cols].astype(BF16)
    gn_own[0] = gnacc[cols : cols + rows_out]
    gn_down[0] = gnacc[cols + rows_out :].astype(BF16)

    @pl.when(s == slots - 1)
    def _():
        dsw[...] = dsw_t[...].T


def attend_back_body(*refs, pieces, cols):
    (gn, up, down, stream_two, g, attended, probs, queries, vec, ow), refs = refs[:10], refs[10:]
    kvs, refs = refs[:pieces], refs[pieces:]
    gst, gq, dow, dvec = refs[:4]
    dkvs, (gpbuf, dsbuf, branch, gabuf) = refs[4 : 4 + pieces], refs[4 + pieces :]
    s = pl.program_id(0)

    @pl.when(s == 0)
    def _():
        dow[...] = jnp.zeros_like(dow)
        dvec[...] = jnp.zeros_like(dvec)

    for i in range(REDUCE):
        rows = slice(i * cols, (i + 1) * cols)
        grad = gn[0, rows]
        if i == 0:
            grad = grad + up[0].astype(F32)
        if i == REDUCE - 1:
            grad = grad + down[0].astype(F32)
        hat, scale = norm_stats(stream_two[0, rows], 1e-06)
        dvec[SECOND_GAIN : SECOND_GAIN + 1] += row_sum(grad * hat)
        dvec[SECOND_SHIFT : SECOND_SHIFT + 1] += row_sum(grad)
        gi = g[0, rows].astype(F32)
        dvec[SHRINK_BIAS : SHRINK_BIAS + 1] += row_sum(gi)
        value = norm_back(grad, hat, scale, vec[SECOND_GAIN : SECOND_GAIN + 1]) + gi
        gst[0, rows] = value
        low = value.astype(BF16)
        branch[rows] = low
        dvec[OUTPUT_BIAS : OUTPUT_BIAS + 1] += row_sum(low.astype(F32))
    dow[...] += tn(attended[0], branch[...])
    gabuf[...] = nt(branch[...], ow[...]).astype(BF16)
    gpbuf[...] = nt(gabuf[...], both_heads(kvs, 128))
    keys = gpbuf.shape[1] // HEADS
    half = cols // 2
    for at in range(0, REDUCE * cols, half):
        for h in range(HEADS):
            span = slice(h * keys, (h + 1) * keys)
            p = probs[0, at : at + half, span].astype(F32)
            gp = gpbuf[at : at + half, span]
            inner = jnp.sum(gp * p, axis=-1, keepdims=True)
            dsbuf[at : at + half, span] = (p * (gp - inner)).astype(BF16)
    scale = (128 // HEADS) ** (-0.5)
    gql = (nn(dsbuf[...], both_heads(kvs, 0)) * scale).astype(BF16)
    gq[0] = gql
    dvec[QUERY_BIAS : QUERY_BIAS + 1] += row_sum(gql.astype(F32))

    def fold(both):
        return jnp.concatenate([both[:64, :keys], both[64:, keys:]], axis=0).T

    dk = fold(nn(queries[0].T, dsbuf[...])) * scale
    dv = fold(nn(gabuf[...].T, probs[0]))
    dkv = jnp.concatenate([dk, dv], axis=1).astype(BF16)
    each = keys // pieces
    for n in range(pieces):
        dkvs[n][0] = dkv[n * each : (n + 1) * each]


def reduce_back_body(own, arrived, reduced, blocks, vec, rw, kw, vw, gnb, drw, dkw, dvw, dvec):
    dkv = own[...] + arrived[...].astype(F32)
    dk, dv = dkv[:, :128], dkv[:, 128:]
    hat, scale = norm_stats(reduced[...], 1e-06)
    gain = vec[REDUCE_GAIN : REDUCE_GAIN + 1]
    rn = (hat * gain + vec[REDUCE_SHIFT : REDUCE_SHIFT + 1]).astype(BF16).astype(F32)
    dkw[...] = tn(rn, dk, HIGHEST)
    dvw[...] = tn(rn, dv, HIGHEST)
    grad = nt(dk, kw[...].astype(F32), HIGHEST) + nt(dv, vw[...].astype(F32), HIGHEST)
    dvec[...] = jnp.zeros_like(dvec)
    dvec[VALUE_BIAS : VALUE_BIAS + 1] = row_sum(dv)
    dvec[REDUCE_GAIN : REDUCE_GAIN + 1] = row_sum(grad * hat)
    dvec[REDUCE_SHIFT : REDUCE_SHIFT + 1] = row_sum(grad)
    low = norm_back(grad, hat, scale, gain).astype(BF16)
    dvec[REDUCE_BIAS : REDUCE_BIAS + 1] = row_sum(low.astype(F32))
    drw[...] = tn(blocks[...], low)
    gnb[...] = nt(low, rw[...])


def embed_back_body(
    flags, gnb, gq, gst, esum, normed, pairs, vec, qw,
    ge, ge_first, dqw, dew, dvec,
    gbuf, both, *, cols, half,
):
    s = pl.program_id(0)
    same_sides = flags[s, 0]
    same_up = flags[s, 1]
    keys = cols // REDUCE

    @pl.when(s == 0)
    def _():
        dqw[...] = jnp.zeros_like(dqw)
        dew[...] = jnp.zeros_like(dew)
        dvec[...] = jnp.zeros_like(dvec)

    for a in range(REDUCE):
        for b in range(REDUCE):
            at = (a * REDUCE + b) * 128
            gbuf[pl.ds(a * cols + b, keys, REDUCE), :] = gnb[:, at : at + 128]
    gbuf[...] += nt(gq[0], qw[...])
    dqw[...] += tn(normed[0], gq[0])
    column = lax.broadcasted_iota(jnp.int32, (cols, 1), 0)
    mask = jnp.where(column == cols - 1, 0.0, jnp.where(column == cols // 2 - 1, same_sides, 1.0))
    gain = vec[EMBED_GAIN : EMBED_GAIN + 1]
    gain_one = vec[FIRST_GAIN : FIRST_GAIN + 1]
    for i in range(REDUCE):
        rows = slice(i * cols, (i + 1) * cols)
        hat, scale = norm_stats(esum[0, rows], 1e-05)
        hat_one, scale_one = norm_stats(hat * gain + vec[EMBED_SHIFT : EMBED_SHIFT + 1], 1e-06)
        grad = gbuf[rows]
        dvec[FIRST_GAIN : FIRST_GAIN + 1] += row_sum(grad * hat_one)
        dvec[FIRST_SHIFT : FIRST_SHIFT + 1] += row_sum(grad)
        grad = norm_back(grad, hat_one, scale_one, gain_one) + gst[0, rows]
        dvec[EMBED_GAIN : EMBED_GAIN + 1] += row_sum(grad * hat)
        dvec[EMBED_SHIFT : EMBED_SHIFT + 1] += row_sum(grad)
        low = norm_back(grad, hat, scale, gain).astype(BF16)
        wide = low.astype(F32)
        dvec[EMBED_BIAS : EMBED_BIAS + 1] += row_sum(wide)
        if i == 0:
            ge_first[0] = (wide * same_up).astype(BF16)
        both[rows, :128] = low
        both[rows, 128:] = (pltpu.roll(wide, cols - 1, 0) * mask).astype(BF16)
    ge[0] = both[...]
    for a in range(3):
        lhs = jnp.concatenate([pairs[0, 2 * i + a] for i in range(REDUCE)], axis=0)
        part = tn(lhs, both[...])
        dew[a, 1:3] += part[:, :128].reshape(2, half, 128)
        dew[a, 0] += part[half:, 128:]


def input_back_body(flags, ge, below, ew, gx, *, cols, half):
    s = pl.program_id(0)
    same_sides = flags[s, 0]

    def spread(a, with_first):
        pad = jnp.zeros((half, 256), BF16)
        none = jnp.zeros_like(ew[a, 0])
        even = jnp.concatenate([ew[a, 1], none], axis=1)
        odd = jnp.concatenate([ew[a, 2], ew[a, 0]], axis=1)
        return jnp.concatenate([even, pad, odd, pad], axis=0)

    column = lax.broadcasted_iota(jnp.int32, (cols, 1), 0)
    mask = jnp.where(column == cols - 1, 0.0, jnp.where(column == cols // 2 - 1, same_sides, 1.0))
    under = below[0].astype(F32)
    shifted = (pltpu.roll(under, cols - 1, 0) * mask).astype(BF16)
    under = jnp.concatenate([below[0], shifted], axis=1)
    own = ge[0]
    lower = jnp.concatenate([own[cols:], under], axis=0)
    upper_rows = nt(own, spread(1, True))
    lower_rows = nt(own, spread(2, True)) + nt(lower, spread(0, True))
    for i in range(REDUCE):
        for parity, rows in ((0, upper_rows), (1, lower_rows)):
            part = rows[i * cols : (i + 1) * cols]
            gx[0, 2 * i + parity, pl.ds(0, cols, 2), :] = part[:, :half]
            gx[0, 2 * i + parity, pl.ds(1, cols, 2), :] = part[:, 128 : 128 + half]


def shifted_by(array, distance):
    count = lax.axis_size("tile")
    route = [(i, i + distance) for i in range(count) if 0 <= i + distance < count]
    return lax.ppermute(array, "tile", route)


def turned_by(array, distance):
    count = lax.axis_size("tile")
    return lax.ppermute(array, "tile", [(i, (i + distance) % count) for i in range(count)])


def swapped(array):
    count = lax.axis_size("tile")
    return lax.ppermute(array, "tile", [(i, i ^ 1) for i in range(count)])


def sum_everywhere(packed):
    batch_count, tile_count = lax.axis_size("batch"), lax.axis_size("tile")
    batch_at, tile_at = lax.axis_index("batch"), lax.axis_index("tile")
    high_batch, high_tile = batch_count // 2, tile_count // 2

    def flat(core, upper, low, high):
        return (upper * 2 + core) * tile_count + high * 2 + low

    def routes(size, place):
        result = []
        for turn in range(1, size):
            pairs = []
            for core in range(2):
                for upper in range(high_batch):
                    for low in range(2):
                        for high in range(high_tile):
                            here = (core, upper, low, high)
                            pairs.append((flat(*here), flat(*place(here, turn))))
            result.append(pairs)
        return result

    def core_place(here, turn):
        core, upper, low, high = here
        return ((core + turn) % 2, upper, low, high)

    middle = high_batch * 2

    def middle_place(here, turn):
        core, upper, low, high = here
        at = (upper * 2 + low + turn) % middle
        return (core, at // 2, at % 2, high)

    def high_place(here, turn):
        core, upper, low, high = here
        return (core, upper, low, (high + turn) % high_tile)

    levels = [
        (2, batch_at % 2, routes(2, core_place)),
        (middle, (batch_at // 2) * 2 + tile_at % 2, routes(middle, middle_place)),
        (high_tile, tile_at // 2, routes(high_tile, high_place)),
    ]
    axes = ("batch", "tile")
    value = packed
    for size, at, turns in levels:
        parts = value.reshape((size, -1, 128))
        value = lax.dynamic_index_in_dim(parts, at, 0, keepdims=False)
        sent = [
            lax.ppermute(
                lax.dynamic_index_in_dim(parts, (at + turn) % size, 0, keepdims=False).astype(BF16),
                axes,
                turns[turn - 1],
            )
            for turn in range(1, size)
        ]
        for part in sent:
            value = value + part.astype(F32)
    low = value.astype(BF16)
    for size, at, turns in reversed(levels):
        got = [low] + [lax.ppermute(low, axes, turns[turn - 1]) for turn in range(1, size)]
        order = jnp.stack(got[::-1] * 2)
        low = lax.dynamic_slice_in_dim(order, size - 1 - at, size, 0).reshape(-1, 128)
    return low.astype(F32)


def shards(
    embed_input,
    piece_image,
    embed_weight,
    embed_bias,
    embed_gain,
    embed_shift,
    first_gain,
    first_shift,
    query_weight,
    query_bias,
    reduce_weight,
    reduce_bias,
    reduce_gain,
    reduce_shift,
    key_weight,
    value_weight,
    value_bias,
    output_weight,
    output_bias,
    second_gain,
    second_shift,
    expand_weight,
    expand_bias,
    depth_weight,
    depth_bias,
    shrink_weight,
    shrink_bias,
    cotangent,
):
    source = embed_input[0]
    slots, _, wide_cols, channels = source.shape
    cols = wide_cols // 2
    cells = REDUCE * cols
    keys = cols // REDUCE
    model = embed_weight.shape[3]
    hidden = expand_weight.shape[1]
    tile_count = lax.axis_size("tile")
    tile_at = lax.axis_index("tile")
    pieces = tile_count // 2
    ids = piece_image[0]

    top = shifted_by(source[:, 2 * REDUCE - 1], 1)
    vec = jnp.stack(
        [
            embed_bias, embed_gain, embed_shift, first_gain, first_shift, query_bias, reduce_bias,
            reduce_gain, reduce_shift, value_bias, output_bias, second_gain, second_shift,
            shrink_bias, shrink_bias, shrink_bias,
        ]
    ).astype(F32)
    hv = jnp.concatenate(
        [
            expand_bias[None], depth_bias[None], depth_weight.reshape(9, hidden),
            jnp.zeros((HIDDEN_VECTORS - 11, hidden), BF16),
        ]
    ).astype(F32)
    own_ids = lax.dynamic_index_in_dim(ids, tile_at, 1, keepdims=False)
    up_ids = lax.dynamic_index_in_dim(ids, jnp.maximum(tile_at - 1, 0), 1, keepdims=False)
    down_ids = lax.dynamic_index_in_dim(
        ids, jnp.minimum(tile_at + 1, tile_count - 1), 1, keepdims=False
    )
    flags = jnp.stack(
        [
            own_ids[:, 0] == own_ids[:, 1],
            (own_ids[:, 0] == up_ids[:, 0]) & (tile_at > 0),
            (own_ids[:, 0] == down_ids[:, 0]) & (tile_at < tile_count - 1),
        ],
        axis=1,
    ).astype(F32)
    place = []
    for n in range(pieces):
        near = (tile_at - 2 * n) % tile_count
        place += [near, near ^ 1]
    key_ids = jnp.take(ids, jnp.stack(place), axis=1)
    key_ids = jnp.repeat(key_ids, keys // 2, axis=2).reshape(slots, 1, -1)
    key_bias = jnp.where(own_ids[:, :, None] == key_ids, 0.0, -1e30).astype(F32)

    kw = dict(cols=cols)
    flat_reduce = reduce_weight.reshape(-1, model)
    pairs, esum, stream, normed, blocks, reduced, kv = slot_call(
        partial(embed_body, **kw),
        slots,
        [
            (flags, "smem"), (source, "slot"), (top, "slot"), (embed_weight, "whole"),
            (vec, "whole"), (flat_reduce, "whole"), (key_weight, "whole"), (value_weight, "whole"),
        ],
        [
            ((slots, 2 * REDUCE + 1, cols, 2 * channels), BF16, "slot"),
            ((slots, cells, model), F32, "slot"),
            ((slots, cells, model), F32, "slot"),
            ((slots, cells, model), BF16, "slot"),
            ((slots * keys, REDUCE * REDUCE * model), BF16, "whole"),
            ((slots * keys, model), F32, "whole"),
            ((slots * keys, 2 * model), BF16, "whole"),
        ],
        [
            pltpu.VMEM((2 * REDUCE + 1, wide_cols, 128), F32),
            pltpu.VMEM((cells, 2 * model), F32),
            pltpu.VMEM((cells, model), F32),
        ],
        name="embed",
    )

    kv = kv.reshape(slots, keys, 2 * model)
    pair_kv = jnp.concatenate([kv, swapped(kv)], axis=1)
    kvs = [pair_kv] + [turned_by(pair_kv, 2 * n) for n in range(1, pieces)]

    all_keys = keys * tile_count
    queries, probs, attended, stream_two, normed_two, first_row, last_row = slot_call(
        partial(attend_body, pieces=pieces, **kw),
        slots,
        [
            (normed, "slot"), (key_bias, "slot"), (stream, "slot"), (vec, "whole"),
            (query_weight, "whole"), (output_weight, "whole"),
        ]
        + [(a, "slot") for a in kvs],
        [
            ((slots, cells, model), BF16, "slot"),
            ((slots, cells, HEADS * all_keys), BF16, "slot"),
            ((slots, cells, model), BF16, "slot"),
            ((slots, cells, model), F32, "slot"),
            ((slots, cells, model), BF16, "slot"),
            ((slots, cols, model), BF16, "slot"),
            ((slots, cols, model), BF16, "slot"),
        ],
        [pltpu.VMEM((cells, HEADS * all_keys), F32)],
        name="attend",
    )

    row_up = shifted_by(last_row, 1)
    row_down = shifted_by(first_row, -1)
    width = 256
    pitch = cols + 4 * HALF_PAD
    grad_out = cotangent[0].reshape(slots, cells, model)
    out, gn_own, gn_up, gn_down, d_expand, d_shrink, d_hv = slot_call(
        partial(feed_body, width=width, **kw),
        slots,
        [
            (flags, "smem"), (normed_two, "slot"), (row_up, "slot"), (row_down, "slot"),
            (grad_out, "slot"), (stream_two, "slot"), (vec, "whole"), (hv, "whole"),
            (expand_weight, "whole"), (shrink_weight, "whole"),
        ],
        [
            ((slots, cells, model), BF16, "slot"),
            ((slots, cells, model), F32, "slot"),
            ((slots, cols, model), BF16, "slot"),
            ((slots, cols, model), BF16, "slot"),
            ((model, hidden), F32, "whole"),
            ((hidden, model), F32, "whole"),
            ((HIDDEN_VECTORS, hidden), F32, "whole"),
        ],
        [
            pltpu.VMEM((width // 128, (REDUCE + 2) * pitch, 128), F32),
            pltpu.VMEM((width // 128, REDUCE * pitch, 128), F32),
            pltpu.VMEM((cells, width), F32),
            pltpu.VMEM((cells, width), BF16),
            pltpu.VMEM((cells + 2 * cols, width), BF16),
            pltpu.VMEM((cells, model), F32),
            pltpu.VMEM((cells + 2 * cols, model), F32),
            pltpu.VMEM((cells + 2 * cols, model), BF16),
            pltpu.VMEM((model, cells + 2 * cols), BF16),
            pltpu.VMEM((model, cells), BF16),
            pltpu.VMEM((model, hidden), F32),
        ],
        name="feed_forward",
    )

    from_up = shifted_by(gn_down, 1)
    from_down = shifted_by(gn_up, -1)
    results = slot_call(
        partial(attend_back_body, pieces=pieces, **kw),
        slots,
        [
            (gn_own, "slot"), (from_up, "slot"), (from_down, "slot"), (stream_two, "slot"),
            (grad_out, "slot"), (attended, "slot"), (probs, "slot"), (queries, "slot"),
            (vec, "whole"), (output_weight, "whole"),
        ]
        + [(a, "slot") for a in kvs],
        [
            ((slots, cells, model), F32, "slot"),
            ((slots, cells, model), BF16, "slot"),
            ((model, model), F32, "whole"),
            ((VECTORS, model), F32, "whole"),
        ]
        + [((slots, 2 * keys, 2 * model), BF16, "slot")] * pieces,
        [
            pltpu.VMEM((cells, HEADS * all_keys), F32),
            pltpu.VMEM((cells, HEADS * all_keys), BF16),
            pltpu.VMEM((cells, model), BF16),
            pltpu.VMEM((cells, model), BF16),
        ],
        name="attend_back",
    )
    gst, gq, d_output, dvec_a = results[:4]
    dkvs = results[4:]
    pair_sum = dkvs[0].astype(F32)
    for n in range(1, pieces):
        pair_sum = pair_sum + turned_by(dkvs[n], -2 * n).astype(F32)
    arrived = swapped(pair_sum[:, keys:].astype(BF16)).reshape(slots * keys, 2 * model)
    own_dkv = pair_sum[:, :keys].reshape(slots * keys, 2 * model)

    gnb, d_reduce, d_key, d_value, dvec_b = pl.pallas_call(
        reduce_back_body,
        out_shape=[
            jax.ShapeDtypeStruct((slots * keys, REDUCE * REDUCE * model), F32),
            jax.ShapeDtypeStruct((REDUCE * REDUCE * model, model), F32),
            jax.ShapeDtypeStruct((model, model), F32),
            jax.ShapeDtypeStruct((model, model), F32),
            jax.ShapeDtypeStruct((VECTORS, model), F32),
        ],
        compiler_params=pltpu.CompilerParams(vmem_limit_bytes=VMEM_BYTES),
        name="reduce_back",
    )(own_dkv, arrived, reduced, blocks, vec, flat_reduce, key_weight, value_weight)

    gnb_spec = pl.BlockSpec((keys, REDUCE * REDUCE * model), lambda s: (s, 0))
    grid_in = [
        (flags, smem()), (gnb, gnb_spec), (gq, per_slot(gq.shape)), (gst, per_slot(gst.shape)),
        (esum, per_slot(esum.shape)), (normed, per_slot(normed.shape)),
        (pairs, per_slot(pairs.shape)), (vec, whole(vec.shape)),
        (query_weight, whole(query_weight.shape)),
    ]
    grid_out = [
        ((slots, cells, 2 * model), BF16, per_slot),
        ((slots, cols, model), BF16, per_slot),
        ((model, model), F32, whole),
        ((3, 3, channels, model), F32, whole),
        ((VECTORS, model), F32, whole),
    ]
    ge, ge_first, d_query, d_embed, dvec_c = pl.pallas_call(
        partial(embed_back_body, half=channels, **kw),
        grid=(slots,),
        in_specs=[spec for _, spec in grid_in],
        out_specs=[make(shape) for shape, _, make in grid_out],
        out_shape=[jax.ShapeDtypeStruct(shape, dtype) for shape, dtype, _ in grid_out],
        scratch_shapes=[pltpu.VMEM((cells, model), F32), pltpu.VMEM((cells, 2 * model), BF16)],
        compiler_params=params(),
        name="embed_back",
    )(*[a for a, _ in grid_in])
    below = shifted_by(ge_first, -1)
    (grad_input,) = slot_call(
        partial(input_back_body, half=channels, **kw),
        slots,
        [(flags, "smem"), (ge, "slot"), (below, "slot"), (embed_weight, "whole")],
        [(source.shape, F32, "slot")],
        name="input_back",
    )

    dvec = dvec_a + dvec_b + dvec_c
    d_hv = d_hv.reshape(HIDDEN_VECTORS, hidden // 128, 128)
    sections = [
        d_reduce,
        d_embed.reshape(-1, model),
        d_query,
        d_key,
        d_value,
        d_output,
        d_expand.reshape(model, hidden // 128, 128).swapaxes(0, 1).reshape(-1, 128),
        d_shrink,
        d_hv.reshape(-1, 128),
        dvec,
    ]
    counts = [a.shape[0] for a in sections]
    total = sum(counts)
    padded = -(-total // 512) * 512
    packed = jnp.concatenate(sections + [jnp.zeros((padded - total, 128), F32)])
    summed = sum_everywhere(packed)
    cuts = []
    at = 0
    for count in counts:
        cuts.append(summed[at : at + count])
        at += count
    s_reduce, s_embed, s_query, s_key, s_value, s_output, s_expand, s_shrink, s_hv, s_vec = cuts
    s_hv = s_hv.reshape(HIDDEN_VECTORS, hidden)
    s_expand = s_expand.reshape(hidden // 128, model, 128).swapaxes(0, 1).reshape(model, hidden)
    return (
        out.reshape(cotangent.shape),
        grad_input[None],
        s_embed.reshape(embed_weight.shape),
        s_vec[EMBED_BIAS],
        s_vec[EMBED_GAIN],
        s_vec[EMBED_SHIFT],
        s_vec[FIRST_GAIN],
        s_vec[FIRST_SHIFT],
        s_query,
        s_vec[QUERY_BIAS],
        s_reduce.reshape(reduce_weight.shape),
        s_vec[REDUCE_BIAS],
        s_vec[REDUCE_GAIN],
        s_vec[REDUCE_SHIFT],
        s_key,
        s_value,
        s_vec[VALUE_BIAS],
        s_output,
        s_vec[OUTPUT_BIAS],
        s_vec[SECOND_GAIN],
        s_vec[SECOND_SHIFT],
        s_expand,
        s_hv[0],
        s_hv[2:11].reshape(depth_weight.shape),
        s_hv[1],
        s_shrink,
        s_vec[SHRINK_BIAS],
    )


def solution(mesh):
    shard_rows = P("batch", None, "tile", None, None)
    in_specs = (shard_rows, P("batch", None, None, None)) + (P(),) * 25 + (shard_rows,)
    out_specs = (shard_rows, shard_rows) + (P(),) * 25
    return jax.shard_map(shards, mesh=mesh, in_specs=in_specs, out_specs=out_specs, check_vma=False)
```

```python
import math
from functools import partial

import jax
import jax.numpy as jnp
from jax import lax
from jax.experimental import pallas as pl
from jax.experimental.pallas import tpu as pltpu
from jax.sharding import PartitionSpec as P

HEADS = 2
REDUCE = 4
F32 = jnp.float32
BF16 = jnp.bfloat16
HIGHEST = lax.Precision.HIGHEST
LOG2E = math.log2(math.e)
VMEM_BYTES = 56 * 1024 * 1024

(
    EMBED_BIAS,
    EMBED_GAIN,
    EMBED_SHIFT,
    FIRST_GAIN,
    FIRST_SHIFT,
    QUERY_BIAS,
    REDUCE_BIAS,
    REDUCE_GAIN,
    REDUCE_SHIFT,
    VALUE_BIAS,
    OUTPUT_BIAS,
    SECOND_GAIN,
    SECOND_SHIFT,
    SHRINK_BIAS,
) = range(14)
VECTORS = 16
HIDDEN_VECTORS = 16

HALF_PAD = 8


def nn(left, right, precision=None):
    return lax.dot_general(
        left, right, (((1,), (0,)), ((), ())), precision=precision, preferred_element_type=F32
    )


def nt(left, right, precision=None):
    return lax.dot_general(
        left, right, (((1,), (1,)), ((), ())), precision=precision, preferred_element_type=F32
    )


def tn(left, right, precision=None):
    return lax.dot_general(
        left, right, (((0,), (0,)), ((), ())), precision=precision, preferred_element_type=F32
    )


def norm_stats(values, epsilon):
    centered = values - jnp.mean(values, axis=-1, keepdims=True)
    scale = lax.rsqrt(jnp.mean(centered * centered, axis=-1, keepdims=True) + epsilon)
    return centered * scale, scale


def norm_back(grad, hat, scale, gain):
    grad_hat = grad * gain
    mean_grad = jnp.mean(grad_hat, axis=-1, keepdims=True)
    mean_dot = jnp.mean(grad_hat * hat, axis=-1, keepdims=True)
    return scale * (grad_hat - mean_grad - hat * mean_dot)


def row_sum(values):
    return jnp.sum(values, axis=0, keepdims=True)


def params(vmem=VMEM_BYTES, axes=1):
    return pltpu.CompilerParams(
        vmem_limit_bytes=vmem, dimension_semantics=("arbitrary",) * axes
    )


def whole(shape):
    rank = len(shape)
    return pl.BlockSpec(tuple(shape), lambda *_: (0,) * rank)


def per_slot(shape):
    rank = len(shape)
    return pl.BlockSpec((1,) + tuple(shape[1:]), lambda s: (s,) + (0,) * (rank - 1))


def smem():
    return pl.BlockSpec(memory_space=pltpu.SMEM)


def slot_call(body, slots, inputs, outputs, scratch=(), name=None):
    kinds = {"slot": per_slot, "whole": whole}

    def spec(shape, kind):
        return smem() if kind == "smem" else kinds[kind](shape)

    return pl.pallas_call(
        body,
        grid=(slots,),
        in_specs=[spec(a.shape, k) for a, k in inputs],
        out_specs=[spec(s, k) for s, _, k in outputs],
        out_shape=[jax.ShapeDtypeStruct(s, d) for s, d, _ in outputs],
        scratch_shapes=list(scratch),
        compiler_params=params(),
        name=name,
    )(*[a for a, _ in inputs])


def tile_ids(meta, s, tile, tiles):
    at = (s * tiles + tile) * 2
    return meta[at], meta[at + 1]


def tile_place(meta, slots, tiles):
    return meta[slots * tiles * 2]


def core_place(meta, slots, tiles):
    return meta[slots * tiles * 2 + 1]


def middle_place(meta, slots, tiles):
    return meta[slots * tiles * 2 + 2]


def as_flag(condition):
    return jnp.where(condition, 1.0, 0.0).astype(F32)


def same_flags(meta, s, slots, tiles):
    at = tile_place(meta, slots, tiles)
    own = tile_ids(meta, s, at, tiles)
    up = tile_ids(meta, s, jnp.maximum(at - 1, 0), tiles)
    down = tile_ids(meta, s, jnp.minimum(at + 1, tiles - 1), tiles)
    return (
        as_flag(own[0] == own[1]),
        as_flag((own[0] == up[0]) & (at > 0)),
        as_flag((own[0] == down[0]) & (at < tiles - 1)),
    )


def split_columns(size):
    source = lax.broadcasted_iota(jnp.int32, (size, size), 0)
    target = lax.broadcasted_iota(jnp.int32, (size, size), 1)
    wanted = jnp.where(target < size // 2, 2 * target, 2 * target - size + 1)
    return jnp.where(source == wanted, 1.0, 0.0).astype(BF16)


def embed_body(
    meta, x, top, ew, vec, rw, kw, vw,
    pairs, esum, stream, normed, blocks, reduced, kv,
    split, zbuf, nbuf, *, cols, slots, tiles,
):
    s = pl.program_id(0)
    same_sides, same_up, _ = same_flags(meta, s, slots, tiles)
    keys = cols // REDUCE
    half = x.shape[2]

    @pl.when(s == 0)
    def _():
        split[...] = split_columns(2 * cols)

    above = nn(top[0], split[...]) * same_up
    own = nn(x[0].reshape(2 * REDUCE * half, 2 * cols), split[...])
    for r in range(2 * REDUCE + 1):
        row = (above if r == 0 else own[(r - 1) * half : r * half]).astype(BF16)
        pairs[0, r, :half] = row[:, :cols]
        pairs[0, r, half:] = row[:, cols:]
    none = jnp.zeros_like(ew[0, 0])
    weights = []
    for a in range(3):
        main = ew[a, 1:3].reshape(2 * half, 128)
        side = jnp.concatenate([none, ew[a, 0]], axis=0)
        weights.append(jnp.concatenate([main, side], axis=1))
    weights = jnp.concatenate(weights, axis=0)
    column = lax.broadcasted_iota(jnp.int32, (cols, 1), 0)
    mask = jnp.where(column == 0, 0.0, jnp.where(column == cols // 2, same_sides, 1.0))
    for i in range(REDUCE):
        rows = slice(i * cols, (i + 1) * cols)
        zbuf[rows] = tn(pairs[0, 2 * i : 2 * i + 3].reshape(3 * 128, cols), weights)
    for i in range(REDUCE):
        rows = slice(i * cols, (i + 1) * cols)
        z = zbuf[rows]
        value = z[:, :128] + pltpu.roll(z[:, 128:], 1, 0) * mask + vec[EMBED_BIAS : EMBED_BIAS + 1]
        esum[0, rows] = value
        hat, _ = norm_stats(value, 1e-05)
        st = hat * vec[EMBED_GAIN : EMBED_GAIN + 1] + vec[EMBED_SHIFT : EMBED_SHIFT + 1]
        stream[0, rows] = st
        hat, _ = norm_stats(st, 1e-06)
        nm = hat * vec[FIRST_GAIN : FIRST_GAIN + 1] + vec[FIRST_SHIFT : FIRST_SHIFT + 1]
        low = nm.astype(BF16)
        normed[0, rows] = low
        nbuf[rows] = low.astype(F32)
    for a in range(REDUCE):
        for b in range(REDUCE):
            at = (a * REDUCE + b) * 128
            piece = nbuf[pl.ds(a * cols + b, keys, REDUCE), :]
            blocks[pl.ds(pl.multiple_of(s * keys, keys), keys), at : at + 128] = piece.astype(BF16)

    @pl.when(s == slots - 1)
    def _():
        value = nn(blocks[...], rw[...]) + vec[REDUCE_BIAS : REDUCE_BIAS + 1]
        reduced[...] = value
        hat, _ = norm_stats(value, 1e-06)
        rn = (hat * vec[REDUCE_GAIN : REDUCE_GAIN + 1] + vec[REDUCE_SHIFT : REDUCE_SHIFT + 1]).astype(BF16)
        kv[:, :128] = nn(rn, kw[...]).astype(BF16)
        kv[:, 128:] = (nn(rn, vw[...]) + vec[VALUE_BIAS : VALUE_BIAS + 1]).astype(BF16)


def both_heads(pieces, at):
    rows = jnp.concatenate([p[0][:, at : at + 128] for p in pieces], axis=0)
    lane = lax.broadcasted_iota(jnp.int32, rows.shape, 1)
    zero = jnp.zeros_like(rows)
    return jnp.concatenate(
        [jnp.where(lane < 64, rows, zero), jnp.where(lane < 64, zero, rows)], axis=0
    )


def key_bias(meta, s, slots, tiles, keys):
    at = tile_place(meta, slots, tiles)
    own = tile_ids(meta, s, at, tiles)
    part = keys // (2 * tiles)
    entry = lax.broadcasted_iota(jnp.int32, (1, keys), 1) // part
    rows = [jnp.zeros((1, keys), F32) for _ in range(2)]
    for n in range(tiles):
        ids = tile_ids(meta, s, at ^ n, tiles)
        for side in range(2):
            for query in range(2):
                value = jnp.where(ids[side] == own[query], 0.0, -1e30).astype(F32)
                rows[query] = jnp.where(entry == 2 * n + side, value, rows[query])
    return rows


def attend_body(*refs, pieces, cols, slots, tiles):
    (meta, normed, stream, vec, qw, ow), refs = refs[:6], refs[6:]
    kvs, refs = refs[:pieces], refs[pieces:]
    queries, probs, attended, stream_two, normed_two, first_row, last_row, sbuf = refs
    q = (nn(normed[0], qw[...]) + vec[QUERY_BIAS : QUERY_BIAS + 1]).astype(BF16)
    queries[0] = q
    sbuf[...] = nt(q, both_heads(kvs, 0))
    keys = sbuf.shape[1] // HEADS
    half = cols // 2
    factor = LOG2E * (128 // HEADS) ** (-0.5)
    bias = key_bias(meta, pl.program_id(0), slots, tiles, keys)
    for i in range(REDUCE):
        for side in range(2):
            at = i * cols + side * half
            for h in range(HEADS):
                s = sbuf[at : at + half, h * keys : (h + 1) * keys] * factor + bias[side]
                e = jnp.exp2(s - jnp.max(s, axis=-1, keepdims=True))
                p = e * (1.0 / jnp.sum(e, axis=-1, keepdims=True))
                probs[0, at : at + half, h * keys : (h + 1) * keys] = p.astype(BF16)
    att = nn(probs[0], both_heads(kvs, 128)).astype(BF16)
    attended[0] = att
    sbuf[:, :128] = nn(att, ow[...])
    for i in range(REDUCE):
        rows = slice(i * cols, (i + 1) * cols)
        value = stream[0, rows] + sbuf[rows, :128] + vec[OUTPUT_BIAS : OUTPUT_BIAS + 1]
        stream_two[0, rows] = value
        hat, _ = norm_stats(value, 1e-06)
        low = (hat * vec[SECOND_GAIN : SECOND_GAIN + 1] + vec[SECOND_SHIFT : SECOND_SHIFT + 1]).astype(BF16)
        normed_two[0, rows] = low
        if i == 0:
            first_row[0] = low
        if i == REDUCE - 1:
            last_row[0] = low


ERF_P = 0.3275911 / math.sqrt(2.0)
ERF_C = [0.5 * c for c in (0.254829592, -0.284496736, 1.421413741, -1.453152027, 1.061405429)]
DENSITY = 1.0 / math.sqrt(2.0 * math.pi)


def gelu_pair(x):
    t = 1.0 / (1.0 + ERF_P * jnp.abs(x))
    e = jnp.exp2((x * x) * (-0.5 * LOG2E))
    poly = t * (ERF_C[0] + t * (ERF_C[1] + t * (ERF_C[2] + t * (ERF_C[3] + t * ERF_C[4]))))
    tail = poly * e
    cdf = jnp.where(x >= 0.0, 1.0 - tail, tail)
    return x * cdf, cdf + x * e * DENSITY


def feed_body(
    meta, nt_own, nt_up, nt_down, g, stream_two, vec, hv, ew, sw,
    out, gn_own, gn_up, gn_down, dew, dsw, dhv,
    hbuf, cbuf, gabuf, abuf, ghbuf, outacc, gnacc, ext, ext_t, g_t, dsw_t,
    *, cols, width, slots, tiles,
):
    s = pl.program_id(0)
    same_sides, same_up, same_down = same_flags(meta, s, slots, tiles)
    half = cols // 2
    half_pitch = half + 2 * HALF_PAD
    pitch = 2 * half_pitch
    lanes_of = width // 128
    hidden = ew.shape[1]
    rows_out = REDUCE * cols

    @pl.when(s == 0)
    def _():
        hbuf[...] = jnp.zeros_like(hbuf)
        cbuf[...] = jnp.zeros_like(cbuf)
        dew[...] = jnp.zeros_like(dew)
        dsw_t[...] = jnp.zeros_like(dsw_t)
        dhv[...] = jnp.zeros_like(dhv)

    ext[:cols] = nt_up[0]
    ext[cols : cols + rows_out] = nt_own[0]
    ext[cols + rows_out :] = nt_down[0]
    ext_t[...] = ext[...].T
    g_t[...] = g[0].T
    outacc[...] = jnp.zeros_like(outacc)
    gnacc[...] = jnp.zeros_like(gnacc)

    def ghosts(buf, rows):
        for t in range(lanes_of):
            for r in range(rows):
                base = r * pitch
                left = base + HALF_PAD + half
                right = base + half_pitch + HALF_PAD
                buf[t, left : left + 1] = buf[t, right : right + 1] * same_sides
                buf[t, right - 1 : right] = buf[t, left - 1 : left] * same_sides

    def block(b, carry):
        at = pl.multiple_of(b * width, width)
        ewb = ew[:, pl.ds(at, width)]
        swb = sw[pl.ds(at, width), :]
        hid = nn(ext[...], ewb) + hv[0:1, pl.ds(at, width)]
        for r in range(REDUCE + 2):
            for side in range(2):
                part = hid[r * cols + side * half : r * cols + (side + 1) * half]
                part = part.astype(BF16).astype(F32)
                if r == 0:
                    part = part * same_up
                if r == REDUCE + 1:
                    part = part * same_down
                base = r * pitch + side * half_pitch + HALF_PAD
                for t in range(lanes_of):
                    hbuf[t, base : base + half] = part[:, t * 128 : (t + 1) * 128]
        ghosts(hbuf, REDUCE + 2)
        gabuf[...] = nt(g[0], swb)

        strip = 16
        per_half = half // strip
        for t in range(lanes_of):
            lanes = pl.ds(pl.multiple_of(at + t * 128, 128), 128)
            taps = [[hv[2 + 3 * a + c : 3 + 3 * a + c, lanes] for c in range(3)] for a in range(3)]
            depth_bias = hv[1:2, lanes]
            sums = [jnp.zeros((8, 128), F32) for _ in range(10)]
            for k in range(2 * per_half):
                side, col = divmod(k, per_half)
                base = side * half_pitch + HALF_PAD + col * strip
                h = [
                    [hbuf[t, r * pitch + base + d - 1 : r * pitch + base + d - 1 + strip] for d in range(3)]
                    for r in range(REDUCE + 2)
                ]
                for i in range(REDUCE):
                    conv = depth_bias
                    for a in range(3):
                        for c in range(3):
                            conv = conv + h[i + a][c] * taps[a][c]
                    act, slope = gelu_pair(conv)
                    rows = slice(i * cols + side * half + col * strip, i * cols + side * half + (col + 1) * strip)
                    abuf[rows, t * 128 : (t + 1) * 128] = act.astype(BF16)
                    gc = gabuf[rows, t * 128 : (t + 1) * 128] * slope
                    cbuf[t, i * pitch + base : i * pitch + base + strip] = gc
                    for a in range(3):
                        for c in range(3):
                            prod = gc * h[i + a][c]
                            sums[1 + 3 * a + c] = sums[1 + 3 * a + c] + (prod[:8] + prod[8:])
                    sums[0] = sums[0] + (gc[:8] + gc[8:])
            for n in range(10):
                dhv[1 + n : 2 + n, lanes] += row_sum(sums[n])
        ghosts(cbuf, REDUCE)
        for t in range(lanes_of):
            lanes = pl.ds(pl.multiple_of(at + t * 128, 128), 128)
            taps = [[hv[2 + 3 * a + c : 3 + 3 * a + c, lanes] for c in range(3)] for a in range(3)]
            total = jnp.zeros((8, 128), F32)
            for k in range(2 * per_half):
                side, col = divmod(k, per_half)
                base = side * half_pitch + HALF_PAD + col * strip
                gc = [
                    [cbuf[t, i * pitch + base + d - 1 : i * pitch + base + d - 1 + strip] for d in range(3)]
                    for i in range(REDUCE)
                ]
                for r in range(REDUCE + 2):
                    gh = None
                    for a in range(3):
                        if not 0 <= r - a < REDUCE:
                            continue
                        for c in range(3):
                            term = gc[r - a][2 - c] * taps[a][c]
                            gh = term if gh is None else gh + term
                    if r == 0:
                        gh = gh * same_up
                    if r == REDUCE + 1:
                        gh = gh * same_down
                    total = total + (gh[:8] + gh[8:])
                    rows = slice(r * cols + side * half + col * strip, r * cols + side * half + (col + 1) * strip)
                    ghbuf[rows, t * 128 : (t + 1) * 128] = gh.astype(BF16)
            dhv[0:1, lanes] += row_sum(total)
        outacc[...] += nn(abuf[...], swb)
        gnacc[...] += nt(ghbuf[...], ewb)
        dew[:, pl.ds(at, width)] += nn(ext_t[...], ghbuf[...])
        dsw_t[:, pl.ds(at, width)] += nn(g_t[...], abuf[...])
        return carry

    lax.fori_loop(0, hidden // width, block, 0)
    out[0] = (outacc[...] + stream_two[0] + vec[SHRINK_BIAS : SHRINK_BIAS + 1]).astype(BF16)
    gn_up[0] = gnacc[:cols].astype(BF16)
    gn_own[0] = gnacc[cols : cols + rows_out]
    gn_down[0] = gnacc[cols + rows_out :].astype(BF16)

    @pl.when(s == slots - 1)
    def _():
        dsw[...] = dsw_t[...].T


def attend_back_body(*refs, pieces, cols):
    (gn, up, down, stream_two, g, attended, probs, queries, normed, vec, ow), refs = refs[:11], refs[11:]
    kvs, refs = refs[:pieces], refs[pieces:]
    gst, gq, dow, dqw, dvec = refs[:5]
    dkvs, (gpbuf, dsbuf, branch, gabuf) = refs[5 : 5 + pieces], refs[5 + pieces :]
    s = pl.program_id(0)

    @pl.when(s == 0)
    def _():
        dow[...] = jnp.zeros_like(dow)
        dqw[...] = jnp.zeros_like(dqw)
        dvec[...] = jnp.zeros_like(dvec)

    for i in range(REDUCE):
        rows = slice(i * cols, (i + 1) * cols)
        grad = gn[0, rows]
        if i == 0:
            grad = grad + up[0].astype(F32)
        if i == REDUCE - 1:
            grad = grad + down[0].astype(F32)
        hat, scale = norm_stats(stream_two[0, rows], 1e-06)
        dvec[SECOND_GAIN : SECOND_GAIN + 1] += row_sum(grad * hat)
        dvec[SECOND_SHIFT : SECOND_SHIFT + 1] += row_sum(grad)
        gi = g[0, rows].astype(F32)
        dvec[SHRINK_BIAS : SHRINK_BIAS + 1] += row_sum(gi)
        value = norm_back(grad, hat, scale, vec[SECOND_GAIN : SECOND_GAIN + 1]) + gi
        gst[0, rows] = value
        low = value.astype(BF16)
        branch[rows] = low
        dvec[OUTPUT_BIAS : OUTPUT_BIAS + 1] += row_sum(low.astype(F32))
    dow[...] += tn(attended[0], branch[...])
    gabuf[...] = nt(branch[...], ow[...]).astype(BF16)
    gpbuf[...] = nt(gabuf[...], both_heads(kvs, 128))
    keys = gpbuf.shape[1] // HEADS
    half = cols // 2
    for at in range(0, REDUCE * cols, half):
        for h in range(HEADS):
            span = slice(h * keys, (h + 1) * keys)
            p = probs[0, at : at + half, span].astype(F32)
            gp = gpbuf[at : at + half, span]
            inner = jnp.sum(gp * p, axis=-1, keepdims=True)
            dsbuf[at : at + half, span] = (p * (gp - inner)).astype(BF16)
    scale = (128 // HEADS) ** (-0.5)
    gql = (nn(dsbuf[...], both_heads(kvs, 0)) * scale).astype(BF16)
    gq[0] = gql
    dvec[QUERY_BIAS : QUERY_BIAS + 1] += row_sum(gql.astype(F32))
    dqw[...] += tn(normed[0], gql)

    def fold(both):
        return jnp.concatenate([both[:64, :keys], both[64:, keys:]], axis=0).T

    dk = fold(nn(queries[0].T, dsbuf[...])) * scale
    dv = fold(nn(gabuf[...].T, probs[0]))
    dkv = jnp.concatenate([dk, dv], axis=1).astype(BF16)
    each = keys // pieces
    for n in range(pieces):
        dkvs[n][0] = dkv[n * each : (n + 1) * each]


def reduce_back_body(
    meta, own, arrived, reduced, blocks, vec, rw, kw, vw, dexpand, dshrink, dhv, doutput, dquery, dvec_in,
    gnb, dvec, keep, send, *, slots, tiles,
):
    upper = core_place(meta, slots, tiles) == 1

    def place(chunk, first, second):
        rows = slice(chunk * 128, (chunk + 1) * 128)
        keep[rows] = jnp.where(upper, second, first)
        send[rows] = jnp.where(upper, first, second).astype(BF16)

    dkv = own[...] + arrived[...].astype(F32)
    dk, dv = dkv[:, :128], dkv[:, 128:]
    hat, scale = norm_stats(reduced[...], 1e-06)
    gain = vec[REDUCE_GAIN : REDUCE_GAIN + 1]
    rn = (hat * gain + vec[REDUCE_SHIFT : REDUCE_SHIFT + 1]).astype(BF16).astype(F32)
    dkw = tn(rn, dk, HIGHEST)
    dvw = tn(rn, dv, HIGHEST)
    grad = nt(dk, kw[...].astype(F32), HIGHEST) + nt(dv, vw[...].astype(F32), HIGHEST)
    low = norm_back(grad, hat, scale, gain).astype(BF16)
    gnb[...] = nt(low, rw[...])
    sums = {
        VALUE_BIAS: row_sum(dv),
        REDUCE_GAIN: row_sum(grad * hat),
        REDUCE_SHIFT: row_sum(grad),
        REDUCE_BIAS: row_sum(low.astype(F32)),
    }
    dvec[...] = jnp.concatenate(
        [sums.get(n, dvec_in[n : n + 1]) for n in range(VECTORS)], axis=0
    )
    spans = dexpand.shape[1] // 128
    second = [dexpand[:, t * 128 : (t + 1) * 128] for t in range(spans)]
    second += [dshrink[t * 128 : (t + 1) * 128] for t in range(spans)]
    second += [jnp.concatenate([dhv[:, t * 128 : (t + 1) * 128] for t in range(spans)], axis=0)]
    second += [doutput[...], dquery[...]]
    first = [tn(blocks[:, t * 128 : (t + 1) * 128], low) for t in range(REDUCE * REDUCE)]
    first += [dkw, dvw, jnp.zeros((128, 128), F32)]
    for chunk, (one, two) in enumerate(zip(first, second, strict=True)):
        place(chunk, one, two)


EARLY_ROWS = 19 * 128
LATE_ROWS = 3 * 128


def embed_back_body(
    meta, gnb, gq, gst, esum, pairs, vec, qw, dvec_in,
    ge, ge_first, keep, send,
    gbuf, dew, dvec, *, cols, half, slots, tiles,
):
    s = pl.program_id(0)
    same_sides, same_up, _ = same_flags(meta, s, slots, tiles)
    keys = cols // REDUCE

    @pl.when(s == 0)
    def _():
        dew[...] = jnp.zeros_like(dew)
        dvec[...] = dvec_in[...]

    for a in range(REDUCE):
        for b in range(REDUCE):
            at = (a * REDUCE + b) * 128
            gbuf[pl.ds(a * cols + b, keys, REDUCE), :] = gnb[:, at : at + 128]
    gbuf[...] += nt(gq[0], qw[...])
    column = lax.broadcasted_iota(jnp.int32, (cols, 1), 0)
    mask = jnp.where(column == cols - 1, 0.0, jnp.where(column == cols // 2 - 1, same_sides, 1.0))
    gain = vec[EMBED_GAIN : EMBED_GAIN + 1]
    gain_one = vec[FIRST_GAIN : FIRST_GAIN + 1]
    for i in range(REDUCE):
        rows = slice(i * cols, (i + 1) * cols)
        hat, scale = norm_stats(esum[0, rows], 1e-05)
        hat_one, scale_one = norm_stats(hat * gain + vec[EMBED_SHIFT : EMBED_SHIFT + 1], 1e-06)
        grad = gbuf[rows]
        dvec[FIRST_GAIN : FIRST_GAIN + 1] += row_sum(grad * hat_one)
        dvec[FIRST_SHIFT : FIRST_SHIFT + 1] += row_sum(grad)
        grad = norm_back(grad, hat_one, scale_one, gain_one) + gst[0, rows]
        dvec[EMBED_GAIN : EMBED_GAIN + 1] += row_sum(grad * hat)
        dvec[EMBED_SHIFT : EMBED_SHIFT + 1] += row_sum(grad)
        low = norm_back(grad, hat, scale, gain).astype(BF16)
        wide = low.astype(F32)
        dvec[EMBED_BIAS : EMBED_BIAS + 1] += row_sum(wide)
        if i == 0:
            ge_first[0] = (wide * same_up).astype(BF16)
        ge[0, rows, :128] = low
        ge[0, rows, 128:] = (pltpu.roll(wide, cols - 1, 0) * mask).astype(BF16)
    for a in range(3):
        lhs = jnp.concatenate([pairs[0, 2 * i + a] for i in range(REDUCE)], axis=1)
        part = nn(lhs, ge[0])
        at = a * 3 * half
        dew[at : at + half] += part[half:, 128:]
        dew[at + half : at + 3 * half] += part[:, :128]

    @pl.when(s == slots - 1)
    def _():
        upper = core_place(meta, slots, tiles) == 1
        count = 9 * half // 2
        first, second = dew[:count], dew[count:]
        keep[:count] = jnp.where(upper, second, first)
        send[:count] = jnp.where(upper, first, second).astype(BF16)
        vectors = dvec[...]
        none = jnp.zeros_like(vectors)
        end = count + VECTORS
        keep[count:end] = jnp.where(upper, none, vectors)
        send[count:end] = jnp.where(upper, vectors, none).astype(BF16)
        keep[end:] = jnp.zeros((LATE_ROWS - end, 128), F32)
        send[end:] = jnp.zeros((LATE_ROWS - end, 128), BF16)


def input_back_body(meta, ge, below, ew, gx, split, *, cols, half, slots, tiles):
    s = pl.program_id(0)
    same_sides, _, _ = same_flags(meta, s, slots, tiles)

    @pl.when(s == 0)
    def _():
        split[...] = split_columns(2 * cols)

    none = jnp.zeros_like(ew[0, 0])

    def spread(a):
        even = jnp.concatenate([ew[a, 1], none], axis=1)
        odd = jnp.concatenate([ew[a, 2], ew[a, 0]], axis=1)
        return jnp.concatenate([even, odd], axis=0)

    column = lax.broadcasted_iota(jnp.int32, (cols, 1), 0)
    mask = jnp.where(column == cols - 1, 0.0, jnp.where(column == cols // 2 - 1, same_sides, 1.0))
    shifted = (pltpu.roll(below[0].astype(F32), cols - 1, 0) * mask).astype(BF16)
    under = jnp.concatenate([below[0], shifted], axis=1)
    own = ge[0]
    lower = jnp.concatenate([own[cols:], under], axis=0)
    upper_rows = nt(spread(1), own).astype(BF16)
    lower_rows = (nt(spread(2), own) + nt(spread(0), lower)).astype(BF16)
    lines = []
    for i in range(REDUCE):
        for rows in (upper_rows, lower_rows):
            part = rows[:, i * cols : (i + 1) * cols]
            lines.append(jnp.concatenate([part[:half], part[half:]], axis=1))
    mixed = nt(jnp.concatenate(lines, axis=0), split[...])
    gx[0] = mixed.reshape(2 * REDUCE, half, 2 * cols)


def unpack_body(meta, own, other, *outs, slots, tiles, half, middle):
    upper = core_place(meta, slots, tiles) == 1
    at = middle_place(meta, slots, tiles)
    early, late = EARLY_ROWS // middle, LATE_ROWS // middle

    def pick(start, count, base, size):
        step = math.gcd(size, 128)
        mine, theirs = [], []
        for row in range(start, start + count, step):
            chunk, offset = divmod(row, size)
            where = (chunk ^ at) * (early + late) + base + offset
            rows = pl.ds(pl.multiple_of(where, math.gcd(step, 16)), step)
            mine.append(own[rows])
            theirs.append(other[rows])
        mine = jnp.concatenate(mine, axis=0).astype(F32)[:count]
        theirs = jnp.concatenate(theirs, axis=0).astype(F32)[:count]
        return jnp.where(upper, theirs, mine), jnp.where(upper, mine, theirs)

    (embed, reduce, query, key, value, output, expand, shrink, *vectors) = outs
    spans = expand.shape[1] // 128
    taps = REDUCE * REDUCE
    for chunk in range(EARLY_ROWS // 128):
        first, second = pick(chunk * 128, 128, 0, early)
        if chunk < taps:
            reduce[chunk * 128 : (chunk + 1) * 128] = first
        elif chunk == taps:
            key[...] = first
        elif chunk == taps + 1:
            value[...] = first
        if chunk < spans:
            expand[:, chunk * 128 : (chunk + 1) * 128] = second
        elif chunk < 2 * spans:
            shrink[(chunk - spans) * 128 : (chunk - spans + 1) * 128] = second
        elif chunk == 2 * spans:
            hidden_vectors = second
        elif chunk == 2 * spans + 1:
            output[...] = second
        else:
            query[...] = second
    count = 9 * half // 2
    first, second = pick(0, count + VECTORS, early, late)
    embed[:count] = first[:count]
    embed[count:] = second[:count]
    *short, expand_bias, depth, depth_bias = vectors
    for n, out in enumerate(short):
        out[...] = first[count + n]
    for t in range(spans):
        lanes = slice(t * 128, (t + 1) * 128)
        at = t * HIDDEN_VECTORS
        expand_bias[lanes] = hidden_vectors[at]
        depth_bias[lanes] = hidden_vectors[at + 1]
        depth[:, lanes] = hidden_vectors[at + 2 : at + 11]


def turned_by(array, distance):
    count = lax.axis_size("tile")
    return lax.ppermute(array, "tile", [(i, (i + distance) % count) for i in range(count)])


def crossed(array, bits):
    count = lax.axis_size("tile")
    return lax.ppermute(array, "tile", [(i, i ^ bits) for i in range(count)])


def device_levels():
    batch_count, tile_count = lax.axis_size("batch"), lax.axis_size("tile")
    batch_at, tile_at = lax.axis_index("batch"), lax.axis_index("tile")

    def routes(size, target):
        return [
            [
                (b * tile_count + t, target(b, t, turn))
                for b in range(batch_count)
                for t in range(tile_count)
            ]
            for turn in range(1, size)
        ]

    def flat(batch, tile):
        return batch * tile_count + tile

    return (
        (2, batch_at % 2, routes(2, lambda b, t, turn: flat(b ^ turn, t))),
        (
            batch_count,
            (batch_at // 2) * 2 + tile_at % 2,
            routes(batch_count, lambda b, t, turn: flat(b ^ (turn // 2 * 2), t ^ (turn % 2))),
        ),
        (
            tile_count // 2,
            tile_at // 2,
            routes(tile_count // 2, lambda b, t, turn: flat(b, t ^ (2 * turn))),
        ),
    )


AXES = ("batch", "tile")


def scatter_level(parts, level):
    size, at, turns = level
    own = lax.dynamic_index_in_dim(parts, at, 0, keepdims=False)
    sent = [
        lax.ppermute(
            lax.dynamic_index_in_dim(parts, at ^ turn, 0, keepdims=False).astype(BF16),
            AXES,
            turns[turn - 1],
        )
        for turn in range(1, size)
    ]
    return own, sent


def added(own, sent):
    for part in sent:
        own = own + part.astype(F32)
    return own


def gather_level(low, level):
    size, _, turns = level
    return jnp.stack([low] + [lax.ppermute(low, AXES, turns[turn - 1]) for turn in range(1, size)])


def from_first(blocks, level):
    size, at, _ = level
    return jnp.stack(
        [lax.dynamic_index_in_dim(blocks, at ^ n, 0, keepdims=False) for n in range(size)]
    )


def shards(
    embed_input,
    piece_image,
    embed_weight,
    embed_bias,
    embed_gain,
    embed_shift,
    first_gain,
    first_shift,
    query_weight,
    query_bias,
    reduce_weight,
    reduce_bias,
    reduce_gain,
    reduce_shift,
    key_weight,
    value_weight,
    value_bias,
    output_weight,
    output_bias,
    second_gain,
    second_shift,
    expand_weight,
    expand_bias,
    depth_weight,
    depth_bias,
    shrink_weight,
    shrink_bias,
    cotangent,
):
    source = embed_input[0].swapaxes(2, 3)
    slots, _, channels, wide_cols = source.shape
    cols = wide_cols // 2
    cells = REDUCE * cols
    keys = cols // REDUCE
    model = embed_weight.shape[3]
    hidden = expand_weight.shape[1]
    tiles = lax.axis_size("tile")
    tile_at = lax.axis_index("tile")
    pieces = tiles // 2
    core_level, middle_level, high_level = device_levels()

    top = turned_by(source[:, 2 * REDUCE - 1], 1)
    meta = jnp.concatenate(
        [piece_image.reshape(-1), jnp.stack([tile_at, core_level[1], middle_level[1]]).astype(jnp.int32)]
    )
    vec = jnp.stack(
        [
            embed_bias, embed_gain, embed_shift, first_gain, first_shift, query_bias, reduce_bias,
            reduce_gain, reduce_shift, value_bias, output_bias, second_gain, second_shift,
            shrink_bias, shrink_bias, shrink_bias,
        ]
    ).astype(F32)
    hv = jnp.concatenate(
        [
            expand_bias[None], depth_bias[None], depth_weight.reshape(9, hidden),
            jnp.zeros((HIDDEN_VECTORS - 11, hidden), BF16),
        ]
    ).astype(F32)

    kw = dict(cols=cols)
    place = dict(slots=slots, tiles=tiles)
    flat_reduce = reduce_weight.reshape(-1, model)
    pairs, esum, stream, normed, blocks, reduced, kv = slot_call(
        partial(embed_body, **kw, **place),
        slots,
        [
            (meta, "smem"), (source, "slot"), (top, "slot"), (embed_weight, "whole"),
            (vec, "whole"), (flat_reduce, "whole"), (key_weight, "whole"), (value_weight, "whole"),
        ],
        [
            ((slots, 2 * REDUCE + 1, 2 * channels, cols), BF16, "slot"),
            ((slots, cells, model), F32, "slot"),
            ((slots, cells, model), F32, "slot"),
            ((slots, cells, model), BF16, "slot"),
            ((slots * keys, REDUCE * REDUCE * model), BF16, "whole"),
            ((slots * keys, model), F32, "whole"),
            ((slots * keys, 2 * model), BF16, "whole"),
        ],
        [
            pltpu.VMEM((wide_cols, wide_cols), BF16),
            pltpu.VMEM((cells, 2 * model), F32),
            pltpu.VMEM((cells, model), F32),
        ],
        name="embed",
    )

    kv = kv.reshape(slots, keys, 2 * model)
    pair_kv = jnp.concatenate([kv, crossed(kv, 1)], axis=1)
    kvs = [pair_kv] + [crossed(pair_kv, 2 * n) for n in range(1, pieces)]

    all_keys = keys * tiles
    queries, probs, attended, stream_two, normed_two, first_row, last_row = slot_call(
        partial(attend_body, pieces=pieces, **kw, **place),
        slots,
        [
            (meta, "smem"), (normed, "slot"), (stream, "slot"), (vec, "whole"),
            (query_weight, "whole"), (output_weight, "whole"),
        ]
        + [(a, "slot") for a in kvs],
        [
            ((slots, cells, model), BF16, "slot"),
            ((slots, cells, HEADS * all_keys), BF16, "slot"),
            ((slots, cells, model), BF16, "slot"),
            ((slots, cells, model), F32, "slot"),
            ((slots, cells, model), BF16, "slot"),
            ((slots, cols, model), BF16, "slot"),
            ((slots, cols, model), BF16, "slot"),
        ],
        [pltpu.VMEM((cells, HEADS * all_keys), F32)],
        name="attend",
    )

    row_up = turned_by(last_row, 1)
    row_down = turned_by(first_row, -1)
    width = 256
    pitch = cols + 4 * HALF_PAD
    grad_out = cotangent[0].reshape(slots, cells, model)
    out, gn_own, gn_up, gn_down, d_expand, d_shrink, d_hv = slot_call(
        partial(feed_body, width=width, **kw, **place),
        slots,
        [
            (meta, "smem"), (normed_two, "slot"), (row_up, "slot"), (row_down, "slot"),
            (grad_out, "slot"), (stream_two, "slot"), (vec, "whole"), (hv, "whole"),
            (expand_weight, "whole"), (shrink_weight, "whole"),
        ],
        [
            ((slots, cells, model), BF16, "slot"),
            ((slots, cells, model), F32, "slot"),
            ((slots, cols, model), BF16, "slot"),
            ((slots, cols, model), BF16, "slot"),
            ((model, hidden), F32, "whole"),
            ((hidden, model), F32, "whole"),
            ((HIDDEN_VECTORS, hidden), F32, "whole"),
        ],
        [
            pltpu.VMEM((width // 128, (REDUCE + 2) * pitch, 128), F32),
            pltpu.VMEM((width // 128, REDUCE * pitch, 128), F32),
            pltpu.VMEM((cells, width), F32),
            pltpu.VMEM((cells, width), BF16),
            pltpu.VMEM((cells + 2 * cols, width), BF16),
            pltpu.VMEM((cells, model), F32),
            pltpu.VMEM((cells + 2 * cols, model), F32),
            pltpu.VMEM((cells + 2 * cols, model), BF16),
            pltpu.VMEM((model, cells + 2 * cols), BF16),
            pltpu.VMEM((model, cells), BF16),
            pltpu.VMEM((model, hidden), F32),
        ],
        name="feed_forward",
    )

    from_up = turned_by(gn_down, 1)
    from_down = turned_by(gn_up, -1)
    results = slot_call(
        partial(attend_back_body, pieces=pieces, **kw),
        slots,
        [
            (gn_own, "slot"), (from_up, "slot"), (from_down, "slot"), (stream_two, "slot"),
            (grad_out, "slot"), (attended, "slot"), (probs, "slot"), (queries, "slot"),
            (normed, "slot"), (vec, "whole"), (output_weight, "whole"),
        ]
        + [(a, "slot") for a in kvs],
        [
            ((slots, cells, model), F32, "slot"),
            ((slots, cells, model), BF16, "slot"),
            ((model, model), F32, "whole"),
            ((model, model), F32, "whole"),
            ((VECTORS, model), F32, "whole"),
        ]
        + [((slots, 2 * keys, 2 * model), BF16, "slot")] * pieces,
        [
            pltpu.VMEM((cells, HEADS * all_keys), F32),
            pltpu.VMEM((cells, HEADS * all_keys), BF16),
            pltpu.VMEM((cells, model), BF16),
            pltpu.VMEM((cells, model), BF16),
        ],
        name="attend_back",
    )
    gst, gq, d_output, d_query, dvec_a = results[:5]
    dkvs = results[5:]
    pair_sum = dkvs[0].astype(F32)
    for n in range(1, pieces):
        pair_sum = pair_sum + crossed(dkvs[n], 2 * n).astype(F32)
    arrived = crossed(pair_sum[:, keys:].astype(BF16), 1).reshape(slots * keys, 2 * model)
    own_dkv = pair_sum[:, :keys].reshape(slots * keys, 2 * model)

    vmem = pl.BlockSpec(memory_space=pltpu.VMEM)
    gnb, dvec_b, keep, send = pl.pallas_call(
        partial(reduce_back_body, **place),
        in_specs=[smem()] + [vmem] * 14,
        out_specs=[vmem] * 4,
        out_shape=[
            jax.ShapeDtypeStruct((slots * keys, REDUCE * REDUCE * model), F32),
            jax.ShapeDtypeStruct((VECTORS, model), F32),
            jax.ShapeDtypeStruct((EARLY_ROWS, 128), F32),
            jax.ShapeDtypeStruct((EARLY_ROWS, 128), BF16),
        ],
        compiler_params=pltpu.CompilerParams(vmem_limit_bytes=VMEM_BYTES),
        name="reduce_back",
    )(
        meta, own_dkv, arrived, reduced, blocks, vec, flat_reduce, key_weight, value_weight,
        d_expand, d_shrink, d_hv, d_output, d_query, dvec_a,
    )
    got = lax.ppermute(send, AXES, core_level[2][0])

    gnb_spec = pl.BlockSpec((keys, REDUCE * REDUCE * model), lambda s: (s, 0))
    grid_in = [
        (meta, smem()), (gnb, gnb_spec), (gq, per_slot(gq.shape)), (gst, per_slot(gst.shape)),
        (esum, per_slot(esum.shape)), (pairs, per_slot(pairs.shape)), (vec, whole(vec.shape)),
        (query_weight, whole(query_weight.shape)), (dvec_b, whole(dvec_b.shape)),
    ]
    grid_out = [
        ((slots, cells, 2 * model), BF16, per_slot),
        ((slots, cols, model), BF16, per_slot),
        ((LATE_ROWS, 128), F32, whole),
        ((LATE_ROWS, 128), BF16, whole),
    ]
    ge, ge_first, late_keep, late_send = pl.pallas_call(
        partial(embed_back_body, half=channels, **kw, **place),
        grid=(slots,),
        in_specs=[spec for _, spec in grid_in],
        out_specs=[make(shape) for shape, _, make in grid_out],
        out_shape=[jax.ShapeDtypeStruct(shape, dtype) for shape, dtype, _ in grid_out],
        scratch_shapes=[
            pltpu.VMEM((cells, model), F32),
            pltpu.VMEM((9 * channels, model), F32),
            pltpu.VMEM((VECTORS, model), F32),
        ],
        compiler_params=params(),
        name="embed_back",
    )(*[a for a, _ in grid_in])
    below = turned_by(ge_first, -1)
    late_got = lax.ppermute(late_send, AXES, core_level[2][0])

    (grad_input,) = slot_call(
        partial(input_back_body, half=channels, **kw, **place),
        slots,
        [(meta, "smem"), (ge, "slot"), (below, "slot"), (embed_weight, "whole")],
        [(source.shape, F32, "slot")],
        [pltpu.VMEM((wide_cols, wide_cols), BF16)],
        name="input_back",
    )

    middle, high = middle_level[0], high_level[0]
    parts = jnp.concatenate(
        [
            (keep + got.astype(F32)).reshape(middle, -1, 128),
            (late_keep + late_got.astype(F32)).reshape(middle, -1, 128),
        ],
        axis=1,
    )
    own, sent = scatter_level(parts, middle_level)
    sent, grad_input = lax.optimization_barrier((sent, grad_input))
    own = added(own, sent)
    low = added(*scatter_level(own.reshape(high, -1, 128), high_level)).astype(BF16)
    low = from_first(gather_level(low, high_level), high_level).reshape(-1, 128)
    low = gather_level(low, middle_level).reshape(-1, 128)
    other = lax.ppermute(low, AXES, core_level[2][0])

    shapes = [(9 * channels, model), (REDUCE * REDUCE * model, model)]
    shapes += [(model, model)] * 4 + [(model, hidden), (hidden, model)]
    shapes += [(model,)] * 14 + [(hidden,), (9, hidden), (hidden,)]
    results = pl.pallas_call(
        partial(unpack_body, half=channels, middle=middle, **place),
        in_specs=[smem()] + [vmem] * 2,
        out_specs=[vmem] * len(shapes),
        out_shape=[jax.ShapeDtypeStruct(shape, F32) for shape in shapes],
        compiler_params=pltpu.CompilerParams(vmem_limit_bytes=VMEM_BYTES),
        name="unpack",
    )(meta, low, other)
    (s_embed, s_reduce, s_query, s_key, s_value, s_output, s_expand, s_shrink) = results[:8]
    vectors = results[8:22]
    s_expand_bias, s_depth, s_depth_bias = results[22:]
    return (
        out.reshape(cotangent.shape),
        grad_input.swapaxes(2, 3)[None],
        s_embed.reshape(embed_weight.shape),
        vectors[EMBED_BIAS],
        vectors[EMBED_GAIN],
        vectors[EMBED_SHIFT],
        vectors[FIRST_GAIN],
        vectors[FIRST_SHIFT],
        s_query,
        vectors[QUERY_BIAS],
        s_reduce.reshape(reduce_weight.shape),
        vectors[REDUCE_BIAS],
        vectors[REDUCE_GAIN],
        vectors[REDUCE_SHIFT],
        s_key,
        s_value,
        vectors[VALUE_BIAS],
        s_output,
        vectors[OUTPUT_BIAS],
        vectors[SECOND_GAIN],
        vectors[SECOND_SHIFT],
        s_expand,
        s_expand_bias,
        s_depth.reshape(depth_weight.shape),
        s_depth_bias,
        s_shrink,
        vectors[SHRINK_BIAS],
    )


def solution(mesh):
    shard_rows = P("batch", None, "tile", None, None)
    in_specs = (shard_rows, P("batch", None, None, None)) + (P(),) * 25 + (shard_rows,)
    out_specs = (shard_rows, shard_rows) + (P(),) * 25
    return jax.shard_map(shards, mesh=mesh, in_specs=in_specs, out_specs=out_specs, check_vma=False)
```

```python
import math
from functools import partial

import jax
import jax.numpy as jnp
from jax import lax
from jax.experimental import pallas as pl
from jax.experimental.pallas import tpu as pltpu
from jax.sharding import PartitionSpec as P

HEADS = 2
REDUCE = 4
F32 = jnp.float32
BF16 = jnp.bfloat16
HIGHEST = lax.Precision.HIGHEST
LOG2E = math.log2(math.e)
VMEM_BYTES = 32 * 1024 * 1024

(
    EMBED_BIAS,
    EMBED_GAIN,
    EMBED_SHIFT,
    FIRST_GAIN,
    FIRST_SHIFT,
    QUERY_BIAS,
    REDUCE_BIAS,
    REDUCE_GAIN,
    REDUCE_SHIFT,
    VALUE_BIAS,
    OUTPUT_BIAS,
    SECOND_GAIN,
    SECOND_SHIFT,
    SHRINK_BIAS,
) = range(14)
VECTORS = 16
HIDDEN_VECTORS = 16


def nn(left, right, precision=None):
    return lax.dot_general(
        left, right, (((1,), (0,)), ((), ())), precision=precision, preferred_element_type=F32
    )


def nt(left, right, precision=None):
    return lax.dot_general(
        left, right, (((1,), (1,)), ((), ())), precision=precision, preferred_element_type=F32
    )


def tn(left, right, precision=None):
    return lax.dot_general(
        left, right, (((0,), (0,)), ((), ())), precision=precision, preferred_element_type=F32
    )


def norm_stats(values, epsilon):
    centered = values - jnp.mean(values, axis=-1, keepdims=True)
    scale = lax.rsqrt(jnp.mean(centered * centered, axis=-1, keepdims=True) + epsilon)
    return centered * scale, scale


def norm_back(grad, hat, scale, gain):
    grad_hat = grad * gain
    mean_grad = jnp.mean(grad_hat, axis=-1, keepdims=True)
    mean_dot = jnp.mean(grad_hat * hat, axis=-1, keepdims=True)
    return scale * (grad_hat - mean_grad - hat * mean_dot)


def row_sum(values):
    return jnp.sum(values, axis=0, keepdims=True)


def params(vmem=VMEM_BYTES, axes=1):
    return pltpu.CompilerParams(
        vmem_limit_bytes=vmem, dimension_semantics=("arbitrary",) * axes
    )


def whole(shape, slots=None):
    rank = len(shape)
    return pl.BlockSpec(tuple(shape), lambda *_: (0,) * rank)


def per_slot(shape, slots=None):
    rank = len(shape)
    return pl.BlockSpec((1,) + tuple(shape[1:]), lambda s: (s,) + (0,) * (rank - 1))


def per_slot_rows(shape, slots):
    return pl.BlockSpec((shape[0] // slots, shape[1]), lambda s: (s, 0))


def smem():
    return pl.BlockSpec(memory_space=pltpu.SMEM)


def far(shape, dtype):
    return pltpu.HBM(tuple(shape), dtype)


def from_far(array):
    return pltpu.with_memory_space_constraint(array, pltpu.HBM)


def cost(microseconds):
    return pl.CostEstimate(
        flops=int(microseconds * 1.0e9), bytes_accessed=int(microseconds * 3.0e6), transcendentals=0
    )


def slot_call(body, slots, inputs, outputs, scratch=(), name=None, lasts=5):
    kinds = {"slot": per_slot, "whole": whole, "keys": per_slot_rows}

    def spec(shape, kind):
        kind = kind.removeprefix("far ")
        return smem() if kind == "smem" else kinds[kind](shape, slots)

    return pl.pallas_call(
        body,
        grid=(slots,),
        in_specs=[spec(a.shape, k) for a, k in inputs],
        out_specs=[spec(s, k) for s, _, k in outputs],
        out_shape=[
            (far if k.startswith("far ") else jax.ShapeDtypeStruct)(s, d) for s, d, k in outputs
        ],
        scratch_shapes=list(scratch),
        compiler_params=params(),
        cost_estimate=cost(lasts),
        name=name,
    )(*[from_far(a) if k.startswith("far ") else a for a, k in inputs])


def tile_ids(meta, s, tile, tiles):
    at = (s * tiles + tile) * 2
    return meta[at], meta[at + 1]


def tile_place(meta, slots, tiles):
    return meta[slots * tiles * 2]


def core_place(meta, slots, tiles):
    return meta[slots * tiles * 2 + 1]


def middle_place(meta, slots, tiles):
    return meta[slots * tiles * 2 + 2]


def as_flag(condition):
    return jnp.where(condition, 1.0, 0.0).astype(F32)


def same_flags(meta, s, slots, tiles):
    at = tile_place(meta, slots, tiles)
    own = tile_ids(meta, s, at, tiles)
    up = tile_ids(meta, s, jnp.maximum(at - 1, 0), tiles)
    down = tile_ids(meta, s, jnp.minimum(at + 1, tiles - 1), tiles)
    return (
        as_flag(own[0] == own[1]),
        as_flag((own[0] == up[0]) & (at > 0)),
        as_flag((own[0] == down[0]) & (at < tiles - 1)),
    )


def split_columns(size):
    source = lax.broadcasted_iota(jnp.int32, (size, size), 0)
    target = lax.broadcasted_iota(jnp.int32, (size, size), 1)
    wanted = jnp.where(target < size // 2, 2 * target, 2 * target - size + 1)
    return jnp.where(source == wanted, 1.0, 0.0).astype(BF16)


def embed_weights(ew):
    half = ew.shape[2]
    none = jnp.zeros_like(ew[0, 0])
    weights = []
    for a in range(3):
        main = ew[a, 1:3].reshape(2 * half, 128)
        side = jnp.concatenate([none, ew[a, 0]], axis=0)
        weights.append(jnp.concatenate([main, side], axis=1))
    return jnp.concatenate(weights, axis=0)


def embed_own_body(x, ew, pairs, partial_sum, split, *, cols):
    half = x.shape[2]

    @pl.when(pl.program_id(0) == 0)
    def _():
        split[...] = split_columns(2 * cols)

    own = nn(x[0].reshape(2 * REDUCE * half, 2 * cols), split[...])
    for r in range(2 * REDUCE):
        row = own[r * half : (r + 1) * half].astype(BF16)
        pairs[0, r, :half] = row[:, :cols]
        pairs[0, r, half:] = row[:, cols:]
    weights = embed_weights(ew)
    for i in range(REDUCE):
        first = max(2 * i - 1, 0)
        lines = pairs[0, first : 2 * i + 2]
        lines = lines.reshape(lines.shape[0] * 128, cols)
        partial_sum[0, i * cols : (i + 1) * cols] = tn(lines, weights[-lines.shape[0] :])


def embed_body(
    meta, partial_sum, top, ew, vec, rw, kw, vw,
    top_pairs, esum, stream, normed, blocks, reduced, kv,
    split, nbuf, *, cols, slots, tiles,
):
    s = pl.program_id(0)
    same_sides, same_up, _ = same_flags(meta, s, slots, tiles)
    keys = cols // REDUCE
    half = top.shape[1]

    @pl.when(s == 0)
    def _():
        split[...] = split_columns(2 * cols)

    above = nn(top[0], split[...]) * same_up
    row = above.astype(BF16)
    top_pairs[0, :half] = row[:, :cols]
    top_pairs[0, half:] = row[:, cols:]
    from_top = tn(top_pairs[0], embed_weights(ew)[:128])
    column = lax.broadcasted_iota(jnp.int32, (cols, 1), 0)
    mask = jnp.where(column == 0, 0.0, jnp.where(column == cols // 2, same_sides, 1.0))
    for i in range(REDUCE):
        rows = slice(i * cols, (i + 1) * cols)
        z = partial_sum[0, rows]
        if i == 0:
            z = z + from_top
        value = z[:, :128] + pltpu.roll(z[:, 128:], 1, 0) * mask + vec[EMBED_BIAS : EMBED_BIAS + 1]
        esum[0, rows] = value
        hat, _ = norm_stats(value, 1e-05)
        st = hat * vec[EMBED_GAIN : EMBED_GAIN + 1] + vec[EMBED_SHIFT : EMBED_SHIFT + 1]
        stream[0, rows] = st
        hat, _ = norm_stats(st, 1e-06)
        nm = hat * vec[FIRST_GAIN : FIRST_GAIN + 1] + vec[FIRST_SHIFT : FIRST_SHIFT + 1]
        low = nm.astype(BF16)
        normed[0, rows] = low
        nbuf[rows] = low.astype(F32)
    for a in range(REDUCE):
        for b in range(REDUCE):
            at = (a * REDUCE + b) * 128
            piece = nbuf[pl.ds(a * cols + b, keys, REDUCE), :]
            blocks[pl.ds(pl.multiple_of(s * keys, keys), keys), at : at + 128] = piece.astype(BF16)

    @pl.when(s == slots - 1)
    def _():
        value = nn(blocks[...], rw[...]) + vec[REDUCE_BIAS : REDUCE_BIAS + 1]
        reduced[...] = value
        hat, _ = norm_stats(value, 1e-06)
        rn = (hat * vec[REDUCE_GAIN : REDUCE_GAIN + 1] + vec[REDUCE_SHIFT : REDUCE_SHIFT + 1]).astype(BF16)
        kv[:, :128] = nn(rn, kw[...]).astype(BF16)
        kv[:, 128:] = (nn(rn, vw[...]) + vec[VALUE_BIAS : VALUE_BIAS + 1]).astype(BF16)


def both_heads(kv, at):
    rows = kv[0, :, at : at + 128]
    lane = lax.broadcasted_iota(jnp.int32, rows.shape, 1)
    zero = jnp.zeros_like(rows)
    return jnp.concatenate(
        [jnp.where(lane < 64, rows, zero), jnp.where(lane < 64, zero, rows)], axis=0
    )


def key_bias(meta, s, slots, tiles, keys):
    at = tile_place(meta, slots, tiles)
    own = tile_ids(meta, s, at, tiles)
    part = keys // (2 * tiles)
    entry = lax.broadcasted_iota(jnp.int32, (1, keys), 1) // part
    rows = [jnp.zeros((1, keys), F32) for _ in range(2)]
    for n in range(tiles):
        ids = tile_ids(meta, s, at ^ n, tiles)
        for side in range(2):
            for query in range(2):
                value = jnp.where(ids[side] == own[query], 0.0, -1e30).astype(F32)
                rows[query] = jnp.where(entry == 2 * n + side, value, rows[query])
    return rows


def attend_body(*refs, pieces, cols, slots, tiles):
    (meta, normed, stream, vec, qw, ow), refs = refs[:6], refs[6:]
    kvs, refs = refs[:pieces], refs[pieces:]
    queries, probs, attended, stream_two, normed_two, first_row, last_row, kv_all, sbuf = refs
    kv_all[0] = jnp.concatenate([p[0] for p in kvs], axis=0)
    q = (nn(normed[0], qw[...]) + vec[QUERY_BIAS : QUERY_BIAS + 1]).astype(BF16)
    queries[0] = q
    sbuf[...] = nt(q, both_heads(kv_all, 0))
    keys = sbuf.shape[1] // HEADS
    half = cols // 2
    factor = LOG2E * (128 // HEADS) ** (-0.5)
    bias = key_bias(meta, pl.program_id(0), slots, tiles, keys)
    for i in range(REDUCE):
        for side in range(2):
            at = i * cols + side * half
            for h in range(HEADS):
                s = sbuf[at : at + half, h * keys : (h + 1) * keys] * factor + bias[side]
                e = jnp.exp2(s - jnp.max(s, axis=-1, keepdims=True))
                p = e * (1.0 / jnp.sum(e, axis=-1, keepdims=True))
                probs[0, at : at + half, h * keys : (h + 1) * keys] = p.astype(BF16)
    att = nn(probs[0], both_heads(kv_all, 128)).astype(BF16)
    attended[0] = att
    sbuf[:, :128] = nn(att, ow[...])
    for i in range(REDUCE):
        rows = slice(i * cols, (i + 1) * cols)
        value = stream[0, rows] + sbuf[rows, :128] + vec[OUTPUT_BIAS : OUTPUT_BIAS + 1]
        stream_two[0, rows] = value
        hat, _ = norm_stats(value, 1e-06)
        low = (hat * vec[SECOND_GAIN : SECOND_GAIN + 1] + vec[SECOND_SHIFT : SECOND_SHIFT + 1]).astype(BF16)
        normed_two[0, rows] = low
        if i == 0:
            first_row[0] = low
        if i == REDUCE - 1:
            last_row[0] = low


DENSITY = 1.0 / math.sqrt(2.0 * math.pi)


def gelu_pair(x):
    twice_cdf = 1.0 + lax.erf(x * math.sqrt(0.5))
    e = jnp.exp2((x * x) * (-0.5 * LOG2E))
    return x * twice_cdf, twice_cdf + x * (e * (2.0 * DENSITY))


GROUP = 16


def fold_rows(values):
    return values[: GROUP // 2] + values[GROUP // 2 :]


def group(n):
    return slice(n * GROUP, (n + 1) * GROUP)


def group_places(r, s, q, cols, slots):
    spans = GROUP // slots
    span = cols // spans
    return pl.ds(r * span * GROUP + s * spans + q, span, GROUP)


def grouped_body(g, gp, g_t, buf, *, cols, slots):
    spans = GROUP // slots
    span = cols // spans
    line = span * GROUP
    for s in range(slots):
        for q in range(spans):
            for r in range(REDUCE):
                row = g[s, r * cols + q * span : r * cols + (q + 1) * span]
                buf[group_places(r, s, q, cols, slots), :] = row.astype(F32)
    for r in range(REDUCE):
        rows = slice(r * line, (r + 1) * line)
        gp[rows] = buf[rows].astype(BF16)
        g_t[:, rows] = gp[rows].T


def feed_body(
    meta, nt_own, nt_up, nt_down, gp, g_t, hv, dw, ew, sw,
    gn_own, gn_up, gn_down, dew, dsw, deb, a_out, h_out, c_out,
    abuf0, abuf1, hbuf0, hbuf1, cbuf0, cbuf1, ghbuf, gabuf, gnacc, ext, ext_t, sems,
    *, cols, slots, tiles, width,
):
    abufs, hbufs, cbufs = (abuf0, abuf1), (hbuf0, hbuf1), (cbuf0, cbuf1)
    model = ew.shape[0]
    blocks = ew.shape[1] // width
    spans = GROUP // slots
    span = cols // spans
    line = span * GROUP
    padded = line + 2 * GROUP
    rows_in = REDUCE + 2
    lane_tiles = width // 128

    def copies(b, side):
        lanes = pl.ds(pl.multiple_of(b * width, width), width)
        tiles_at = pl.ds(b * lane_tiles, lane_tiles)
        pairs = (
            (abufs, a_out.at[:, lanes]), (hbufs, h_out.at[tiles_at]), (cbufs, c_out.at[tiles_at]),
        )
        return [
            pltpu.make_async_copy(bufs[side], there, sems.at[n, side])
            for n, (bufs, there) in enumerate(pairs)
        ]

    sub = lax.broadcasted_iota(jnp.int32, (GROUP, 1), 0)
    at_slot, at_span = sub // spans, sub % spans
    same = [jnp.zeros((GROUP, 1), F32) for _ in range(3)]
    for s in range(slots):
        flags = same_flags(meta, s, slots, tiles)
        same = [jnp.where(at_slot == s, flag, mask) for flag, mask in zip(flags, same)]
    sides, same_up, same_down = same
    from_left = jnp.where(at_span == 0, 0.0, jnp.where(at_span == spans // 2, sides, 1.0))
    from_right = jnp.where(
        at_span == spans - 1, 0.0, jnp.where(at_span == spans // 2 - 1, sides, 1.0)
    )
    low_up = jnp.broadcast_to(same_up, (GROUP, 128)).astype(BF16)
    low_down = jnp.broadcast_to(same_down, (GROUP, 128)).astype(BF16)

    for s in range(slots):
        for q in range(spans):
            for r in range(rows_in):
                if r == 0:
                    row = nt_up[s, q * span : (q + 1) * span]
                elif r == rows_in - 1:
                    row = nt_down[s, q * span : (q + 1) * span]
                else:
                    at = (r - 1) * cols + q * span
                    row = nt_own[s, at : at + span]
                gnacc[group_places(r, s, q, cols, slots), :] = row.astype(F32)
    for r in range(rows_in):
        rows = slice(r * line, (r + 1) * line)
        ext[rows] = gnacc[rows].astype(BF16)
        ext_t[:model, rows] = ext[rows].T
    ext_t[model:] = jnp.ones_like(ext_t[model:])
    gnacc[...] = jnp.zeros_like(gnacc)

    def ghosts(buf, rows):
        for t in range(lane_tiles):
            for r in range(rows):
                base = r * padded
                first = buf[t, base + GROUP : base + 2 * GROUP].astype(F32)
                last = buf[t, base + line : base + line + GROUP].astype(F32)
                left = pltpu.roll(last, 1, 0) * from_left
                right = pltpu.roll(first, GROUP - 1, 0) * from_right
                buf[t, base : base + GROUP] = left.astype(BF16)
                buf[t, base + line + GROUP : base + padded] = right.astype(BF16)

    def taps_of(lanes):
        return [
            [jnp.broadcast_to(dw[a, c : c + 1, lanes], (GROUP, 128)) for c in range(3)]
            for a in range(3)
        ]

    def block(b, side):
        abuf, hbuf, cbuf = abufs[side], hbufs[side], cbufs[side]
        to_a, to_h, to_c = copies(b, side)
        at = pl.multiple_of(b * width, width)
        ewb = ew[:, pl.ds(at, width)]
        half_sw = sw[pl.ds(at, width), :] * 0.5
        bias = hv[0:1, pl.ds(at, width)]
        for r in range(rows_in):
            hid = nn(ext[r * line : (r + 1) * line], ewb) + bias
            if r == 0 or r == rows_in - 1:
                mask = same_up if r == 0 else same_down
                hid = (hid.reshape(span, GROUP, width) * mask[None]).reshape(line, width)
            for t in range(lane_tiles):
                base = r * padded + GROUP
                hbuf[t, base : base + line] = hid[:, t * 128 : (t + 1) * 128].astype(BF16)
        ghosts(hbuf, rows_in)
        to_h.start()
        for r in range(REDUCE):
            rows = slice(r * line, (r + 1) * line)
            gabuf[rows] = nt(gp[rows], half_sw)
        for t in range(lane_tiles):
            lanes = slice(t * 128, (t + 1) * 128)
            spot = pl.ds(pl.multiple_of(at + t * 128, 128), 128)
            taps = taps_of(spot)
            depth_bias = hv[1:2, spot]
            for col in range(span):
                h = [
                    [hbuf[t, group(r * (span + 2) + col + d)] for d in range(3)]
                    for r in range(rows_in)
                ]
                for i in range(REDUCE):
                    conv = None
                    for a in range(3):
                        for c in range(3):
                            term = h[i + a][c] * taps[a][c]
                            conv = term if conv is None else conv + term
                    act, slope = gelu_pair(conv.astype(F32) + depth_bias)
                    rows = group(i * span + col)
                    abuf[rows, lanes] = act.astype(BF16)
                    grad = gabuf[rows, lanes] * slope
                    cbuf[t, group(i * (span + 2) + col + 1)] = grad.astype(BF16)
        to_a.start()
        ghosts(cbuf, REDUCE)
        to_c.start()
        for t in range(lane_tiles):
            lanes = slice(t * 128, (t + 1) * 128)
            taps = taps_of(pl.ds(pl.multiple_of(at + t * 128, 128), 128))
            for col in range(span):
                gc = [
                    [cbuf[t, group(i * (span + 2) + col + d)] for d in range(3)]
                    for i in range(REDUCE)
                ]
                for r in range(rows_in):
                    gh = None
                    for a in range(3):
                        if not 0 <= r - a < REDUCE:
                            continue
                        for c in range(3):
                            term = gc[r - a][2 - c] * taps[a][c]
                            gh = term if gh is None else gh + term
                    if r == 0:
                        gh = gh * low_up
                    if r == rows_in - 1:
                        gh = gh * low_down
                    ghbuf[group(r * span + col), lanes] = gh
        for r in range(rows_in):
            rows = slice(r * line, (r + 1) * line)
            gnacc[rows] += nt(ghbuf[rows], ewb)
        grad = nn(ext_t[...], ghbuf[...])
        dew[:, pl.ds(at, width)] = grad[:model]
        deb[:, pl.ds(at, width)] = grad[model : model + 8]
        dsw[pl.ds(at, width), :] = nn(g_t[...], abuf[...]).T * 0.5

    def two_blocks(k, carry):
        for side in range(2):
            b = 2 * k + side

            @pl.when(k > 0)
            def _():
                for copy in copies(b - 2, side):
                    copy.wait()

            block(b, side)
        return carry

    lax.fori_loop(0, blocks // 2, two_blocks, 0)
    for s in range(slots):
        for q in range(spans):
            there = slice(q * span, (q + 1) * span)
            for r in range(rows_in):
                grad = gnacc[group_places(r, s, q, cols, slots), :]
                if r == 0:
                    gn_up[s, there] = grad.astype(BF16)
                elif r == rows_in - 1:
                    gn_down[s, there] = grad.astype(BF16)
                else:
                    at = (r - 1) * cols + q * span
                    gn_own[s, at : at + span] = grad
    for side in range(2):
        for copy in copies(blocks - 2 + side, side):
            copy.wait()


def depth_weight_body(hbuf, cbuf, deb, dhv, *, span):
    dhv[...] = jnp.zeros_like(dhv)
    dhv[0:1] = deb[0:1]
    per_sum = 4
    for t in range(hbuf.shape[0]):
        lanes = slice(t * 128, (t + 1) * 128)
        sums = [jnp.zeros((GROUP // 2, 128), F32) for _ in range(10)]
        for m in range(span // per_sum):
            parts = [None] * 10
            for col in range(per_sum * m, per_sum * (m + 1)):
                h = [
                    [hbuf[t, group(r * (span + 2) + col + d)] for d in range(3)]
                    for r in range(REDUCE + 2)
                ]
                for i in range(REDUCE):
                    gc = cbuf[t, group(i * (span + 2) + col + 1)]
                    terms = [gc] + [gc * h[i + a][c] for a in range(3) for c in range(3)]
                    parts = [
                        term if part is None else part + term for part, term in zip(parts, terms)
                    ]
            sums = [total + fold_rows(part.astype(F32)) for total, part in zip(sums, parts)]
        for n in range(10):
            dhv[1 + n : 2 + n, lanes] = row_sum(sums[n])


def output_body(abuf, stream_two, vec, sw, out, acc, *, cols, slots):
    spans = GROUP // slots
    span = cols // spans
    line = span * GROUP
    for r in range(REDUCE):
        rows = slice(r * line, (r + 1) * line)
        acc[rows] = nn(abuf[rows], sw[...] * 0.5)
    for s in range(slots):
        for q in range(spans):
            for r in range(REDUCE):
                there = slice(r * cols + q * span, r * cols + (q + 1) * span)
                value = acc[group_places(r, s, q, cols, slots), :] + stream_two[s, there]
                out[s, there] = (value + vec[SHRINK_BIAS : SHRINK_BIAS + 1]).astype(BF16)


def attend_back_body(*refs, pairs, cols):
    (gn, up, down, stream_two, g, attended, probs, queries, normed, vec, ow, kv_all), refs = (
        refs[:12],
        refs[12:],
    )
    gst, gq, dow, dqw, dvec = refs[:5]
    dkvs, (gpbuf, dsbuf, branch, gabuf) = refs[5 : 5 + pairs], refs[5 + pairs :]
    s = pl.program_id(0)

    @pl.when(s == 0)
    def _():
        dow[...] = jnp.zeros_like(dow)
        dqw[...] = jnp.zeros_like(dqw)
        dvec[...] = jnp.zeros_like(dvec)

    for i in range(REDUCE):
        rows = slice(i * cols, (i + 1) * cols)
        grad = gn[0, rows]
        if i == 0:
            grad = grad + up[0].astype(F32)
        if i == REDUCE - 1:
            grad = grad + down[0].astype(F32)
        hat, scale = norm_stats(stream_two[0, rows], 1e-06)
        dvec[SECOND_GAIN : SECOND_GAIN + 1] += row_sum(grad * hat)
        dvec[SECOND_SHIFT : SECOND_SHIFT + 1] += row_sum(grad)
        gi = g[0, rows].astype(F32)
        dvec[SHRINK_BIAS : SHRINK_BIAS + 1] += row_sum(gi)
        value = norm_back(grad, hat, scale, vec[SECOND_GAIN : SECOND_GAIN + 1]) + gi
        gst[0, rows] = value
        low = value.astype(BF16)
        branch[rows] = low
        dvec[OUTPUT_BIAS : OUTPUT_BIAS + 1] += row_sum(low.astype(F32))
    dow[...] += tn(attended[0], branch[...])
    gabuf[...] = nt(branch[...], ow[...]).astype(BF16)
    gpbuf[...] = nt(gabuf[...], both_heads(kv_all, 128))
    keys = gpbuf.shape[1] // HEADS
    half = cols // 2
    for at in range(0, REDUCE * cols, half):
        for h in range(HEADS):
            span = slice(h * keys, (h + 1) * keys)
            p = probs[0, at : at + half, span].astype(F32)
            gp = gpbuf[at : at + half, span]
            inner = jnp.sum(gp * p, axis=-1, keepdims=True)
            dsbuf[at : at + half, span] = (p * (gp - inner)).astype(BF16)
    scale = (128 // HEADS) ** (-0.5)
    gql = (nn(dsbuf[...], both_heads(kv_all, 0)) * scale).astype(BF16)
    gq[0] = gql
    dvec[QUERY_BIAS : QUERY_BIAS + 1] += row_sum(gql.astype(F32))
    dqw[...] += tn(normed[0], gql)

    def fold(both):
        return jnp.concatenate([both[:64, :keys], both[64:, keys:]], axis=0).T

    dk = fold(nn(queries[0].T, dsbuf[...])) * scale
    dv = fold(nn(gabuf[...].T, probs[0]))
    dkv = jnp.concatenate([dk, dv], axis=1).astype(BF16)
    each = keys // pairs
    for n in range(pairs):
        dkvs[n][0] = dkv[n * each : (n + 1) * each]


def reduce_back_body(*refs, parts, slots, tiles):
    arrived, refs = refs[:parts], refs[parts:]
    (meta, reduced, blocks, vec, rw, kw, vw, dexpand, dshrink, dhv, doutput, dquery, dvec_in) = refs[:13]
    gnb, dvec, keep, send = refs[13:]
    upper = core_place(meta, slots, tiles) == 1

    def place(chunk, first, second):
        rows = slice(chunk * 128, (chunk + 1) * 128)
        keep[rows] = jnp.where(upper, second, first)
        send[rows] = jnp.where(upper, first, second).astype(BF16)

    keys = reduced.shape[0] // slots
    dkv = arrived[-1][...].astype(F32)
    for part in arrived[:-1]:
        dkv = dkv + part[:, :keys].astype(F32)
    dkv = dkv.reshape(slots * keys, 256)
    dk, dv = dkv[:, :128], dkv[:, 128:]
    hat, scale = norm_stats(reduced[...], 1e-06)
    gain = vec[REDUCE_GAIN : REDUCE_GAIN + 1]
    rn = (hat * gain + vec[REDUCE_SHIFT : REDUCE_SHIFT + 1]).astype(BF16).astype(F32)
    dkw = tn(rn, dk, HIGHEST)
    dvw = tn(rn, dv, HIGHEST)
    grad = nt(dk, kw[...].astype(F32), HIGHEST) + nt(dv, vw[...].astype(F32), HIGHEST)
    low = norm_back(grad, hat, scale, gain).astype(BF16)
    gnb[...] = nt(low, rw[...])
    sums = {
        VALUE_BIAS: row_sum(dv),
        REDUCE_GAIN: row_sum(grad * hat),
        REDUCE_SHIFT: row_sum(grad),
        REDUCE_BIAS: row_sum(low.astype(F32)),
    }
    dvec[...] = jnp.concatenate(
        [sums.get(n, dvec_in[n : n + 1]) for n in range(VECTORS)], axis=0
    )
    spans = dexpand.shape[1] // 128
    second = [dexpand[:, t * 128 : (t + 1) * 128] for t in range(spans)]
    second += [dshrink[t * 128 : (t + 1) * 128] for t in range(spans)]
    second += [jnp.concatenate([dhv[:, t * 128 : (t + 1) * 128] for t in range(spans)], axis=0)]
    second += [doutput[...], dquery[...]]
    first = [tn(blocks[:, t * 128 : (t + 1) * 128], low) for t in range(REDUCE * REDUCE)]
    first += [dkw, dvw, jnp.zeros((128, 128), F32)]
    for chunk, (one, two) in enumerate(zip(first, second, strict=True)):
        place(chunk, one, two)


EARLY_ROWS = 19 * 128
LATE_ROWS = 3 * 128


def embed_back_body(
    meta, gnb, gq, gst, esum, vec, qw, dvec_in,
    ge, ge_first, dvec,
    gbuf, *, cols, slots, tiles,
):
    s = pl.program_id(0)
    same_sides, same_up, _ = same_flags(meta, s, slots, tiles)
    keys = cols // REDUCE

    @pl.when(s == 0)
    def _():
        dvec[...] = dvec_in[...]

    for a in range(REDUCE):
        for b in range(REDUCE):
            at = (a * REDUCE + b) * 128
            gbuf[pl.ds(a * cols + b, keys, REDUCE), :] = gnb[:, at : at + 128]
    gbuf[...] += nt(gq[0], qw[...])
    column = lax.broadcasted_iota(jnp.int32, (cols, 1), 0)
    mask = jnp.where(column == cols - 1, 0.0, jnp.where(column == cols // 2 - 1, same_sides, 1.0))
    gain = vec[EMBED_GAIN : EMBED_GAIN + 1]
    gain_one = vec[FIRST_GAIN : FIRST_GAIN + 1]
    for i in range(REDUCE):
        rows = slice(i * cols, (i + 1) * cols)
        hat, scale = norm_stats(esum[0, rows], 1e-05)
        hat_one, scale_one = norm_stats(hat * gain + vec[EMBED_SHIFT : EMBED_SHIFT + 1], 1e-06)
        grad = gbuf[rows]
        dvec[FIRST_GAIN : FIRST_GAIN + 1] += row_sum(grad * hat_one)
        dvec[FIRST_SHIFT : FIRST_SHIFT + 1] += row_sum(grad)
        grad = norm_back(grad, hat_one, scale_one, gain_one) + gst[0, rows]
        dvec[EMBED_GAIN : EMBED_GAIN + 1] += row_sum(grad * hat)
        dvec[EMBED_SHIFT : EMBED_SHIFT + 1] += row_sum(grad)
        low = norm_back(grad, hat, scale, gain).astype(BF16)
        wide = low.astype(F32)
        dvec[EMBED_BIAS : EMBED_BIAS + 1] += row_sum(wide)
        if i == 0:
            ge_first[0] = (wide * same_up).astype(BF16)
        ge[0, rows, :128] = low
        ge[0, rows, 128:] = (pltpu.roll(wide, cols - 1, 0) * mask).astype(BF16)


def embed_weight_body(meta, ge, pairs, top_pairs, dvec, keep, send, dew, *, half, slots, tiles):
    s = pl.program_id(0)

    @pl.when(s == 0)
    def _():
        dew[...] = jnp.zeros_like(dew)

    for a in range(3):
        lines = [2 * i + a - 1 for i in range(REDUCE)]
        lhs = jnp.concatenate([top_pairs[0] if n < 0 else pairs[0, n] for n in lines], axis=1)
        part = nn(lhs, ge[0])
        at = a * 3 * half
        dew[at : at + half] += part[half:, 128:]
        dew[at + half : at + 3 * half] += part[:, :128]

    @pl.when(s == slots - 1)
    def _():
        upper = core_place(meta, slots, tiles) == 1
        count = 9 * half // 2
        first, second = dew[:count], dew[count:]
        keep[:count] = jnp.where(upper, second, first)
        send[:count] = jnp.where(upper, first, second).astype(BF16)
        vectors = dvec[...]
        none = jnp.zeros_like(vectors)
        end = count + VECTORS
        keep[count:end] = jnp.where(upper, none, vectors)
        send[count:end] = jnp.where(upper, vectors, none).astype(BF16)
        keep[end:] = jnp.zeros((LATE_ROWS - end, 128), F32)
        send[end:] = jnp.zeros((LATE_ROWS - end, 128), BF16)


def spread_weights(ew, a):
    none = jnp.zeros_like(ew[0, 0])
    even = jnp.concatenate([ew[a, 1], none], axis=1)
    odd = jnp.concatenate([ew[a, 2], ew[a, 0]], axis=1)
    return jnp.concatenate([even, odd], axis=0)


def mixed_columns(lines, split, half, cols):
    lines = [jnp.concatenate([part[:half], part[half:]], axis=1) for part in lines]
    mixed = nt(jnp.concatenate(lines, axis=0), split[...])
    return mixed.reshape(len(lines), half, 2 * cols)


def input_back_body(ge, ew, gx, split, *, cols, half):
    @pl.when(pl.program_id(0) == 0)
    def _():
        split[...] = split_columns(2 * cols)

    own = ge[0]
    upper_rows = nt(spread_weights(ew, 1), own).astype(BF16)
    inner = nt(spread_weights(ew, 2), own[:-cols]) + nt(spread_weights(ew, 0), own[cols:])
    inner = inner.astype(BF16)
    lines = []
    for i in range(REDUCE):
        cells = slice(i * cols, (i + 1) * cols)
        lines.append(upper_rows[:, cells])
        lines.append(inner[:, cells] if i < REDUCE - 1 else jnp.zeros_like(upper_rows[:, cells]))
    gx[0] = mixed_columns(lines, split, half, cols)


def last_row_body(meta, ge, below, ew, done, gx, split, *, cols, half, slots, tiles):
    s = pl.program_id(0)
    same_sides, _, _ = same_flags(meta, s, slots, tiles)

    @pl.when(s == 0)
    def _():
        split[...] = split_columns(2 * cols)

    column = lax.broadcasted_iota(jnp.int32, (cols, 1), 0)
    mask = jnp.where(column == cols - 1, 0.0, jnp.where(column == cols // 2 - 1, same_sides, 1.0))
    shifted = (pltpu.roll(below[0].astype(F32), cols - 1, 0) * mask).astype(BF16)
    under = jnp.concatenate([below[0], shifted], axis=1)
    line = nt(spread_weights(ew, 2), ge[0]) + nt(spread_weights(ew, 0), under)
    gx[0] = mixed_columns([line.astype(BF16)], split, half, cols)


def unpack_body(meta, own, other, *outs, slots, tiles, half, middle):
    upper = core_place(meta, slots, tiles) == 1
    at = middle_place(meta, slots, tiles)
    early, late = EARLY_ROWS // middle, LATE_ROWS // middle

    def pick(start, count, base, size):
        step = math.gcd(size, 128)
        mine, theirs = [], []
        for row in range(start, start + count, step):
            chunk, offset = divmod(row, size)
            where = (chunk ^ at) * (early + late) + base + offset
            rows = pl.ds(pl.multiple_of(where, math.gcd(step, 16)), step)
            mine.append(own[rows])
            theirs.append(other[rows])
        mine = jnp.concatenate(mine, axis=0).astype(F32)[:count]
        theirs = jnp.concatenate(theirs, axis=0).astype(F32)[:count]
        return jnp.where(upper, theirs, mine), jnp.where(upper, mine, theirs)

    (embed, reduce, query, key, value, output, expand, shrink, *vectors) = outs
    spans = expand.shape[1] // 128
    taps = REDUCE * REDUCE
    for chunk in range(EARLY_ROWS // 128):
        first, second = pick(chunk * 128, 128, 0, early)
        if chunk < taps:
            reduce[chunk * 128 : (chunk + 1) * 128] = first
        elif chunk == taps:
            key[...] = first
        elif chunk == taps + 1:
            value[...] = first
        if chunk < spans:
            expand[:, chunk * 128 : (chunk + 1) * 128] = second
        elif chunk < 2 * spans:
            shrink[(chunk - spans) * 128 : (chunk - spans + 1) * 128] = second
        elif chunk == 2 * spans:
            hidden_vectors = second
        elif chunk == 2 * spans + 1:
            output[...] = second
        else:
            query[...] = second
    count = 9 * half // 2
    first, second = pick(0, count + VECTORS, early, late)
    embed[:count] = first[:count]
    embed[count:] = second[:count]
    *short, expand_bias, depth, depth_bias = vectors
    for n, out in enumerate(short):
        out[...] = first[count + n]
    for t in range(spans):
        lanes = slice(t * 128, (t + 1) * 128)
        at = t * HIDDEN_VECTORS
        expand_bias[lanes] = hidden_vectors[at]
        depth_bias[lanes] = hidden_vectors[at + 1]
        for a in range(3):
            depth[a, :, lanes] = hidden_vectors[at + 2 + 3 * a : at + 5 + 3 * a]


def turned_by(array, distance):
    count = lax.axis_size("tile")
    return lax.ppermute(array, "tile", [(i, (i + distance) % count) for i in range(count)])


def crossed(array, bits):
    count = lax.axis_size("tile")
    return lax.ppermute(array, "tile", [(i, i ^ bits) for i in range(count)])


def device_levels():
    batch_count, tile_count = lax.axis_size("batch"), lax.axis_size("tile")
    batch_at, tile_at = lax.axis_index("batch"), lax.axis_index("tile")

    def routes(size, target):
        return [
            [
                (b * tile_count + t, target(b, t, turn))
                for b in range(batch_count)
                for t in range(tile_count)
            ]
            for turn in range(1, size)
        ]

    def flat(batch, tile):
        return batch * tile_count + tile

    return (
        (2, batch_at % 2, routes(2, lambda b, t, turn: flat(b ^ turn, t))),
        (
            batch_count,
            (batch_at // 2) * 2 + tile_at % 2,
            routes(batch_count, lambda b, t, turn: flat(b ^ (turn // 2 * 2), t ^ (turn % 2))),
        ),
        (
            tile_count // 2,
            tile_at // 2,
            routes(tile_count // 2, lambda b, t, turn: flat(b, t ^ (2 * turn))),
        ),
    )


AXES = ("batch", "tile")


def scatter_level(parts, level):
    size, at, turns = level
    own = lax.dynamic_index_in_dim(parts, at, 0, keepdims=False)
    sent = [
        lax.ppermute(
            lax.dynamic_index_in_dim(parts, at ^ turn, 0, keepdims=False).astype(BF16),
            AXES,
            turns[turn - 1],
        )
        for turn in range(1, size)
    ]
    return own, sent


def added(own, sent):
    for part in sent:
        own = own + part.astype(F32)
    return own


def gather_level(low, level):
    size, _, turns = level
    return jnp.stack([low] + [lax.ppermute(low, AXES, turns[turn - 1]) for turn in range(1, size)])


def from_first(blocks, level):
    size, at, _ = level
    return jnp.stack(
        [lax.dynamic_index_in_dim(blocks, at ^ n, 0, keepdims=False) for n in range(size)]
    )


def shards(
    embed_input,
    piece_image,
    embed_weight,
    embed_bias,
    embed_gain,
    embed_shift,
    first_gain,
    first_shift,
    query_weight,
    query_bias,
    reduce_weight,
    reduce_bias,
    reduce_gain,
    reduce_shift,
    key_weight,
    value_weight,
    value_bias,
    output_weight,
    output_bias,
    second_gain,
    second_shift,
    expand_weight,
    expand_bias,
    depth_weight,
    depth_bias,
    shrink_weight,
    shrink_bias,
    cotangent,
):
    source = embed_input[0].swapaxes(2, 3)
    slots, _, channels, wide_cols = source.shape
    cols = wide_cols // 2
    cells = REDUCE * cols
    keys = cols // REDUCE
    model = embed_weight.shape[3]
    hidden = expand_weight.shape[1]
    tiles = lax.axis_size("tile")
    tile_at = lax.axis_index("tile")
    pieces = tiles
    core_level, middle_level, high_level = device_levels()

    top = turned_by(embed_input[0, :, 2 * REDUCE - 1].swapaxes(1, 2), 1)
    meta = jnp.concatenate(
        [piece_image.reshape(-1), jnp.stack([tile_at, core_level[1], middle_level[1]]).astype(jnp.int32)]
    )
    vec = jnp.stack(
        [
            embed_bias, embed_gain, embed_shift, first_gain, first_shift, query_bias, reduce_bias,
            reduce_gain, reduce_shift, value_bias, output_bias, second_gain, second_shift,
            shrink_bias, shrink_bias, shrink_bias,
        ]
    ).astype(F32)
    hv = jnp.stack([expand_bias, depth_bias]).astype(F32)

    kw = dict(cols=cols)
    place = dict(slots=slots, tiles=tiles)
    flat_reduce = reduce_weight.reshape(-1, model)
    pairs, partial_sum = slot_call(
        partial(embed_own_body, **kw),
        slots,
        [(source, "far slot"), (embed_weight, "far whole")],
        [
            ((slots, 2 * REDUCE, 2 * channels, cols), BF16, "far slot"),
            ((slots, cells, 2 * model), F32, "far slot"),
        ],
        [pltpu.VMEM((wide_cols, wide_cols), BF16)],
        name="embed_own",
        lasts=4,
    )
    top_pairs, esum, stream, normed, blocks, reduced, kv = slot_call(
        partial(embed_body, **kw, **place),
        slots,
        [
            (meta, "smem"), (partial_sum, "far slot"), (top, "far slot"), (embed_weight, "far whole"),
            (vec, "whole"), (flat_reduce, "far whole"), (key_weight, "far whole"),
            (value_weight, "far whole"),
        ],
        [
            ((slots, 2 * channels, cols), BF16, "far slot"),
            ((slots, cells, model), F32, "far slot"),
            ((slots, cells, model), F32, "slot"),
            ((slots, cells, model), BF16, "slot"),
            ((slots * keys, REDUCE * REDUCE * model), BF16, "far whole"),
            ((slots * keys, model), F32, "far whole"),
            ((slots * keys, 2 * model), BF16, "whole"),
        ],
        [
            pltpu.VMEM((wide_cols, wide_cols), BF16),
            pltpu.VMEM((cells, model), F32),
        ],
        name="embed",
        lasts=5,
    )

    grad_out = cotangent[0].reshape(slots, cells, model)
    all_cells = slots * cells
    gp, g_t = pl.pallas_call(
        partial(grouped_body, cols=cols, slots=slots),
        out_shape=[
            jax.ShapeDtypeStruct((all_cells, model), BF16),
            jax.ShapeDtypeStruct((model, all_cells), BF16),
        ],
        scratch_shapes=[pltpu.VMEM((all_cells, model), F32)],
        compiler_params=pltpu.CompilerParams(vmem_limit_bytes=VMEM_BYTES),
        cost_estimate=cost(3),
        name="grouped",
    )(grad_out)

    kv = kv.reshape(slots, keys, 2 * model)
    crossing = {n: crossed(kv, n) for n in range(tiles - 1, 0, -1)}
    kvs = [kv] + [crossing[n] for n in range(1, tiles)]
    kvs, gp, g_t = lax.optimization_barrier((kvs, gp, g_t))

    all_keys = keys * tiles
    queries, probs, attended, stream_two, normed_two, first_row, last_row, kv_all = slot_call(
        partial(attend_body, pieces=pieces, **kw, **place),
        slots,
        [
            (meta, "smem"), (normed, "slot"), (stream, "slot"), (vec, "whole"),
            (query_weight, "whole"), (output_weight, "whole"),
        ]
        + [(a, "slot") for a in kvs],
        [
            ((slots, cells, model), BF16, "far slot"),
            ((slots, cells, HEADS * all_keys), BF16, "far slot"),
            ((slots, cells, model), BF16, "far slot"),
            ((slots, cells, model), F32, "slot"),
            ((slots, cells, model), BF16, "slot"),
            ((slots, cols, model), BF16, "slot"),
            ((slots, cols, model), BF16, "slot"),
            ((slots, all_keys, 2 * model), BF16, "far slot"),
        ],
        [pltpu.VMEM((cells, HEADS * all_keys), F32)],
        name="attend",
    )

    row_up = turned_by(last_row, 1)
    row_down = turned_by(first_row, -1)
    width = 256
    vmem = pl.BlockSpec(memory_space=pltpu.VMEM)
    ext_cells = slots * (cells + 2 * cols)
    lane_tiles = width // 128
    hidden_blocks = (hidden // width,)
    by_lanes = lambda shape: pl.BlockSpec((shape[0], width), lambda b: (0, b))
    by_tiles = lambda shape: pl.BlockSpec((lane_tiles,) + tuple(shape[1:]), lambda b: (b, 0, 0))
    hidden_shape = (hidden // 128, ext_cells + 2 * GROUP * (REDUCE + 2), 128)
    conv_shape = (hidden // 128, all_cells + 2 * GROUP * REDUCE, 128)
    (
        gn_own, gn_up, gn_down, d_expand, d_shrink, d_expand_bias, active, hidden_cells, grad_conv,
    ) = pl.pallas_call(
        partial(feed_body, width=width, **kw, **place),
        in_specs=[smem()] + [vmem] * 9,
        out_specs=[vmem] * 6 + [pl.BlockSpec(memory_space=pltpu.HBM)] * 3,
        out_shape=[
            jax.ShapeDtypeStruct((slots, cells, model), F32),
            jax.ShapeDtypeStruct((slots, cols, model), BF16),
            jax.ShapeDtypeStruct((slots, cols, model), BF16),
            jax.ShapeDtypeStruct((model, hidden), F32),
            jax.ShapeDtypeStruct((hidden, model), F32),
            jax.ShapeDtypeStruct((8, hidden), F32),
            far((all_cells, hidden), BF16),
            far(hidden_shape, BF16),
            far(conv_shape, BF16),
        ],
        scratch_shapes=[pltpu.VMEM((all_cells, width), BF16)] * 2
        + [pltpu.VMEM((lane_tiles,) + hidden_shape[1:], BF16)] * 2
        + [pltpu.VMEM((lane_tiles,) + conv_shape[1:], BF16)] * 2
        + [
            pltpu.VMEM((ext_cells, width), BF16),
            pltpu.VMEM((all_cells, width), F32),
            pltpu.VMEM((ext_cells, model), F32),
            pltpu.VMEM((ext_cells, model), BF16),
            pltpu.VMEM((model + GROUP, ext_cells), BF16),
            pltpu.SemaphoreType.DMA((3, 2)),
        ],
        compiler_params=pltpu.CompilerParams(vmem_limit_bytes=VMEM_BYTES),
        cost_estimate=cost(18),
        name="feed_forward",
    )(
        meta, normed_two, row_up, row_down, gp, g_t, hv, depth_weight, expand_weight, shrink_weight
    )

    from_up = turned_by(gn_down, 1)
    from_down = turned_by(gn_up, -1)
    pairs_of_tiles = tiles // 2
    results = slot_call(
        partial(attend_back_body, pairs=pairs_of_tiles, **kw),
        slots,
        [
            (gn_own, "slot"), (from_up, "slot"), (from_down, "slot"), (stream_two, "slot"),
            (grad_out, "slot"), (attended, "far slot"), (probs, "far slot"), (queries, "far slot"),
            (normed, "slot"), (vec, "whole"), (output_weight, "whole"), (kv_all, "far slot"),
        ],
        [
            ((slots, cells, model), F32, "slot"),
            ((slots, cells, model), BF16, "slot"),
            ((model, model), F32, "whole"),
            ((model, model), F32, "whole"),
            ((VECTORS, model), F32, "whole"),
        ]
        + [((slots, 2 * keys, 2 * model), BF16, "slot")] * pairs_of_tiles,
        [
            pltpu.VMEM((cells, HEADS * all_keys), F32),
            pltpu.VMEM((cells, HEADS * all_keys), BF16),
            pltpu.VMEM((cells, model), BF16),
            pltpu.VMEM((cells, model), BF16),
        ],
        name="attend_back",
    )
    gst, gq, d_output, d_query, dvec_a = results[:5]
    dkvs = results[5:]
    crossing = {n: crossed(dkvs[n], 2 * n) for n in range(pairs_of_tiles - 1, 0, -1)}
    own_dkvs = [dkvs[0]] + [crossing[n] for n in range(1, pairs_of_tiles)]
    d_hv = pl.pallas_call(
        partial(depth_weight_body, span=cols * slots // GROUP),
        grid=hidden_blocks,
        in_specs=[by_tiles(hidden_shape), by_tiles(conv_shape), by_lanes((8, hidden))],
        out_specs=by_lanes((HIDDEN_VECTORS, hidden)),
        out_shape=jax.ShapeDtypeStruct((HIDDEN_VECTORS, hidden), F32),
        compiler_params=params(),
        cost_estimate=cost(6),
        name="depth_weights",
    )(from_far(hidden_cells), from_far(grad_conv), d_expand_bias)
    own_dkvs, d_hv = lax.optimization_barrier((own_dkvs, d_hv))
    for_mate = own_dkvs[0][:, keys:].astype(F32)
    for part in own_dkvs[1:]:
        for_mate = for_mate + part[:, keys:].astype(F32)
    own_dkvs.append(crossed(for_mate.astype(BF16), 1))

    gnb, dvec_b, keep, send = pl.pallas_call(
        partial(reduce_back_body, parts=len(own_dkvs), **place),
        in_specs=[vmem] * len(own_dkvs) + [smem()] + [vmem] * 12,
        out_specs=[vmem] * 4,
        out_shape=[
            jax.ShapeDtypeStruct((slots * keys, REDUCE * REDUCE * model), F32),
            jax.ShapeDtypeStruct((VECTORS, model), F32),
            jax.ShapeDtypeStruct((EARLY_ROWS, 128), F32),
            jax.ShapeDtypeStruct((EARLY_ROWS, 128), BF16),
        ],
        compiler_params=pltpu.CompilerParams(vmem_limit_bytes=VMEM_BYTES),
        cost_estimate=cost(3),
        name="reduce_back",
    )(
        *own_dkvs, meta, from_far(reduced), from_far(blocks), vec, flat_reduce, key_weight, value_weight,
        d_expand, d_shrink, d_hv, d_output, d_query, dvec_a,
    )
    got = lax.ppermute(send, AXES, core_level[2][0])

    ge, ge_first, dvec_c = slot_call(
        partial(embed_back_body, **kw, **place),
        slots,
        [
            (meta, "smem"), (gnb, "keys"), (gq, "slot"), (gst, "slot"), (esum, "far slot"),
            (vec, "whole"), (query_weight, "whole"), (dvec_b, "whole"),
        ],
        [
            ((slots, cells, 2 * model), BF16, "slot"),
            ((slots, cols, model), BF16, "slot"),
            ((VECTORS, model), F32, "whole"),
        ],
        [pltpu.VMEM((cells, model), F32)],
        name="embed_back",
    )
    below = turned_by(ge_first, -1)
    late_keep, late_send = slot_call(
        partial(embed_weight_body, half=channels, **place),
        slots,
        [
            (meta, "smem"), (ge, "slot"), (pairs, "far slot"), (top_pairs, "far slot"),
            (dvec_c, "whole"),
        ],
        [((LATE_ROWS, 128), F32, "whole"), ((LATE_ROWS, 128), BF16, "whole")],
        [pltpu.VMEM((9 * channels, model), F32)],
        name="embed_weights",
        lasts=3,
    )
    late_got = lax.ppermute(late_send, AXES, core_level[2][0])

    middle, high = middle_level[0], high_level[0]
    parts = jnp.concatenate(
        [
            (keep + got.astype(F32)).reshape(middle, -1, 128),
            (late_keep + late_got.astype(F32)).reshape(middle, -1, 128),
        ],
        axis=1,
    )
    (grad_input,) = slot_call(
        partial(input_back_body, half=channels, **kw),
        slots,
        [(ge, "slot"), (embed_weight, "whole")],
        [(source.shape, F32, "slot")],
        [pltpu.VMEM((wide_cols, wide_cols), BF16)],
        name="input_back",
    )
    own, sent = scatter_level(parts, middle_level)
    sent, grad_input = lax.optimization_barrier((sent, grad_input))
    own = added(own, sent)
    own, sent = scatter_level(own.reshape(high, -1, 128), high_level)
    last_line = pl.BlockSpec((1, 1, channels, wide_cols), lambda s: (s, 2 * REDUCE - 1, 0, 0))
    grad_input = pl.pallas_call(
        partial(last_row_body, half=channels, **kw, **place),
        grid=(slots,),
        in_specs=[
            smem(),
            pl.BlockSpec((1, cols, 2 * model), lambda s: (s, REDUCE - 1, 0)),
            per_slot(below.shape),
            whole(embed_weight.shape),
            pl.BlockSpec(memory_space=pl.ANY),
        ],
        out_specs=last_line,
        out_shape=jax.ShapeDtypeStruct(source.shape, F32),
        scratch_shapes=[pltpu.VMEM((wide_cols, wide_cols), BF16)],
        input_output_aliases={4: 0},
        compiler_params=params(),
        cost_estimate=cost(2),
        name="last_row",
    )(meta, ge, below, embed_weight, grad_input)
    sent, grad_input = lax.optimization_barrier((sent, grad_input))
    low = added(own, sent).astype(BF16)
    low = from_first(gather_level(low, high_level), high_level).reshape(-1, 128)
    out = pl.pallas_call(
        partial(output_body, cols=cols, slots=slots),
        out_shape=jax.ShapeDtypeStruct((slots, cells, model), BF16),
        scratch_shapes=[pltpu.VMEM((all_cells, model), F32)],
        compiler_params=pltpu.CompilerParams(vmem_limit_bytes=VMEM_BYTES),
        cost_estimate=cost(3),
        name="output",
    )(active, stream_two, vec, shrink_weight)
    gathered = gather_level(low, middle_level)
    gathered, out = lax.optimization_barrier((gathered, out))
    low = gathered.reshape(-1, 128)
    other = lax.ppermute(low, AXES, core_level[2][0])

    shapes = [(9 * channels, model), (REDUCE * REDUCE * model, model)]
    shapes += [(model, model)] * 4 + [(model, hidden), (hidden, model)]
    shapes += [(model,)] * 14 + [(hidden,), (3, 3, hidden), (hidden,)]
    results = pl.pallas_call(
        partial(unpack_body, half=channels, middle=middle, **place),
        in_specs=[smem()] + [vmem] * 2,
        out_specs=[vmem] * len(shapes),
        out_shape=[jax.ShapeDtypeStruct(shape, F32) for shape in shapes],
        compiler_params=pltpu.CompilerParams(vmem_limit_bytes=VMEM_BYTES),
        cost_estimate=cost(3),
        name="unpack",
    )(meta, low, other)
    (s_embed, s_reduce, s_query, s_key, s_value, s_output, s_expand, s_shrink) = results[:8]
    vectors = results[8:22]
    s_expand_bias, s_depth, s_depth_bias = results[22:]
    return (
        out.reshape(cotangent.shape),
        grad_input.swapaxes(2, 3)[None],
        s_embed.reshape(embed_weight.shape),
        vectors[EMBED_BIAS],
        vectors[EMBED_GAIN],
        vectors[EMBED_SHIFT],
        vectors[FIRST_GAIN],
        vectors[FIRST_SHIFT],
        s_query,
        vectors[QUERY_BIAS],
        s_reduce.reshape(reduce_weight.shape),
        vectors[REDUCE_BIAS],
        vectors[REDUCE_GAIN],
        vectors[REDUCE_SHIFT],
        s_key,
        s_value,
        vectors[VALUE_BIAS],
        s_output,
        vectors[OUTPUT_BIAS],
        vectors[SECOND_GAIN],
        vectors[SECOND_SHIFT],
        s_expand,
        s_expand_bias,
        s_depth,
        s_depth_bias,
        s_shrink,
        vectors[SHRINK_BIAS],
    )


def solution(mesh):
    shard_rows = P("batch", None, "tile", None, None)
    in_specs = (shard_rows, P("batch", None, None, None)) + (P(),) * 25 + (shard_rows,)
    out_specs = (shard_rows, shard_rows) + (P(),) * 25
    return jax.shard_map(shards, mesh=mesh, in_specs=in_specs, out_specs=out_specs, check_vma=False)
```

```python
import math
from functools import partial

import jax
import jax.numpy as jnp
from jax import lax
from jax.experimental import pallas as pl
from jax.experimental.pallas import tpu as pltpu
from jax.sharding import PartitionSpec as P

HEADS = 2
REDUCE = 4
F32 = jnp.float32
BF16 = jnp.bfloat16
HIGHEST = lax.Precision.HIGHEST
LOG2E = math.log2(math.e)
VMEM_BYTES = 32 * 1024 * 1024

(
    EMBED_BIAS,
    EMBED_GAIN,
    EMBED_SHIFT,
    FIRST_GAIN,
    FIRST_SHIFT,
    QUERY_BIAS,
    REDUCE_BIAS,
    REDUCE_GAIN,
    REDUCE_SHIFT,
    VALUE_BIAS,
    OUTPUT_BIAS,
    SECOND_GAIN,
    SECOND_SHIFT,
    SHRINK_BIAS,
) = range(14)
VECTORS = 16
HIDDEN_VECTORS = 16


def nn(left, right, precision=None):
    return lax.dot_general(
        left, right, (((1,), (0,)), ((), ())), precision=precision, preferred_element_type=F32
    )


def nt(left, right, precision=None):
    return lax.dot_general(
        left, right, (((1,), (1,)), ((), ())), precision=precision, preferred_element_type=F32
    )


def tn(left, right, precision=None):
    return lax.dot_general(
        left, right, (((0,), (0,)), ((), ())), precision=precision, preferred_element_type=F32
    )


def norm_stats(values, epsilon):
    centered = values - jnp.mean(values, axis=-1, keepdims=True)
    scale = lax.rsqrt(jnp.mean(centered * centered, axis=-1, keepdims=True) + epsilon)
    return centered * scale, scale


def norm_back(grad, hat, scale, gain):
    grad_hat = grad * gain
    mean_grad = jnp.mean(grad_hat, axis=-1, keepdims=True)
    mean_dot = jnp.mean(grad_hat * hat, axis=-1, keepdims=True)
    return scale * (grad_hat - mean_grad - hat * mean_dot)


def row_sum(values):
    return jnp.sum(values, axis=0, keepdims=True)


def params(vmem=VMEM_BYTES, axes=1):
    return pltpu.CompilerParams(
        vmem_limit_bytes=vmem, dimension_semantics=("arbitrary",) * axes
    )


def whole(shape, slots=None):
    rank = len(shape)
    return pl.BlockSpec(tuple(shape), lambda *_: (0,) * rank)


def per_slot(shape, slots=None):
    rank = len(shape)
    return pl.BlockSpec((1,) + tuple(shape[1:]), lambda s: (s,) + (0,) * (rank - 1))


def per_slot_rows(shape, slots):
    return pl.BlockSpec((shape[0] // slots, shape[1]), lambda s: (s, 0))


def smem():
    return pl.BlockSpec(memory_space=pltpu.SMEM)


def far(shape, dtype):
    return pltpu.HBM(tuple(shape), dtype)


def from_far(array):
    return pltpu.with_memory_space_constraint(array, pltpu.HBM)


def cost(microseconds):
    return pl.CostEstimate(
        flops=int(microseconds * 1.0e9), bytes_accessed=int(microseconds * 3.0e6), transcendentals=0
    )


def slot_call(body, slots, inputs, outputs, scratch=(), name=None, lasts=5, looped=False):
    kinds = {"slot": per_slot, "whole": whole, "keys": per_slot_rows}
    arrays = [(a.shape, a.dtype, k) for a, k in inputs] + list(outputs)
    names = [k.removeprefix("far ") for *_, k in arrays]
    are_far = [k.startswith("far ") for *_, k in arrays]
    count_in = len(inputs)
    moved = [n for n, is_far in enumerate(are_far) if is_far and looped]

    def spec(shape, kind, is_far):
        if kind == "smem":
            return smem()
        if looped:
            return pl.BlockSpec(memory_space=pltpu.HBM if is_far else pltpu.VMEM)
        return kinds[kind](shape, slots)

    def grid_body(*refs):
        body(pl.program_id(0), *refs)

    def loop_body(*refs):
        refs = list(refs)
        extra = refs[len(names) :]
        if moved:
            sems, extra = extra[-1], extra[:-1]
            buffers, extra = extra[len(extra) - len(moved) :], extra[: len(extra) - len(moved)]

        def copy(m, s):
            n = moved[m]
            here, there = buffers[m], refs[n]
            if names[n] == "slot":
                here, there = here.at[pl.ds(s, 1)], there.at[pl.ds(s, 1)]
            source, target = (there, here) if n < count_in else (here, there)
            return pltpu.make_async_copy(source, target, sems.at[m, s])

        into = [m for m, n in enumerate(moved) if n < count_in]
        out_of = [m for m, n in enumerate(moved) if n >= count_in]
        whole_in = [m for m in into if names[moved[m]] == "whole"]
        slot_in = [m for m in into if names[moved[m]] == "slot"]
        slot_out = [m for m in out_of if names[moved[m]] == "slot"]
        whole_out = [m for m in out_of if names[moved[m]] == "whole"]
        for m in slot_in:
            copy(m, 0).start()
        for m in whole_in:
            copy(m, 0).start()
        for s in range(1, slots):
            for m in slot_in:
                copy(m, s).start()
        local = list(refs[: len(names)])
        for m, n in enumerate(moved):
            local[n] = buffers[m]
        for m in whole_in:
            copy(m, 0).wait()

        def step(s, carry):
            views = []
            for ref, kind, (shape, *_) in zip(local, names, arrays):
                if kind == "slot":
                    ref = ref.at[pl.ds(s, 1)]
                elif kind == "keys":
                    count = shape[0] // slots
                    ref = ref.at[pl.ds(pl.multiple_of(s * count, count), count)]
                views.append(ref)
            for m in slot_in:
                copy(m, s).wait()
            body(s, *views, *extra)
            for m in slot_out:
                copy(m, s).start()
            return carry

        lax.fori_loop(0, slots, step, 0)
        for m in whole_out:
            copy(m, 0).start()
        for s in range(slots):
            for m in slot_out:
                copy(m, s).wait()
        for m in whole_out:
            copy(m, 0).wait()

    specs = [spec(shape, kind, f) for (shape, *_), kind, f in zip(arrays, names, are_far)]
    scratch = list(scratch)
    if moved:
        scratch += [pltpu.VMEM(arrays[n][0], arrays[n][1]) for n in moved]
        scratch += [pltpu.SemaphoreType.DMA((len(moved), slots))]
    return pl.pallas_call(
        loop_body if looped else grid_body,
        grid=() if looped else (slots,),
        in_specs=specs[:count_in],
        out_specs=specs[count_in:],
        out_shape=[
            (far if k.startswith("far ") else jax.ShapeDtypeStruct)(s, d) for s, d, k in outputs
        ],
        scratch_shapes=scratch,
        compiler_params=pltpu.CompilerParams(vmem_limit_bytes=VMEM_BYTES) if looped else params(),
        cost_estimate=cost(lasts),
        name=name,
    )(*[from_far(a) if k.startswith("far ") else a for a, k in inputs])


def vmem_call(body, inputs, outputs, scratch=(), name=None, lasts=5):
    vmem = pl.BlockSpec(memory_space=pltpu.VMEM)
    return pl.pallas_call(
        body,
        in_specs=[smem() if a.dtype == jnp.int32 else vmem for a in inputs],
        out_specs=[vmem] * len(outputs),
        out_shape=[jax.ShapeDtypeStruct(shape, dtype) for shape, dtype in outputs],
        scratch_shapes=list(scratch),
        compiler_params=pltpu.CompilerParams(vmem_limit_bytes=VMEM_BYTES),
        cost_estimate=cost(lasts),
        name=name,
    )(*inputs)


def flat_rows(ref):
    return ref[...].reshape(-1, ref.shape[-1])


def by_slot(values, slots):
    count = values.shape[0] // slots
    return [values[s * count : (s + 1) * count] for s in range(slots)]


def tile_ids(meta, s, tile, tiles):
    at = (s * tiles + tile) * 2
    return meta[at], meta[at + 1]


def tile_place(meta, slots, tiles):
    return meta[slots * tiles * 2]


def core_place(meta, slots, tiles):
    return meta[slots * tiles * 2 + 1]


def middle_place(meta, slots, tiles):
    return meta[slots * tiles * 2 + 2]


def as_flag(condition):
    return jnp.where(condition, 1.0, 0.0).astype(F32)


def same_flags(meta, s, slots, tiles):
    at = tile_place(meta, slots, tiles)
    own = tile_ids(meta, s, at, tiles)
    up = tile_ids(meta, s, jnp.maximum(at - 1, 0), tiles)
    down = tile_ids(meta, s, jnp.minimum(at + 1, tiles - 1), tiles)
    return (
        as_flag(own[0] == own[1]),
        as_flag((own[0] == up[0]) & (at > 0)),
        as_flag((own[0] == down[0]) & (at < tiles - 1)),
    )


def split_columns(size):
    source = lax.broadcasted_iota(jnp.int32, (size, size), 0)
    target = lax.broadcasted_iota(jnp.int32, (size, size), 1)
    wanted = jnp.where(target < size // 2, 2 * target, 2 * target - size + 1)
    return jnp.where(source == wanted, 1.0, 0.0).astype(BF16)


def embed_weights(ew):
    half = ew.shape[2]
    none = jnp.zeros_like(ew[0, 0])
    weights = []
    for a in range(3):
        main = ew[a, 1:3].reshape(2 * half, 128)
        side = jnp.concatenate([none, ew[a, 0]], axis=0)
        weights.append(jnp.concatenate([main, side], axis=1))
    return jnp.concatenate(weights, axis=0)


def embed_own_body(s, x, ew, pairs, partial_sum, split, *, cols):
    half = x.shape[2]

    @pl.when(s == 0)
    def _():
        split[...] = split_columns(2 * cols)

    own = nn(x[0].reshape(2 * REDUCE * half, 2 * cols), split[...])
    for r in range(2 * REDUCE):
        row = own[r * half : (r + 1) * half].astype(BF16)
        pairs[0, r, :half] = row[:, :cols]
        pairs[0, r, half:] = row[:, cols:]
    weights = embed_weights(ew)
    for i in range(REDUCE):
        first = max(2 * i - 1, 0)
        lines = pairs[0, first : 2 * i + 2]
        lines = lines.reshape(lines.shape[0] * 128, cols)
        partial_sum[0, i * cols : (i + 1) * cols] = tn(lines, weights[-lines.shape[0] :])


def side_mask(meta, slots, tiles, cols, rows, forward):
    column = lax.broadcasted_iota(jnp.int32, (rows * cols, 1), 0) % cols
    outside = 0 if forward else cols - 1
    border = cols // 2 if forward else cols // 2 - 1
    masks = []
    for s in range(slots):
        same_sides, _, _ = same_flags(meta, s, slots, tiles)
        masks.append(jnp.where(column == outside, 0.0, jnp.where(column == border, same_sides, 1.0)))
    return jnp.concatenate(masks, axis=0)


def embed_body(
    meta, partial_sum, top, ew, vec, rw, kw, vw,
    top_pairs, esum, stream, normed, blocks, reduced, kv,
    nbuf, *, cols, slots, tiles,
):
    keys = cols // REDUCE
    cells = REDUCE * cols
    half = top.shape[1]
    above = by_slot(nn(flat_rows(top), split_columns(2 * cols)), slots)
    weights = embed_weights(ew)[:128]
    lines = []
    for s in range(slots):
        _, same_up, _ = same_flags(meta, s, slots, tiles)
        row = (above[s] * same_up).astype(BF16)
        top_pairs[s, :half] = row[:, :cols]
        top_pairs[s, half:] = row[:, cols:]
        lines += [partial_sum[s, :cols] + tn(top_pairs[s], weights), partial_sum[s, cols:]]
    z = jnp.concatenate(lines, axis=0)
    mask = side_mask(meta, slots, tiles, cols, REDUCE, True)
    value = z[:, :128] + pltpu.roll(z[:, 128:], 1, 0) * mask + vec[EMBED_BIAS : EMBED_BIAS + 1]
    esum[...] = value.reshape(esum.shape)
    hat, _ = norm_stats(value, 1e-05)
    st = hat * vec[EMBED_GAIN : EMBED_GAIN + 1] + vec[EMBED_SHIFT : EMBED_SHIFT + 1]
    stream[...] = st.reshape(stream.shape)
    hat, _ = norm_stats(st, 1e-06)
    nm = hat * vec[FIRST_GAIN : FIRST_GAIN + 1] + vec[FIRST_SHIFT : FIRST_SHIFT + 1]
    low = nm.astype(BF16)
    normed[...] = low.reshape(normed.shape)
    nbuf[...] = low.astype(F32)
    for s in range(slots):
        for a in range(REDUCE):
            for b in range(REDUCE):
                at = (a * REDUCE + b) * 128
                piece = nbuf[pl.ds(s * cells + a * cols + b, keys, REDUCE), :]
                blocks[s * keys : (s + 1) * keys, at : at + 128] = piece.astype(BF16)
    value = nn(blocks[...], rw[...]) + vec[REDUCE_BIAS : REDUCE_BIAS + 1]
    reduced[...] = value
    hat, _ = norm_stats(value, 1e-06)
    rn = (hat * vec[REDUCE_GAIN : REDUCE_GAIN + 1] + vec[REDUCE_SHIFT : REDUCE_SHIFT + 1]).astype(BF16)
    kv[:, :128] = nn(rn, kw[...]).astype(BF16)
    kv[:, 128:] = (nn(rn, vw[...]) + vec[VALUE_BIAS : VALUE_BIAS + 1]).astype(BF16)


def both_heads(kv, s, at):
    rows = kv[s, :, at : at + 128]
    lane = lax.broadcasted_iota(jnp.int32, rows.shape, 1)
    zero = jnp.zeros_like(rows)
    return jnp.concatenate(
        [jnp.where(lane < 64, rows, zero), jnp.where(lane < 64, zero, rows)], axis=0
    )


def key_bias(meta, s, slots, tiles, keys):
    at = tile_place(meta, slots, tiles)
    own = tile_ids(meta, s, at, tiles)
    part = keys // (2 * tiles)
    entry = lax.broadcasted_iota(jnp.int32, (1, keys), 1) // part
    rows = [jnp.zeros((1, keys), F32) for _ in range(2)]
    for n in range(tiles):
        ids = tile_ids(meta, s, at ^ n, tiles)
        for side in range(2):
            for query in range(2):
                value = jnp.where(ids[side] == own[query], 0.0, -1e30).astype(F32)
                rows[query] = jnp.where(entry == 2 * n + side, value, rows[query])
    return rows


EDGE_ROWS = (0, REDUCE - 1)
INNER_ROWS = tuple(range(1, REDUCE - 1))


def pick_rows(ref, rows, cols):
    lines = [ref[s, i * cols : (i + 1) * cols] for s in range(ref.shape[0]) for i in rows]
    return jnp.concatenate(lines, axis=0)


def attend_body(*refs, pieces, cols, slots, tiles, rows):
    edge = rows == EDGE_ROWS
    (meta, normed, stream, vec, qw, ow), refs = refs[:6], refs[6:]
    if edge:
        kvs, refs = refs[:pieces], refs[pieces:]
        queries, probs, attended, stream_two, first_row, last_row, kv_all, sbuf = refs
        for s in range(slots):
            kv_all[s] = jnp.concatenate([p[s] for p in kvs], axis=0)
    else:
        kv_all, queries, probs, attended, stream_two, normed_two, sbuf = refs
    q = nn(pick_rows(normed, rows, cols), qw[...]) + vec[QUERY_BIAS : QUERY_BIAS + 1]
    queries[...] = q.astype(BF16).reshape(queries.shape)
    for s in range(slots):
        sbuf[s] = nt(queries[s], both_heads(kv_all, s, 0))
    keys = sbuf.shape[2] // HEADS
    factor = LOG2E * (128 // HEADS) ** (-0.5)
    column = lax.broadcasted_iota(jnp.int32, (len(rows) * cols, 1), 0) % cols
    for s in range(slots):
        left, right = key_bias(meta, s, slots, tiles, keys)
        bias = jnp.where(column < cols // 2, left, right)
        for h in range(HEADS):
            span = slice(h * keys, (h + 1) * keys)
            score = sbuf[s, :, span] * factor + bias
            e = jnp.exp2(score - jnp.max(score, axis=-1, keepdims=True))
            p = e * (1.0 / jnp.sum(e, axis=-1, keepdims=True))
            probs[s, :, span] = p.astype(BF16)
    for s in range(slots):
        attended[s] = nn(probs[s], both_heads(kv_all, s, 128)).astype(BF16)
    value = pick_rows(stream, rows, cols) + nn(flat_rows(attended), ow[...])
    value = value + vec[OUTPUT_BIAS : OUTPUT_BIAS + 1]
    stream_two[...] = value.reshape(stream_two.shape)
    hat, _ = norm_stats(value, 1e-06)
    low = (hat * vec[SECOND_GAIN : SECOND_GAIN + 1] + vec[SECOND_SHIFT : SECOND_SHIFT + 1]).astype(BF16)
    if edge:
        for s, part in enumerate(by_slot(low, slots)):
            first_row[s] = part[:cols]
            last_row[s] = part[cols:]
    else:
        normed_two[...] = low.reshape(normed_two.shape)


DENSITY = 1.0 / math.sqrt(2.0 * math.pi)


def gelu_pair(x):
    twice_cdf = 1.0 + lax.erf(x * math.sqrt(0.5))
    e = jnp.exp2((x * x) * (-0.5 * LOG2E))
    return x * twice_cdf, twice_cdf + x * (e * (2.0 * DENSITY))


GROUP = 16


def fold_rows(values):
    return values[: GROUP // 2] + values[GROUP // 2 :]


def group(n):
    return slice(n * GROUP, (n + 1) * GROUP)


def group_places(r, s, q, cols, slots):
    spans = GROUP // slots
    span = cols // spans
    return pl.ds(r * span * GROUP + s * spans + q, span, GROUP)


def grouped_body(g, gp, g_t, buf, *, cols, slots):
    spans = GROUP // slots
    span = cols // spans
    line = span * GROUP
    for s in range(slots):
        for q in range(spans):
            for r in range(REDUCE):
                row = g[s, r * cols + q * span : r * cols + (q + 1) * span]
                buf[group_places(r, s, q, cols, slots), :] = row.astype(F32)
    for r in range(REDUCE):
        rows = slice(r * line, (r + 1) * line)
        gp[rows] = buf[rows].astype(BF16)
        g_t[:, rows] = gp[rows].T


def feed_body(
    meta, nt_first, nt_inner, nt_last, nt_up, nt_down, gp, g_t, hv, dw, ew, sw,
    gn_edge, gn_inner, gn_up, gn_down, dew, dsw, deb, a_out, h_out, c_out,
    abuf0, abuf1, hbuf0, hbuf1, cbuf0, cbuf1, ghbuf, gabuf, gnacc, ext, ext_t, sems,
    *, cols, slots, tiles, width,
):
    abufs, hbufs, cbufs = (abuf0, abuf1), (hbuf0, hbuf1), (cbuf0, cbuf1)
    model = ew.shape[0]
    blocks = ew.shape[1] // width
    spans = GROUP // slots
    span = cols // spans
    line = span * GROUP
    padded = line + 2 * GROUP
    rows_in = REDUCE + 2
    lane_tiles = width // 128

    def copies(b, side):
        lanes = pl.ds(pl.multiple_of(b * width, width), width)
        tiles_at = pl.ds(b * lane_tiles, lane_tiles)
        pairs = (
            (abufs, a_out.at[:, lanes]), (hbufs, h_out.at[tiles_at]), (cbufs, c_out.at[tiles_at]),
        )
        return [
            pltpu.make_async_copy(bufs[side], there, sems.at[n, side])
            for n, (bufs, there) in enumerate(pairs)
        ]

    sub = lax.broadcasted_iota(jnp.int32, (GROUP, 1), 0)
    at_slot, at_span = sub // spans, sub % spans
    same = [jnp.zeros((GROUP, 1), F32) for _ in range(3)]
    for s in range(slots):
        flags = same_flags(meta, s, slots, tiles)
        same = [jnp.where(at_slot == s, flag, mask) for flag, mask in zip(flags, same)]
    sides, same_up, same_down = same
    from_left = jnp.where(at_span == 0, 0.0, jnp.where(at_span == spans // 2, sides, 1.0))
    from_right = jnp.where(
        at_span == spans - 1, 0.0, jnp.where(at_span == spans // 2 - 1, sides, 1.0)
    )
    low_up = jnp.broadcast_to(same_up, (GROUP, 128)).astype(BF16)
    low_down = jnp.broadcast_to(same_down, (GROUP, 128)).astype(BF16)

    for s in range(slots):
        for q in range(spans):
            for r in range(rows_in):
                if 2 <= r < rows_in - 2:
                    at = (r - 2) * cols + q * span
                    row = nt_inner[s, at : at + span]
                else:
                    lines = {0: nt_up, 1: nt_first, rows_in - 2: nt_last, rows_in - 1: nt_down}
                    row = lines[r][s, q * span : (q + 1) * span]
                gnacc[group_places(r, s, q, cols, slots), :] = row.astype(F32)
    for r in range(rows_in):
        rows = slice(r * line, (r + 1) * line)
        ext[rows] = gnacc[rows].astype(BF16)
        ext_t[:model, rows] = ext[rows].T
    ext_t[model:] = jnp.ones_like(ext_t[model:])
    gnacc[...] = jnp.zeros_like(gnacc)

    def ghosts(buf, rows):
        for t in range(lane_tiles):
            for r in range(rows):
                base = r * padded
                first = buf[t, base + GROUP : base + 2 * GROUP].astype(F32)
                last = buf[t, base + line : base + line + GROUP].astype(F32)
                left = pltpu.roll(last, 1, 0) * from_left
                right = pltpu.roll(first, GROUP - 1, 0) * from_right
                buf[t, base : base + GROUP] = left.astype(BF16)
                buf[t, base + line + GROUP : base + padded] = right.astype(BF16)

    def taps_of(lanes):
        return [
            [jnp.broadcast_to(dw[a, c : c + 1, lanes], (GROUP, 128)) for c in range(3)]
            for a in range(3)
        ]

    def block(b, side):
        abuf, hbuf, cbuf = abufs[side], hbufs[side], cbufs[side]
        to_a, to_h, to_c = copies(b, side)
        at = pl.multiple_of(b * width, width)
        ewb = ew[:, pl.ds(at, width)]
        half_sw = sw[pl.ds(at, width), :] * 0.5
        bias = hv[0:1, pl.ds(at, width)]
        for r in range(rows_in):
            hid = nn(ext[r * line : (r + 1) * line], ewb) + bias
            if r == 0 or r == rows_in - 1:
                mask = same_up if r == 0 else same_down
                hid = (hid.reshape(span, GROUP, width) * mask[None]).reshape(line, width)
            for t in range(lane_tiles):
                base = r * padded + GROUP
                hbuf[t, base : base + line] = hid[:, t * 128 : (t + 1) * 128].astype(BF16)
        ghosts(hbuf, rows_in)
        to_h.start()
        for r in range(REDUCE):
            rows = slice(r * line, (r + 1) * line)
            gabuf[rows] = nt(gp[rows], half_sw)
        for t in range(lane_tiles):
            lanes = slice(t * 128, (t + 1) * 128)
            spot = pl.ds(pl.multiple_of(at + t * 128, 128), 128)
            taps = taps_of(spot)
            depth_bias = hv[1:2, spot]
            for col in range(span):
                h = [
                    [hbuf[t, group(r * (span + 2) + col + d)] for d in range(3)]
                    for r in range(rows_in)
                ]
                for i in range(REDUCE):
                    conv = None
                    for a in range(3):
                        for c in range(3):
                            term = h[i + a][c] * taps[a][c]
                            conv = term if conv is None else conv + term
                    act, slope = gelu_pair(conv.astype(F32) + depth_bias)
                    rows = group(i * span + col)
                    abuf[rows, lanes] = act.astype(BF16)
                    grad = gabuf[rows, lanes] * slope
                    cbuf[t, group(i * (span + 2) + col + 1)] = grad.astype(BF16)
        to_a.start()
        ghosts(cbuf, REDUCE)
        to_c.start()
        for t in range(lane_tiles):
            lanes = slice(t * 128, (t + 1) * 128)
            taps = taps_of(pl.ds(pl.multiple_of(at + t * 128, 128), 128))
            for col in range(span):
                gc = [
                    [cbuf[t, group(i * (span + 2) + col + d)] for d in range(3)]
                    for i in range(REDUCE)
                ]
                for r in range(rows_in):
                    gh = None
                    for a in range(3):
                        if not 0 <= r - a < REDUCE:
                            continue
                        for c in range(3):
                            term = gc[r - a][2 - c] * taps[a][c]
                            gh = term if gh is None else gh + term
                    if r == 0:
                        gh = gh * low_up
                    if r == rows_in - 1:
                        gh = gh * low_down
                    ghbuf[group(r * span + col), lanes] = gh
        for r in range(rows_in):
            rows = slice(r * line, (r + 1) * line)
            gnacc[rows] += nt(ghbuf[rows], ewb)
        grad = nn(ext_t[...], ghbuf[...])
        dew[:, pl.ds(at, width)] = grad[:model]
        deb[:, pl.ds(at, width)] = grad[model : model + 8]
        dsw[pl.ds(at, width), :] = nn(g_t[...], abuf[...]).T * 0.5

    def two_blocks(k, carry):
        for side in range(2):
            b = 2 * k + side

            @pl.when(k > 0)
            def _():
                for copy in copies(b - 2, side):
                    copy.wait()

            block(b, side)
        return carry

    lax.fori_loop(0, blocks // 2, two_blocks, 0)
    for s in range(slots):
        for q in range(spans):
            there = slice(q * span, (q + 1) * span)
            for r in range(rows_in):
                grad = gnacc[group_places(r, s, q, cols, slots), :]
                if r == 0:
                    gn_up[s, there] = grad.astype(BF16)
                elif r == rows_in - 1:
                    gn_down[s, there] = grad.astype(BF16)
                elif r in (1, rows_in - 2):
                    at = (0 if r == 1 else cols) + q * span
                    gn_edge[s, at : at + span] = grad
                else:
                    at = (r - 2) * cols + q * span
                    gn_inner[s, at : at + span] = grad
    for side in range(2):
        for copy in copies(blocks - 2 + side, side):
            copy.wait()


def depth_weight_body(hbuf, cbuf, deb, dhv, *, span):
    dhv[...] = jnp.zeros_like(dhv)
    dhv[0:1] = deb[0:1]
    per_sum = 4
    for t in range(hbuf.shape[0]):
        lanes = slice(t * 128, (t + 1) * 128)
        sums = [jnp.zeros((GROUP // 2, 128), F32) for _ in range(10)]
        for m in range(span // per_sum):
            parts = [None] * 10
            for col in range(per_sum * m, per_sum * (m + 1)):
                h = [
                    [hbuf[t, group(r * (span + 2) + col + d)] for d in range(3)]
                    for r in range(REDUCE + 2)
                ]
                for i in range(REDUCE):
                    gc = cbuf[t, group(i * (span + 2) + col + 1)]
                    terms = [gc] + [gc * h[i + a][c] for a in range(3) for c in range(3)]
                    parts = [
                        term if part is None else part + term for part, term in zip(parts, terms)
                    ]
            sums = [total + fold_rows(part.astype(F32)) for total, part in zip(sums, parts)]
        for n in range(10):
            dhv[1 + n : 2 + n, lanes] = row_sum(sums[n])


def output_body(abuf, stream_edge, stream_inner, vec, sw, out, acc, *, cols, slots):
    spans = GROUP // slots
    span = cols // spans
    line = span * GROUP
    for r in range(REDUCE):
        rows = slice(r * line, (r + 1) * line)
        acc[rows] = nn(abuf[rows], sw[...] * 0.5)
    for s in range(slots):
        for q in range(spans):
            for r in range(REDUCE):
                there = slice(r * cols + q * span, r * cols + (q + 1) * span)
                part = stream_edge if r in EDGE_ROWS else stream_inner
                at = (EDGE_ROWS if r in EDGE_ROWS else INNER_ROWS).index(r) * cols + q * span
                value = acc[group_places(r, s, q, cols, slots), :] + part[s, at : at + span]
                out[s, there] = (value + vec[SHRINK_BIAS : SHRINK_BIAS + 1]).astype(BF16)


def attend_back_body(*refs, pairs, cols, slots, rows):
    edge = rows == EDGE_ROWS
    (gn, stream_two, g, attended, probs, queries, normed, vec, ow, kv_all), refs = refs[:10], refs[10:]
    if edge:
        (up, down, dkv_in, dow_in, dqw_in, dvec_in), refs = refs[:6], refs[6:]
    (gst, gq, dow, dqw, dvec), refs = refs[:5], refs[5:]
    dkvs, (gpbuf, dsbuf, branch, gabuf) = refs[:-4], refs[-4:]
    grad = flat_rows(gn)
    if edge:
        lines = [part[s] for s in range(slots) for part in (up, down)]
        grad = grad + jnp.concatenate(lines, axis=0).astype(F32)
    hat, scale = norm_stats(flat_rows(stream_two), 1e-06)
    gi = pick_rows(g, rows, cols).astype(F32)
    value = norm_back(grad, hat, scale, vec[SECOND_GAIN : SECOND_GAIN + 1]) + gi
    gst[...] = value.reshape(gst.shape)
    low = value.astype(BF16)
    branch[...] = low
    gabuf[...] = nt(low, ow[...]).astype(BF16)
    count = len(rows) * cols
    keys = gpbuf.shape[2] // HEADS
    for s in range(slots):
        gpbuf[s] = nt(gabuf[s * count : (s + 1) * count], both_heads(kv_all, s, 128))
    for s in range(slots):
        for h in range(HEADS):
            span = slice(h * keys, (h + 1) * keys)
            p = probs[s, :, span].astype(F32)
            gp = gpbuf[s, :, span]
            inner = jnp.sum(gp * p, axis=-1, keepdims=True)
            dsbuf[s, :, span] = (p * (gp - inner)).astype(BF16)
    factor = (128 // HEADS) ** (-0.5)
    for s in range(slots):
        gq[s] = (nn(dsbuf[s], both_heads(kv_all, s, 0)) * factor).astype(BF16)

    def fold(both):
        return jnp.concatenate([both[:64, :keys], both[64:, keys:]], axis=0).T

    for s in range(slots):
        dk = fold(nn(queries[s].T, dsbuf[s])) * factor
        dv = fold(nn(gabuf[s * count : (s + 1) * count].T, probs[s]))
        dkv = jnp.concatenate([dk, dv], axis=1)
        if edge:
            dkv = (dkv + dkv_in[s]).astype(BF16)
            each = keys // pairs
            for n in range(pairs):
                dkvs[n][s] = dkv[n * each : (n + 1) * each]
        else:
            dkvs[0][s] = dkv
    dow[...] = tn(flat_rows(attended), branch[...])
    dqw[...] = tn(pick_rows(normed, rows, cols), flat_rows(gq))
    sums = {
        SECOND_GAIN: row_sum(grad * hat),
        SECOND_SHIFT: row_sum(grad),
        SHRINK_BIAS: row_sum(gi),
        OUTPUT_BIAS: row_sum(branch[...].astype(F32)),
        QUERY_BIAS: row_sum(flat_rows(gq).astype(F32)),
    }
    none = jnp.zeros((1, 128), F32)
    dvec[...] = jnp.concatenate([sums.get(n, none) for n in range(VECTORS)], axis=0)
    if edge:
        dow[...] += dow_in[...]
        dqw[...] += dqw_in[...]
        dvec[...] += dvec_in[...]


def reduce_back_body(*refs, parts, slots, tiles):
    arrived, refs = refs[:parts], refs[parts:]
    (meta, reduced, blocks, vec, rw, kw, vw, dexpand, dshrink, dhv, doutput, dquery, dvec_in) = refs[:13]
    gnb, dvec, keep, send = refs[13:]
    upper = core_place(meta, slots, tiles) == 1

    def place(chunk, first, second):
        rows = slice(chunk * 128, (chunk + 1) * 128)
        keep[rows] = jnp.where(upper, second, first)
        send[rows] = jnp.where(upper, first, second).astype(BF16)

    keys = reduced.shape[0] // slots
    dkv = arrived[-1][...].astype(F32)
    for part in arrived[:-1]:
        dkv = dkv + part[:, :keys].astype(F32)
    dkv = dkv.reshape(slots * keys, 256)
    dk, dv = dkv[:, :128], dkv[:, 128:]
    hat, scale = norm_stats(reduced[...], 1e-06)
    gain = vec[REDUCE_GAIN : REDUCE_GAIN + 1]
    rn = (hat * gain + vec[REDUCE_SHIFT : REDUCE_SHIFT + 1]).astype(BF16).astype(F32)
    dkw = tn(rn, dk, HIGHEST)
    dvw = tn(rn, dv, HIGHEST)
    grad = nt(dk, kw[...].astype(F32), HIGHEST) + nt(dv, vw[...].astype(F32), HIGHEST)
    low = norm_back(grad, hat, scale, gain).astype(BF16)
    gnb[...] = nt(low, rw[...])
    sums = {
        VALUE_BIAS: row_sum(dv),
        REDUCE_GAIN: row_sum(grad * hat),
        REDUCE_SHIFT: row_sum(grad),
        REDUCE_BIAS: row_sum(low.astype(F32)),
    }
    dvec[...] = jnp.concatenate(
        [sums.get(n, dvec_in[n : n + 1]) for n in range(VECTORS)], axis=0
    )
    spans = dexpand.shape[1] // 128
    second = [dexpand[:, t * 128 : (t + 1) * 128] for t in range(spans)]
    second += [dshrink[t * 128 : (t + 1) * 128] for t in range(spans)]
    second += [jnp.concatenate([dhv[:, t * 128 : (t + 1) * 128] for t in range(spans)], axis=0)]
    second += [doutput[...], dquery[...]]
    first = [tn(blocks[:, t * 128 : (t + 1) * 128], low) for t in range(REDUCE * REDUCE)]
    first += [dkw, dvw, jnp.zeros((128, 128), F32)]
    for chunk, (one, two) in enumerate(zip(first, second, strict=True)):
        place(chunk, one, two)


EARLY_ROWS = 19 * 128
LATE_ROWS = 3 * 128


def embed_back_body(
    meta, gnb, gq_edge, gq_inner, gst_edge, gst_inner, esum, vec, qw, dvec_in,
    ge, ge_first, dvec,
    gbuf, *, cols, slots, tiles,
):
    keys = cols // REDUCE
    cells = REDUCE * cols
    for s in range(slots):
        for a in range(REDUCE):
            for b in range(REDUCE):
                at = (a * REDUCE + b) * 128
                piece = gnb[s * keys : (s + 1) * keys, at : at + 128]
                gbuf[pl.ds(s * cells + a * cols + b, keys, REDUCE), :] = piece

    def joined(edge, inner):
        lines = []
        for s in range(slots):
            lines += [edge[s, :cols], inner[s], edge[s, cols:]]
        return jnp.concatenate(lines, axis=0)

    grad = gbuf[...] + nt(joined(gq_edge, gq_inner), qw[...])
    gain = vec[EMBED_GAIN : EMBED_GAIN + 1]
    hat, scale = norm_stats(flat_rows(esum), 1e-05)
    hat_one, scale_one = norm_stats(hat * gain + vec[EMBED_SHIFT : EMBED_SHIFT + 1], 1e-06)
    sums = {FIRST_GAIN: row_sum(grad * hat_one), FIRST_SHIFT: row_sum(grad)}
    grad = norm_back(grad, hat_one, scale_one, vec[FIRST_GAIN : FIRST_GAIN + 1])
    grad = grad + joined(gst_edge, gst_inner)
    sums[EMBED_GAIN] = row_sum(grad * hat)
    sums[EMBED_SHIFT] = row_sum(grad)
    low = norm_back(grad, hat, scale, gain).astype(BF16)
    wide = low.astype(F32)
    sums[EMBED_BIAS] = row_sum(wide)
    dvec[...] = jnp.concatenate(
        [sums.get(n, dvec_in[n : n + 1]) for n in range(VECTORS)], axis=0
    )
    for s, part in enumerate(by_slot(wide, slots)):
        _, same_up, _ = same_flags(meta, s, slots, tiles)
        ge_first[s] = (part[:cols] * same_up).astype(BF16)
    mask = side_mask(meta, slots, tiles, cols, REDUCE, False)
    shifted = (pltpu.roll(wide, slots * cells - 1, 0) * mask).astype(BF16)
    ge[:, :, :128] = low.reshape(slots, cells, 128)
    ge[:, :, 128:] = shifted.reshape(slots, cells, 128)


def embed_weight_body(meta, ge, pairs, top_pairs, dvec, keep, send, *, half, slots, tiles):
    upper = core_place(meta, slots, tiles) == 1
    all_ge = ge[...].reshape(-1, ge.shape[2])
    parts = []
    for a in range(3):
        lines = [(s, 2 * i + a - 1) for s in range(slots) for i in range(REDUCE)]
        lhs = [top_pairs[s] if n < 0 else pairs[s, n] for s, n in lines]
        part = nn(jnp.concatenate(lhs, axis=1), all_ge)
        parts += [part[half:, 128:], part[:, :128]]
    dew = jnp.concatenate(parts, axis=0)
    count = 9 * half // 2
    first, second = dew[:count], dew[count:]
    keep[:count] = jnp.where(upper, second, first)
    send[:count] = jnp.where(upper, first, second).astype(BF16)
    vectors = dvec[...]
    none = jnp.zeros_like(vectors)
    end = count + VECTORS
    keep[count:end] = jnp.where(upper, none, vectors)
    send[count:end] = jnp.where(upper, vectors, none).astype(BF16)
    keep[end:] = jnp.zeros((LATE_ROWS - end, 128), F32)
    send[end:] = jnp.zeros((LATE_ROWS - end, 128), BF16)


def spread_weights(ew, a):
    none = jnp.zeros_like(ew[0, 0])
    even = jnp.concatenate([ew[a, 1], none], axis=1)
    odd = jnp.concatenate([ew[a, 2], ew[a, 0]], axis=1)
    return jnp.concatenate([even, odd], axis=0)


def mixed_columns(lines, split, half, cols):
    lines = [jnp.concatenate([part[:half], part[half:]], axis=1) for part in lines]
    mixed = nt(jnp.concatenate(lines, axis=0), split[...])
    return mixed.reshape(len(lines), half, 2 * cols)


def input_back_body(s, ge, ew, gx, split, *, cols, half):
    @pl.when(s == 0)
    def _():
        split[...] = split_columns(2 * cols)

    own = ge[0]
    upper_rows = nt(spread_weights(ew, 1), own).astype(BF16)
    inner = nt(spread_weights(ew, 2), own[:-cols]) + nt(spread_weights(ew, 0), own[cols:])
    inner = inner.astype(BF16)
    lines = []
    for i in range(REDUCE):
        cells = slice(i * cols, (i + 1) * cols)
        lines.append(upper_rows[:, cells])
        lines.append(inner[:, cells] if i < REDUCE - 1 else jnp.zeros_like(upper_rows[:, cells]))
    gx[0] = mixed_columns(lines, split, half, cols)


def last_row_body(meta, ge, below, ew, done, gx, split, *, cols, half, slots, tiles):
    s = pl.program_id(0)
    same_sides, _, _ = same_flags(meta, s, slots, tiles)

    @pl.when(s == 0)
    def _():
        split[...] = split_columns(2 * cols)

    column = lax.broadcasted_iota(jnp.int32, (cols, 1), 0)
    mask = jnp.where(column == cols - 1, 0.0, jnp.where(column == cols // 2 - 1, same_sides, 1.0))
    shifted = (pltpu.roll(below[0].astype(F32), cols - 1, 0) * mask).astype(BF16)
    under = jnp.concatenate([below[0], shifted], axis=1)
    line = nt(spread_weights(ew, 2), ge[0]) + nt(spread_weights(ew, 0), under)
    gx[0] = mixed_columns([line.astype(BF16)], split, half, cols)


def unpack_body(meta, own, other, *outs, slots, tiles, half, middle):
    upper = core_place(meta, slots, tiles) == 1
    at = middle_place(meta, slots, tiles)
    early, late = EARLY_ROWS // middle, LATE_ROWS // middle

    def pick(start, count, base, size):
        step = math.gcd(size, 128)
        mine, theirs = [], []
        for row in range(start, start + count, step):
            chunk, offset = divmod(row, size)
            where = (chunk ^ at) * (early + late) + base + offset
            rows = pl.ds(pl.multiple_of(where, math.gcd(step, 16)), step)
            mine.append(own[rows])
            theirs.append(other[rows])
        mine = jnp.concatenate(mine, axis=0).astype(F32)[:count]
        theirs = jnp.concatenate(theirs, axis=0).astype(F32)[:count]
        return jnp.where(upper, theirs, mine), jnp.where(upper, mine, theirs)

    (embed, reduce, query, key, value, output, expand, shrink, *vectors) = outs
    spans = expand.shape[1] // 128
    taps = REDUCE * REDUCE
    for chunk in range(EARLY_ROWS // 128):
        first, second = pick(chunk * 128, 128, 0, early)
        if chunk < taps:
            reduce[chunk * 128 : (chunk + 1) * 128] = first
        elif chunk == taps:
            key[...] = first
        elif chunk == taps + 1:
            value[...] = first
        if chunk < spans:
            expand[:, chunk * 128 : (chunk + 1) * 128] = second
        elif chunk < 2 * spans:
            shrink[(chunk - spans) * 128 : (chunk - spans + 1) * 128] = second
        elif chunk == 2 * spans:
            hidden_vectors = second
        elif chunk == 2 * spans + 1:
            output[...] = second
        else:
            query[...] = second
    count = 9 * half // 2
    first, second = pick(0, count + VECTORS, early, late)
    embed[:count] = first[:count]
    embed[count:] = second[:count]
    *short, expand_bias, depth, depth_bias = vectors
    for n, out in enumerate(short):
        out[...] = first[count + n]
    for t in range(spans):
        lanes = slice(t * 128, (t + 1) * 128)
        at = t * HIDDEN_VECTORS
        expand_bias[lanes] = hidden_vectors[at]
        depth_bias[lanes] = hidden_vectors[at + 1]
        for a in range(3):
            depth[a, :, lanes] = hidden_vectors[at + 2 + 3 * a : at + 5 + 3 * a]


def turned_by(array, distance):
    count = lax.axis_size("tile")
    return lax.ppermute(array, "tile", [(i, (i + distance) % count) for i in range(count)])


def crossed(array, bits):
    count = lax.axis_size("tile")
    return lax.ppermute(array, "tile", [(i, i ^ bits) for i in range(count)])


def device_levels():
    batch_count, tile_count = lax.axis_size("batch"), lax.axis_size("tile")
    batch_at, tile_at = lax.axis_index("batch"), lax.axis_index("tile")

    def routes(size, target):
        return [
            [
                (b * tile_count + t, target(b, t, turn))
                for b in range(batch_count)
                for t in range(tile_count)
            ]
            for turn in range(1, size)
        ]

    def flat(batch, tile):
        return batch * tile_count + tile

    return (
        (2, batch_at % 2, routes(2, lambda b, t, turn: flat(b ^ turn, t))),
        (
            batch_count,
            (batch_at // 2) * 2 + tile_at % 2,
            routes(batch_count, lambda b, t, turn: flat(b ^ (turn // 2 * 2), t ^ (turn % 2))),
        ),
        (
            tile_count // 2,
            tile_at // 2,
            routes(tile_count // 2, lambda b, t, turn: flat(b, t ^ (2 * turn))),
        ),
    )


AXES = ("batch", "tile")


def scatter_level(parts, level):
    size, at, turns = level
    own = lax.dynamic_index_in_dim(parts, at, 0, keepdims=False)
    sent = [
        lax.ppermute(
            lax.dynamic_index_in_dim(parts, at ^ turn, 0, keepdims=False).astype(BF16),
            AXES,
            turns[turn - 1],
        )
        for turn in range(1, size)
    ]
    return own, sent


def added(own, sent):
    for part in sent:
        own = own + part.astype(F32)
    return own


def gather_level(low, level):
    size, _, turns = level
    return jnp.stack([low] + [lax.ppermute(low, AXES, turns[turn - 1]) for turn in range(1, size)])


def from_first(blocks, level):
    size, at, _ = level
    return jnp.stack(
        [lax.dynamic_index_in_dim(blocks, at ^ n, 0, keepdims=False) for n in range(size)]
    )


def shards(
    embed_input,
    piece_image,
    embed_weight,
    embed_bias,
    embed_gain,
    embed_shift,
    first_gain,
    first_shift,
    query_weight,
    query_bias,
    reduce_weight,
    reduce_bias,
    reduce_gain,
    reduce_shift,
    key_weight,
    value_weight,
    value_bias,
    output_weight,
    output_bias,
    second_gain,
    second_shift,
    expand_weight,
    expand_bias,
    depth_weight,
    depth_bias,
    shrink_weight,
    shrink_bias,
    cotangent,
):
    source = embed_input[0].swapaxes(2, 3)
    slots, _, channels, wide_cols = source.shape
    cols = wide_cols // 2
    cells = REDUCE * cols
    keys = cols // REDUCE
    model = embed_weight.shape[3]
    hidden = expand_weight.shape[1]
    tiles = lax.axis_size("tile")
    tile_at = lax.axis_index("tile")
    pieces = tiles
    core_level, middle_level, high_level = device_levels()

    top = turned_by(embed_input[0, :, 2 * REDUCE - 1].swapaxes(1, 2), 1)
    meta = jnp.concatenate(
        [piece_image.reshape(-1), jnp.stack([tile_at, core_level[1], middle_level[1]]).astype(jnp.int32)]
    )
    vec = jnp.stack(
        [
            embed_bias, embed_gain, embed_shift, first_gain, first_shift, query_bias, reduce_bias,
            reduce_gain, reduce_shift, value_bias, output_bias, second_gain, second_shift,
            shrink_bias, shrink_bias, shrink_bias,
        ]
    ).astype(F32)
    hv = jnp.stack([expand_bias, depth_bias]).astype(F32)

    kw = dict(cols=cols)
    place = dict(slots=slots, tiles=tiles)
    flat_reduce = reduce_weight.reshape(-1, model)
    pairs, partial_sum = slot_call(
        partial(embed_own_body, **kw),
        slots,
        [(source, "far slot"), (embed_weight, "far whole")],
        [
            ((slots, 2 * REDUCE, 2 * channels, cols), BF16, "far slot"),
            ((slots, cells, 2 * model), F32, "slot"),
        ],
        [pltpu.VMEM((wide_cols, wide_cols), BF16)],
        name="embed_own",
        lasts=4,
        looped=True,
    )
    top_pairs, esum, stream, normed, blocks, reduced, kv = vmem_call(
        partial(embed_body, **kw, **place),
        [meta, partial_sum, top, embed_weight, vec, flat_reduce, key_weight, value_weight],
        [
            ((slots, 2 * channels, cols), BF16),
            ((slots, cells, model), F32),
            ((slots, cells, model), F32),
            ((slots, cells, model), BF16),
            ((slots * keys, REDUCE * REDUCE * model), BF16),
            ((slots * keys, model), F32),
            ((slots * keys, 2 * model), BF16),
        ],
        [pltpu.VMEM((slots * cells, model), F32)],
        name="embed",
    )

    grad_out = cotangent[0].reshape(slots, cells, model)
    all_cells = slots * cells
    gp, g_t = pl.pallas_call(
        partial(grouped_body, cols=cols, slots=slots),
        out_shape=[
            jax.ShapeDtypeStruct((all_cells, model), BF16),
            jax.ShapeDtypeStruct((model, all_cells), BF16),
        ],
        scratch_shapes=[pltpu.VMEM((all_cells, model), F32)],
        compiler_params=pltpu.CompilerParams(vmem_limit_bytes=VMEM_BYTES),
        cost_estimate=cost(3),
        name="grouped",
    )(grad_out)

    kv = kv.reshape(slots, keys, 2 * model)
    crossing = {n: crossed(kv, n) for n in range(tiles - 1, 0, -1)}
    kvs = [kv] + [crossing[n] for n in range(1, tiles)]
    kvs, gp, g_t = lax.optimization_barrier((kvs, gp, g_t))

    all_keys = keys * tiles
    part_cells = cells // 2

    def attend(rows, sources, results):
        return vmem_call(
            partial(attend_body, pieces=pieces, rows=rows, **kw, **place),
            [meta, normed, stream, vec, query_weight, output_weight] + sources,
            [
                ((slots, part_cells, model), BF16),
                ((slots, part_cells, HEADS * all_keys), BF16),
                ((slots, part_cells, model), BF16),
                ((slots, part_cells, model), F32),
            ]
            + results,
            [pltpu.VMEM((slots, part_cells, HEADS * all_keys), F32)],
            name="attend",
        )

    *kept_edge, first_row, last_row, kv_all = attend(
        EDGE_ROWS,
        kvs,
        [
            ((slots, cols, model), BF16),
            ((slots, cols, model), BF16),
            ((slots, all_keys, 2 * model), BF16),
        ],
    )
    row_up = turned_by(last_row, 1)
    row_down = turned_by(first_row, -1)
    *kept_inner, normed_inner = attend(
        INNER_ROWS, [kv_all], [((slots, part_cells, model), BF16)]
    )
    row_up, row_down, normed_inner = lax.optimization_barrier((row_up, row_down, normed_inner))
    width = 256
    vmem = pl.BlockSpec(memory_space=pltpu.VMEM)
    ext_cells = slots * (cells + 2 * cols)
    lane_tiles = width // 128
    hidden_blocks = (hidden // width,)
    by_lanes = lambda shape: pl.BlockSpec((shape[0], width), lambda b: (0, b))
    by_tiles = lambda shape: pl.BlockSpec((lane_tiles,) + tuple(shape[1:]), lambda b: (b, 0, 0))
    hidden_shape = (hidden // 128, ext_cells + 2 * GROUP * (REDUCE + 2), 128)
    conv_shape = (hidden // 128, all_cells + 2 * GROUP * REDUCE, 128)
    (
        gn_edge, gn_inner, gn_up, gn_down, d_expand, d_shrink, d_expand_bias, active, hidden_cells, grad_conv,
    ) = pl.pallas_call(
        partial(feed_body, width=width, **kw, **place),
        in_specs=[smem()] + [vmem] * 11,
        out_specs=[vmem] * 7 + [pl.BlockSpec(memory_space=pltpu.HBM)] * 3,
        out_shape=[
            jax.ShapeDtypeStruct((slots, part_cells, model), F32),
            jax.ShapeDtypeStruct((slots, part_cells, model), F32),
            jax.ShapeDtypeStruct((slots, cols, model), BF16),
            jax.ShapeDtypeStruct((slots, cols, model), BF16),
            jax.ShapeDtypeStruct((model, hidden), F32),
            jax.ShapeDtypeStruct((hidden, model), F32),
            jax.ShapeDtypeStruct((8, hidden), F32),
            far((all_cells, hidden), BF16),
            far(hidden_shape, BF16),
            far(conv_shape, BF16),
        ],
        scratch_shapes=[pltpu.VMEM((all_cells, width), BF16)] * 2
        + [pltpu.VMEM((lane_tiles,) + hidden_shape[1:], BF16)] * 2
        + [pltpu.VMEM((lane_tiles,) + conv_shape[1:], BF16)] * 2
        + [
            pltpu.VMEM((ext_cells, width), BF16),
            pltpu.VMEM((all_cells, width), F32),
            pltpu.VMEM((ext_cells, model), F32),
            pltpu.VMEM((ext_cells, model), BF16),
            pltpu.VMEM((model + GROUP, ext_cells), BF16),
            pltpu.SemaphoreType.DMA((3, 2)),
        ],
        compiler_params=pltpu.CompilerParams(vmem_limit_bytes=VMEM_BYTES),
        cost_estimate=cost(18),
        name="feed_forward",
    )(
        meta, first_row, normed_inner, last_row, row_up, row_down, gp, g_t, hv, depth_weight,
        expand_weight, shrink_weight,
    )

    from_up = turned_by(gn_down, 1)
    from_down = turned_by(gn_up, -1)
    pairs_of_tiles = tiles // 2

    def attend_back(rows, grad, kept, sources, results):
        queries, probs, attended, stream_two = kept
        return vmem_call(
            partial(attend_back_body, pairs=pairs_of_tiles, rows=rows, slots=slots, **kw),
            [
                grad, stream_two, grad_out, attended, probs, queries, normed, vec, output_weight,
                kv_all,
            ]
            + sources,
            [
                ((slots, part_cells, model), F32),
                ((slots, part_cells, model), BF16),
                ((model, model), F32),
                ((model, model), F32),
                ((VECTORS, model), F32),
            ]
            + results,
            [
                pltpu.VMEM((slots, part_cells, HEADS * all_keys), F32),
                pltpu.VMEM((slots, part_cells, HEADS * all_keys), BF16),
                pltpu.VMEM((slots * part_cells, model), BF16),
                pltpu.VMEM((slots * part_cells, model), BF16),
            ],
            name="attend_back",
        )

    gst_inner, gq_inner, *sums, dkv_inner = attend_back(
        INNER_ROWS, gn_inner, kept_inner, [], [((slots, all_keys, 2 * model), F32)]
    )
    from_up, from_down, dkv_inner = lax.optimization_barrier((from_up, from_down, dkv_inner))
    gst_edge, gq_edge, d_output, d_query, dvec_a, *dkvs = attend_back(
        EDGE_ROWS,
        gn_edge,
        kept_edge,
        [from_up, from_down, dkv_inner] + sums,
        [((slots, 2 * keys, 2 * model), BF16)] * pairs_of_tiles,
    )
    crossing = {n: crossed(dkvs[n], 2 * n) for n in range(pairs_of_tiles - 1, 0, -1)}
    own_dkvs = [dkvs[0]] + [crossing[n] for n in range(1, pairs_of_tiles)]
    d_hv = pl.pallas_call(
        partial(depth_weight_body, span=cols * slots // GROUP),
        grid=hidden_blocks,
        in_specs=[by_tiles(hidden_shape), by_tiles(conv_shape), by_lanes((8, hidden))],
        out_specs=by_lanes((HIDDEN_VECTORS, hidden)),
        out_shape=jax.ShapeDtypeStruct((HIDDEN_VECTORS, hidden), F32),
        compiler_params=params(),
        cost_estimate=cost(6),
        name="depth_weights",
    )(from_far(hidden_cells), from_far(grad_conv), d_expand_bias)
    own_dkvs, d_hv = lax.optimization_barrier((own_dkvs, d_hv))
    for_mate = own_dkvs[0][:, keys:].astype(F32)
    for part in own_dkvs[1:]:
        for_mate = for_mate + part[:, keys:].astype(F32)
    own_dkvs.append(crossed(for_mate.astype(BF16), 1))

    gnb, dvec_b, keep, send = pl.pallas_call(
        partial(reduce_back_body, parts=len(own_dkvs), **place),
        in_specs=[vmem] * len(own_dkvs) + [smem()] + [vmem] * 12,
        out_specs=[vmem] * 4,
        out_shape=[
            jax.ShapeDtypeStruct((slots * keys, REDUCE * REDUCE * model), F32),
            jax.ShapeDtypeStruct((VECTORS, model), F32),
            jax.ShapeDtypeStruct((EARLY_ROWS, 128), F32),
            jax.ShapeDtypeStruct((EARLY_ROWS, 128), BF16),
        ],
        compiler_params=pltpu.CompilerParams(vmem_limit_bytes=VMEM_BYTES),
        cost_estimate=cost(3),
        name="reduce_back",
    )(
        *own_dkvs, meta, reduced, blocks, vec, flat_reduce, key_weight, value_weight,
        d_expand, d_shrink, d_hv, d_output, d_query, dvec_a,
    )
    got = lax.ppermute(send, AXES, core_level[2][0])

    ge, ge_first, dvec_c = vmem_call(
        partial(embed_back_body, **kw, **place),
        [
            meta, gnb, gq_edge, gq_inner, gst_edge, gst_inner, esum, vec, query_weight, dvec_b,
        ],
        [
            ((slots, cells, 2 * model), BF16),
            ((slots, cols, model), BF16),
            ((VECTORS, model), F32),
        ],
        [pltpu.VMEM((slots * cells, model), F32)],
        name="embed_back",
    )
    below = turned_by(ge_first, -1)
    late_keep, late_send = pl.pallas_call(
        partial(embed_weight_body, half=channels, **place),
        in_specs=[smem()] + [vmem] * 4,
        out_specs=[vmem] * 2,
        out_shape=[
            jax.ShapeDtypeStruct((LATE_ROWS, 128), F32),
            jax.ShapeDtypeStruct((LATE_ROWS, 128), BF16),
        ],
        compiler_params=pltpu.CompilerParams(vmem_limit_bytes=VMEM_BYTES),
        cost_estimate=cost(3),
        name="embed_weights",
    )(meta, ge, pairs, top_pairs, dvec_c)
    late_got = lax.ppermute(late_send, AXES, core_level[2][0])

    middle, high = middle_level[0], high_level[0]
    parts = jnp.concatenate(
        [
            (keep + got.astype(F32)).reshape(middle, -1, 128),
            (late_keep + late_got.astype(F32)).reshape(middle, -1, 128),
        ],
        axis=1,
    )
    (grad_input,) = slot_call(
        partial(input_back_body, half=channels, **kw),
        slots,
        [(ge, "slot"), (embed_weight, "whole")],
        [(source.shape, F32, "slot")],
        [pltpu.VMEM((wide_cols, wide_cols), BF16)],
        name="input_back",
    )
    own, sent = scatter_level(parts, middle_level)
    sent, grad_input = lax.optimization_barrier((sent, grad_input))
    own = added(own, sent)
    own, sent = scatter_level(own.reshape(high, -1, 128), high_level)
    last_line = pl.BlockSpec((1, 1, channels, wide_cols), lambda s: (s, 2 * REDUCE - 1, 0, 0))
    grad_input = pl.pallas_call(
        partial(last_row_body, half=channels, **kw, **place),
        grid=(slots,),
        in_specs=[
            smem(),
            pl.BlockSpec((1, cols, 2 * model), lambda s: (s, REDUCE - 1, 0)),
            per_slot(below.shape),
            whole(embed_weight.shape),
            pl.BlockSpec(memory_space=pl.ANY),
        ],
        out_specs=last_line,
        out_shape=jax.ShapeDtypeStruct(source.shape, F32),
        scratch_shapes=[pltpu.VMEM((wide_cols, wide_cols), BF16)],
        input_output_aliases={4: 0},
        compiler_params=params(),
        cost_estimate=cost(2),
        name="last_row",
    )(meta, ge, below, embed_weight, grad_input)
    sent, grad_input = lax.optimization_barrier((sent, grad_input))
    low = added(own, sent).astype(BF16)
    low = from_first(gather_level(low, high_level), high_level).reshape(-1, 128)
    out = pl.pallas_call(
        partial(output_body, cols=cols, slots=slots),
        out_shape=jax.ShapeDtypeStruct((slots, cells, model), BF16),
        scratch_shapes=[pltpu.VMEM((all_cells, model), F32)],
        compiler_params=pltpu.CompilerParams(vmem_limit_bytes=VMEM_BYTES),
        cost_estimate=cost(3),
        name="output",
    )(active, kept_edge[3], kept_inner[3], vec, shrink_weight)
    gathered = gather_level(low, middle_level)
    gathered, out = lax.optimization_barrier((gathered, out))
    low = gathered.reshape(-1, 128)
    other = lax.ppermute(low, AXES, core_level[2][0])

    shapes = [(9 * channels, model), (REDUCE * REDUCE * model, model)]
    shapes += [(model, model)] * 4 + [(model, hidden), (hidden, model)]
    shapes += [(model,)] * 14 + [(hidden,), (3, 3, hidden), (hidden,)]
    results = pl.pallas_call(
        partial(unpack_body, half=channels, middle=middle, **place),
        in_specs=[smem()] + [vmem] * 2,
        out_specs=[vmem] * len(shapes),
        out_shape=[jax.ShapeDtypeStruct(shape, F32) for shape in shapes],
        compiler_params=pltpu.CompilerParams(vmem_limit_bytes=VMEM_BYTES),
        cost_estimate=cost(3),
        name="unpack",
    )(meta, low, other)
    (s_embed, s_reduce, s_query, s_key, s_value, s_output, s_expand, s_shrink) = results[:8]
    vectors = results[8:22]
    s_expand_bias, s_depth, s_depth_bias = results[22:]
    return (
        out.reshape(cotangent.shape),
        grad_input.swapaxes(2, 3)[None],
        s_embed.reshape(embed_weight.shape),
        vectors[EMBED_BIAS],
        vectors[EMBED_GAIN],
        vectors[EMBED_SHIFT],
        vectors[FIRST_GAIN],
        vectors[FIRST_SHIFT],
        s_query,
        vectors[QUERY_BIAS],
        s_reduce.reshape(reduce_weight.shape),
        vectors[REDUCE_BIAS],
        vectors[REDUCE_GAIN],
        vectors[REDUCE_SHIFT],
        s_key,
        s_value,
        vectors[VALUE_BIAS],
        s_output,
        vectors[OUTPUT_BIAS],
        vectors[SECOND_GAIN],
        vectors[SECOND_SHIFT],
        s_expand,
        s_expand_bias,
        s_depth,
        s_depth_bias,
        s_shrink,
        vectors[SHRINK_BIAS],
    )


def solution(mesh):
    shard_rows = P("batch", None, "tile", None, None)
    in_specs = (shard_rows, P("batch", None, None, None)) + (P(),) * 25 + (shard_rows,)
    out_specs = (shard_rows, shard_rows) + (P(),) * 25
    return jax.shard_map(shards, mesh=mesh, in_specs=in_specs, out_specs=out_specs, check_vma=False)
```

```python
import math
from functools import partial

import jax
import jax.numpy as jnp
from jax import lax
from jax.experimental import pallas as pl
from jax.experimental.pallas import tpu as pltpu
from jax.sharding import PartitionSpec as P

HEADS = 2
REDUCE = 4
F32 = jnp.float32
BF16 = jnp.bfloat16
HIGHEST = lax.Precision.HIGHEST
LOG2E = math.log2(math.e)
VMEM_BYTES = 32 * 1024 * 1024

(
    EMBED_BIAS,
    EMBED_GAIN,
    EMBED_SHIFT,
    FIRST_GAIN,
    FIRST_SHIFT,
    QUERY_BIAS,
    REDUCE_BIAS,
    REDUCE_GAIN,
    REDUCE_SHIFT,
    VALUE_BIAS,
    OUTPUT_BIAS,
    SECOND_GAIN,
    SECOND_SHIFT,
    SHRINK_BIAS,
) = range(14)
VECTORS = 16
HIDDEN_VECTORS = 16


def nn(left, right, precision=None):
    return lax.dot_general(
        left, right, (((1,), (0,)), ((), ())), precision=precision, preferred_element_type=F32
    )


def nt(left, right, precision=None):
    return lax.dot_general(
        left, right, (((1,), (1,)), ((), ())), precision=precision, preferred_element_type=F32
    )


def tn(left, right, precision=None):
    return lax.dot_general(
        left, right, (((0,), (0,)), ((), ())), precision=precision, preferred_element_type=F32
    )


def norm_stats(values, epsilon):
    centered = values - jnp.mean(values, axis=-1, keepdims=True)
    scale = lax.rsqrt(jnp.mean(centered * centered, axis=-1, keepdims=True) + epsilon)
    return centered * scale, scale


def norm_back(grad, hat, scale, gain):
    grad_hat = grad * gain
    mean_grad = jnp.mean(grad_hat, axis=-1, keepdims=True)
    mean_dot = jnp.mean(grad_hat * hat, axis=-1, keepdims=True)
    return scale * (grad_hat - mean_grad - hat * mean_dot)


def row_sum(values):
    return jnp.sum(values, axis=0, keepdims=True)


def params(vmem=VMEM_BYTES, axes=1):
    return pltpu.CompilerParams(
        vmem_limit_bytes=vmem, dimension_semantics=("arbitrary",) * axes
    )


def whole(shape, slots=None):
    rank = len(shape)
    return pl.BlockSpec(tuple(shape), lambda *_: (0,) * rank)


def per_slot(shape, slots=None):
    rank = len(shape)
    return pl.BlockSpec((1,) + tuple(shape[1:]), lambda s: (s,) + (0,) * (rank - 1))


def per_slot_rows(shape, slots):
    return pl.BlockSpec((shape[0] // slots, shape[1]), lambda s: (s, 0))


def smem():
    return pl.BlockSpec(memory_space=pltpu.SMEM)


def far(shape, dtype):
    return pltpu.HBM(tuple(shape), dtype)


def from_far(array):
    return pltpu.with_memory_space_constraint(array, pltpu.HBM)


def cost(microseconds):
    return pl.CostEstimate(
        flops=int(microseconds * 1.0e9), bytes_accessed=int(microseconds * 3.0e6), transcendentals=0
    )


def slot_call(body, slots, inputs, outputs, scratch=(), name=None, lasts=5, looped=False):
    kinds = {"slot": per_slot, "whole": whole, "keys": per_slot_rows}
    arrays = [(a.shape, a.dtype, k) for a, k in inputs] + list(outputs)
    names = [k.removeprefix("far ") for *_, k in arrays]
    are_far = [k.startswith("far ") for *_, k in arrays]
    count_in = len(inputs)
    moved = [n for n, is_far in enumerate(are_far) if is_far and looped]

    def spec(shape, kind, is_far):
        if kind == "smem":
            return smem()
        if looped:
            return pl.BlockSpec(memory_space=pltpu.HBM if is_far else pltpu.VMEM)
        return kinds[kind](shape, slots)

    def grid_body(*refs):
        body(pl.program_id(0), *refs)

    def loop_body(*refs):
        refs = list(refs)
        extra = refs[len(names) :]
        if moved:
            sems, extra = extra[-1], extra[:-1]
            buffers, extra = extra[len(extra) - len(moved) :], extra[: len(extra) - len(moved)]

        def copy(m, s):
            n = moved[m]
            here, there = buffers[m], refs[n]
            if names[n] == "slot":
                here, there = here.at[pl.ds(s, 1)], there.at[pl.ds(s, 1)]
            source, target = (there, here) if n < count_in else (here, there)
            return pltpu.make_async_copy(source, target, sems.at[m, s])

        into = [m for m, n in enumerate(moved) if n < count_in]
        out_of = [m for m, n in enumerate(moved) if n >= count_in]
        whole_in = [m for m in into if names[moved[m]] == "whole"]
        slot_in = [m for m in into if names[moved[m]] == "slot"]
        slot_out = [m for m in out_of if names[moved[m]] == "slot"]
        whole_out = [m for m in out_of if names[moved[m]] == "whole"]
        for m in slot_in:
            copy(m, 0).start()
        for m in whole_in:
            copy(m, 0).start()
        for s in range(1, slots):
            for m in slot_in:
                copy(m, s).start()
        local = list(refs[: len(names)])
        for m, n in enumerate(moved):
            local[n] = buffers[m]
        for m in whole_in:
            copy(m, 0).wait()

        def step(s, carry):
            views = []
            for ref, kind, (shape, *_) in zip(local, names, arrays):
                if kind == "slot":
                    ref = ref.at[pl.ds(s, 1)]
                elif kind == "keys":
                    count = shape[0] // slots
                    ref = ref.at[pl.ds(pl.multiple_of(s * count, count), count)]
                views.append(ref)
            for m in slot_in:
                copy(m, s).wait()
            body(s, *views, *extra)
            for m in slot_out:
                copy(m, s).start()
            return carry

        lax.fori_loop(0, slots, step, 0)
        for m in whole_out:
            copy(m, 0).start()
        for s in range(slots):
            for m in slot_out:
                copy(m, s).wait()
        for m in whole_out:
            copy(m, 0).wait()

    specs = [spec(shape, kind, f) for (shape, *_), kind, f in zip(arrays, names, are_far)]
    scratch = list(scratch)
    if moved:
        scratch += [pltpu.VMEM(arrays[n][0], arrays[n][1]) for n in moved]
        scratch += [pltpu.SemaphoreType.DMA((len(moved), slots))]
    return pl.pallas_call(
        loop_body if looped else grid_body,
        grid=() if looped else (slots,),
        in_specs=specs[:count_in],
        out_specs=specs[count_in:],
        out_shape=[
            (far if k.startswith("far ") else jax.ShapeDtypeStruct)(s, d) for s, d, k in outputs
        ],
        scratch_shapes=scratch,
        compiler_params=pltpu.CompilerParams(vmem_limit_bytes=VMEM_BYTES) if looped else params(),
        cost_estimate=cost(lasts),
        name=name,
    )(*[from_far(a) if k.startswith("far ") else a for a, k in inputs])


def vmem_call(body, inputs, outputs, scratch=(), name=None, lasts=5):
    vmem = pl.BlockSpec(memory_space=pltpu.VMEM)
    return pl.pallas_call(
        body,
        in_specs=[smem() if a.dtype == jnp.int32 else vmem for a in inputs],
        out_specs=[vmem] * len(outputs),
        out_shape=[jax.ShapeDtypeStruct(shape, dtype) for shape, dtype in outputs],
        scratch_shapes=list(scratch),
        compiler_params=pltpu.CompilerParams(vmem_limit_bytes=VMEM_BYTES),
        cost_estimate=cost(lasts),
        name=name,
    )(*inputs)


def flat_rows(ref):
    return ref[...].reshape(-1, ref.shape[-1])


def by_slot(values, slots):
    count = values.shape[0] // slots
    return [values[s * count : (s + 1) * count] for s in range(slots)]


def tile_ids(meta, s, tile, tiles):
    at = (s * tiles + tile) * 2
    return meta[at], meta[at + 1]


def tile_place(meta, slots, tiles):
    return meta[slots * tiles * 2]


def core_place(meta, slots, tiles):
    return meta[slots * tiles * 2 + 1]


def middle_place(meta, slots, tiles):
    return meta[slots * tiles * 2 + 2]


def as_flag(condition):
    return jnp.where(condition, 1.0, 0.0).astype(F32)


def same_flags(meta, s, slots, tiles):
    at = tile_place(meta, slots, tiles)
    own = tile_ids(meta, s, at, tiles)
    up = tile_ids(meta, s, jnp.maximum(at - 1, 0), tiles)
    down = tile_ids(meta, s, jnp.minimum(at + 1, tiles - 1), tiles)
    return (
        as_flag(own[0] == own[1]),
        as_flag((own[0] == up[0]) & (at > 0)),
        as_flag((own[0] == down[0]) & (at < tiles - 1)),
    )


def split_columns(size):
    source = lax.broadcasted_iota(jnp.int32, (size, size), 0)
    target = lax.broadcasted_iota(jnp.int32, (size, size), 1)
    wanted = jnp.where(target < size // 2, 2 * target, 2 * target - size + 1)
    return jnp.where(source == wanted, 1.0, 0.0).astype(BF16)


def embed_weights(ew):
    half = ew.shape[2]
    none = jnp.zeros_like(ew[0, 0])
    weights = []
    for a in range(3):
        main = ew[a, 1:3].reshape(2 * half, 128)
        side = jnp.concatenate([none, ew[a, 0]], axis=0)
        weights.append(jnp.concatenate([main, side], axis=1))
    return jnp.concatenate(weights, axis=0)


def embed_own_body(s, meta, x, ew, pairs, partial_sum, split, zbuf, *, cols, slots, tiles):
    half = x.shape[2]

    @pl.when(s == 0)
    def _():
        split[...] = split_columns(2 * cols)

    own = nn(x[0].reshape(2 * REDUCE * half, 2 * cols), split[...])
    for r in range(2 * REDUCE):
        row = own[r * half : (r + 1) * half].astype(BF16)
        pairs[0, r, :half] = row[:, :cols]
        pairs[0, r, half:] = row[:, cols:]
    weights = embed_weights(ew)
    for i in range(REDUCE):
        first = max(2 * i - 1, 0)
        lines = pairs[0, first : 2 * i + 2]
        lines = lines.reshape(lines.shape[0] * 128, cols)
        zbuf[i * cols : (i + 1) * cols] = tn(lines, weights[-lines.shape[0] :])
    mask = side_mask(meta, s, slots, tiles, cols, REDUCE, True)
    partial_sum[0] = zbuf[:, :128] + pltpu.roll(zbuf[:, 128:], 1, 0) * mask


def side_mask(meta, s, slots, tiles, cols, rows, forward):
    column = lax.broadcasted_iota(jnp.int32, (rows * cols, 1), 0) % cols
    outside = 0 if forward else cols - 1
    border = cols // 2 if forward else cols // 2 - 1
    same_sides, _, _ = same_flags(meta, s, slots, tiles)
    return jnp.where(column == outside, 0.0, jnp.where(column == border, same_sides, 1.0))


def embed_body(
    meta, partial_sum, top, ew, vec, rw, kw, vw,
    top_pairs, esum, stream, normed, blocks, reduced, kv,
    nbuf, *, cols, slots, tiles,
):
    keys = cols // REDUCE
    cells = REDUCE * cols
    half = top.shape[1]
    above = by_slot(nn(flat_rows(top), split_columns(2 * cols)), slots)
    weights = embed_weights(ew)[:128]
    lines = []
    for s in range(slots):
        _, same_up, _ = same_flags(meta, s, slots, tiles)
        row = (above[s] * same_up).astype(BF16)
        top_pairs[s, :half] = row[:, :cols]
        top_pairs[s, half:] = row[:, cols:]
        z = tn(top_pairs[s], weights)
        mask = side_mask(meta, s, slots, tiles, cols, 1, True)
        first = partial_sum[s, :cols] + z[:, :128] + pltpu.roll(z[:, 128:], 1, 0) * mask
        lines += [first, partial_sum[s, cols:]]
    value = jnp.concatenate(lines, axis=0) + vec[EMBED_BIAS : EMBED_BIAS + 1]
    esum[...] = value.reshape(esum.shape)
    hat, _ = norm_stats(value, 1e-05)
    st = hat * vec[EMBED_GAIN : EMBED_GAIN + 1] + vec[EMBED_SHIFT : EMBED_SHIFT + 1]
    stream[...] = st.reshape(stream.shape)
    hat, _ = norm_stats(st, 1e-06)
    nm = hat * vec[FIRST_GAIN : FIRST_GAIN + 1] + vec[FIRST_SHIFT : FIRST_SHIFT + 1]
    low = nm.astype(BF16)
    normed[...] = low.reshape(normed.shape)
    nbuf[...] = low.astype(F32)
    for s in range(slots):
        for a in range(REDUCE):
            for b in range(REDUCE):
                at = (a * REDUCE + b) * 128
                piece = nbuf[pl.ds(s * cells + a * cols + b, keys, REDUCE), :]
                blocks[s * keys : (s + 1) * keys, at : at + 128] = piece.astype(BF16)
    value = nn(blocks[...], rw[...]) + vec[REDUCE_BIAS : REDUCE_BIAS + 1]
    reduced[...] = value
    hat, _ = norm_stats(value, 1e-06)
    rn = (hat * vec[REDUCE_GAIN : REDUCE_GAIN + 1] + vec[REDUCE_SHIFT : REDUCE_SHIFT + 1]).astype(BF16)
    kv[:, :128] = nn(rn, kw[...]).astype(BF16)
    kv[:, 128:] = (nn(rn, vw[...]) + vec[VALUE_BIAS : VALUE_BIAS + 1]).astype(BF16)


def both_heads(kv, s, at):
    rows = kv[s, :, at : at + 128]
    lane = lax.broadcasted_iota(jnp.int32, rows.shape, 1)
    zero = jnp.zeros_like(rows)
    return jnp.concatenate(
        [jnp.where(lane < 64, rows, zero), jnp.where(lane < 64, zero, rows)], axis=0
    )


def key_bias(meta, s, slots, tiles, keys):
    at = tile_place(meta, slots, tiles)
    own = tile_ids(meta, s, at, tiles)
    part = keys // (2 * tiles)
    entry = lax.broadcasted_iota(jnp.int32, (1, keys), 1) // part
    rows = [jnp.zeros((1, keys), F32) for _ in range(2)]
    for n in range(tiles):
        ids = tile_ids(meta, s, at ^ n, tiles)
        for side in range(2):
            for query in range(2):
                value = jnp.where(ids[side] == own[query], 0.0, -1e30).astype(F32)
                rows[query] = jnp.where(entry == 2 * n + side, value, rows[query])
    return rows


EDGE_ROWS = (0, REDUCE - 1)
INNER_ROWS = tuple(range(1, REDUCE - 1))


def pick_rows(ref, rows, cols):
    lines = [ref[s, i * cols : (i + 1) * cols] for s in range(ref.shape[0]) for i in rows]
    return jnp.concatenate(lines, axis=0)


def attend_body(*refs, pieces, cols, slots, tiles, rows):
    edge = rows == EDGE_ROWS
    (meta, normed, stream, vec, qw, ow), refs = refs[:6], refs[6:]
    if edge:
        kvs, refs = refs[:pieces], refs[pieces:]
        queries, probs, attended, stream_two, first_row, last_row, kv_all, sbuf = refs
        for s in range(slots):
            kv_all[s] = jnp.concatenate([p[s] for p in kvs], axis=0)
    else:
        kv_all, queries, probs, attended, stream_two, normed_two, sbuf = refs
    q = nn(pick_rows(normed, rows, cols), qw[...]) + vec[QUERY_BIAS : QUERY_BIAS + 1]
    queries[...] = q.astype(BF16).reshape(queries.shape)
    for s in range(slots):
        sbuf[s] = nt(queries[s], both_heads(kv_all, s, 0))
    keys = sbuf.shape[2] // HEADS
    factor = LOG2E * (128 // HEADS) ** (-0.5)
    column = lax.broadcasted_iota(jnp.int32, (len(rows) * cols, 1), 0) % cols
    for s in range(slots):
        left, right = key_bias(meta, s, slots, tiles, keys)
        bias = jnp.where(column < cols // 2, left, right)
        for h in range(HEADS):
            span = slice(h * keys, (h + 1) * keys)
            score = sbuf[s, :, span] * factor + bias
            e = jnp.exp2(score - jnp.max(score, axis=-1, keepdims=True))
            p = e * (1.0 / jnp.sum(e, axis=-1, keepdims=True))
            probs[s, :, span] = p.astype(BF16)
    for s in range(slots):
        attended[s] = nn(probs[s], both_heads(kv_all, s, 128)).astype(BF16)
    value = pick_rows(stream, rows, cols) + nn(flat_rows(attended), ow[...])
    value = value + vec[OUTPUT_BIAS : OUTPUT_BIAS + 1]
    stream_two[...] = value.reshape(stream_two.shape)
    hat, _ = norm_stats(value, 1e-06)
    low = (hat * vec[SECOND_GAIN : SECOND_GAIN + 1] + vec[SECOND_SHIFT : SECOND_SHIFT + 1]).astype(BF16)
    if edge:
        for s, part in enumerate(by_slot(low, slots)):
            first_row[s] = part[:cols]
            last_row[s] = part[cols:]
    else:
        normed_two[...] = low.reshape(normed_two.shape)


DENSITY = 1.0 / math.sqrt(2.0 * math.pi)


def gelu_pair(x):
    twice_cdf = 1.0 + lax.erf(x * math.sqrt(0.5))
    e = jnp.exp2((x * x) * (-0.5 * LOG2E))
    return x * twice_cdf, twice_cdf + x * (e * (2.0 * DENSITY))


GROUP = 16


def fold_rows(values):
    return values[: GROUP // 2] + values[GROUP // 2 :]


def group(n):
    return slice(n * GROUP, (n + 1) * GROUP)


def group_places(r, s, q, cols, slots):
    spans = GROUP // slots
    span = cols // spans
    return pl.ds(r * span * GROUP + s * spans + q, span, GROUP)


def grouped_body(g, gp, g_t, buf, *, cols, slots):
    spans = GROUP // slots
    span = cols // spans
    line = span * GROUP
    for s in range(slots):
        for q in range(spans):
            for r in range(REDUCE):
                row = g[s, r * cols + q * span : r * cols + (q + 1) * span]
                buf[group_places(r, s, q, cols, slots), :] = row.astype(F32)
    for r in range(REDUCE):
        rows = slice(r * line, (r + 1) * line)
        gp[rows] = buf[rows].astype(BF16)
        g_t[:, rows] = gp[rows].T


def feed_body(
    meta, nt_first, nt_inner, nt_last, nt_up, nt_down, gp, g_t, hv, dw, ew, sw,
    gn_edge, gn_inner, gn_up, gn_down, dew, dsw, deb, a_out, h_out, c_out,
    abuf0, abuf1, hbuf0, hbuf1, cbuf0, cbuf1, ghbuf, gabuf, gnacc, ext, ext_t, sems,
    *, cols, slots, tiles, width,
):
    abufs, hbufs, cbufs = (abuf0, abuf1), (hbuf0, hbuf1), (cbuf0, cbuf1)
    model = ew.shape[0]
    blocks = ew.shape[1] // width
    spans = GROUP // slots
    span = cols // spans
    line = span * GROUP
    padded = line + 2 * GROUP
    rows_in = REDUCE + 2
    lane_tiles = width // 128

    def copies(b, side):
        lanes = pl.ds(pl.multiple_of(b * width, width), width)
        tiles_at = pl.ds(b * lane_tiles, lane_tiles)
        pairs = (
            (abufs, a_out.at[:, lanes]), (hbufs, h_out.at[tiles_at]), (cbufs, c_out.at[tiles_at]),
        )
        return [
            pltpu.make_async_copy(bufs[side], there, sems.at[n, side])
            for n, (bufs, there) in enumerate(pairs)
        ]

    sub = lax.broadcasted_iota(jnp.int32, (GROUP, 1), 0)
    at_slot, at_span = sub // spans, sub % spans
    same = [jnp.zeros((GROUP, 1), F32) for _ in range(3)]
    for s in range(slots):
        flags = same_flags(meta, s, slots, tiles)
        same = [jnp.where(at_slot == s, flag, mask) for flag, mask in zip(flags, same)]
    sides, same_up, same_down = same
    from_left = jnp.where(at_span == 0, 0.0, jnp.where(at_span == spans // 2, sides, 1.0))
    from_right = jnp.where(
        at_span == spans - 1, 0.0, jnp.where(at_span == spans // 2 - 1, sides, 1.0)
    )
    low_up = jnp.broadcast_to(same_up, (GROUP, 128)).astype(BF16)
    low_down = jnp.broadcast_to(same_down, (GROUP, 128)).astype(BF16)

    for s in range(slots):
        for q in range(spans):
            for r in range(rows_in):
                if 2 <= r < rows_in - 2:
                    at = (r - 2) * cols + q * span
                    row = nt_inner[s, at : at + span]
                else:
                    lines = {0: nt_up, 1: nt_first, rows_in - 2: nt_last, rows_in - 1: nt_down}
                    row = lines[r][s, q * span : (q + 1) * span]
                gnacc[group_places(r, s, q, cols, slots), :] = row.astype(F32)
    for r in range(rows_in):
        rows = slice(r * line, (r + 1) * line)
        ext[rows] = gnacc[rows].astype(BF16)
        ext_t[:model, rows] = ext[rows].T
    ext_t[model:] = jnp.ones_like(ext_t[model:])
    gnacc[...] = jnp.zeros_like(gnacc)

    def ghosts(buf, rows):
        for t in range(lane_tiles):
            for r in range(rows):
                base = r * padded
                first = buf[t, base + GROUP : base + 2 * GROUP].astype(F32)
                last = buf[t, base + line : base + line + GROUP].astype(F32)
                left = pltpu.roll(last, 1, 0) * from_left
                right = pltpu.roll(first, GROUP - 1, 0) * from_right
                buf[t, base : base + GROUP] = left.astype(BF16)
                buf[t, base + line + GROUP : base + padded] = right.astype(BF16)

    def taps_of(lanes):
        return [
            [jnp.broadcast_to(dw[a, c : c + 1, lanes], (GROUP, 128)) for c in range(3)]
            for a in range(3)
        ]

    def block(b, side):
        abuf, hbuf, cbuf = abufs[side], hbufs[side], cbufs[side]
        to_a, to_h, to_c = copies(b, side)
        at = pl.multiple_of(b * width, width)
        ewb = ew[:, pl.ds(at, width)]
        half_sw = sw[pl.ds(at, width), :] * 0.5
        bias = hv[0:1, pl.ds(at, width)]
        for r in range(rows_in):
            hid = nn(ext[r * line : (r + 1) * line], ewb) + bias
            if r == 0 or r == rows_in - 1:
                mask = same_up if r == 0 else same_down
                hid = (hid.reshape(span, GROUP, width) * mask[None]).reshape(line, width)
            for t in range(lane_tiles):
                base = r * padded + GROUP
                hbuf[t, base : base + line] = hid[:, t * 128 : (t + 1) * 128].astype(BF16)
        ghosts(hbuf, rows_in)
        to_h.start()
        for r in range(REDUCE):
            rows = slice(r * line, (r + 1) * line)
            gabuf[rows] = nt(gp[rows], half_sw)
        for t in range(lane_tiles):
            lanes = slice(t * 128, (t + 1) * 128)
            spot = pl.ds(pl.multiple_of(at + t * 128, 128), 128)
            taps = taps_of(spot)
            depth_bias = hv[1:2, spot]
            for col in range(span):
                h = [
                    [hbuf[t, group(r * (span + 2) + col + d)] for d in range(3)]
                    for r in range(rows_in)
                ]
                for i in range(REDUCE):
                    conv = None
                    for a in range(3):
                        for c in range(3):
                            term = h[i + a][c] * taps[a][c]
                            conv = term if conv is None else conv + term
                    act, slope = gelu_pair(conv.astype(F32) + depth_bias)
                    rows = group(i * span + col)
                    abuf[rows, lanes] = act.astype(BF16)
                    grad = gabuf[rows, lanes] * slope
                    cbuf[t, group(i * (span + 2) + col + 1)] = grad.astype(BF16)
        to_a.start()
        ghosts(cbuf, REDUCE)
        to_c.start()
        for t in range(lane_tiles):
            lanes = slice(t * 128, (t + 1) * 128)
            taps = taps_of(pl.ds(pl.multiple_of(at + t * 128, 128), 128))
            for col in range(span):
                gc = [
                    [cbuf[t, group(i * (span + 2) + col + d)] for d in range(3)]
                    for i in range(REDUCE)
                ]
                for r in range(rows_in):
                    gh = None
                    for a in range(3):
                        if not 0 <= r - a < REDUCE:
                            continue
                        for c in range(3):
                            term = gc[r - a][2 - c] * taps[a][c]
                            gh = term if gh is None else gh + term
                    if r == 0:
                        gh = gh * low_up
                    if r == rows_in - 1:
                        gh = gh * low_down
                    ghbuf[group(r * span + col), lanes] = gh
        for r in range(rows_in):
            rows = slice(r * line, (r + 1) * line)
            gnacc[rows] += nt(ghbuf[rows], ewb)
        grad = nn(ext_t[...], ghbuf[...])
        dew[:, pl.ds(at, width)] = grad[:model]
        deb[:, pl.ds(at, width)] = grad[model : model + 8]
        dsw[pl.ds(at, width), :] = nn(g_t[...], abuf[...]).T * 0.5

    def two_blocks(k, carry):
        for side in range(2):
            b = 2 * k + side

            @pl.when(k > 0)
            def _():
                for copy in copies(b - 2, side):
                    copy.wait()

            block(b, side)
        return carry

    lax.fori_loop(0, blocks // 2, two_blocks, 0)
    for s in range(slots):
        for q in range(spans):
            there = slice(q * span, (q + 1) * span)
            for r in range(rows_in):
                grad = gnacc[group_places(r, s, q, cols, slots), :]
                if r == 0:
                    gn_up[s, there] = grad.astype(BF16)
                elif r == rows_in - 1:
                    gn_down[s, there] = grad.astype(BF16)
                elif r in (1, rows_in - 2):
                    at = (0 if r == 1 else cols) + q * span
                    gn_edge[s, at : at + span] = grad
                else:
                    at = (r - 2) * cols + q * span
                    gn_inner[s, at : at + span] = grad
    for side in range(2):
        for copy in copies(blocks - 2 + side, side):
            copy.wait()


def depth_weight_body(hbuf, cbuf, deb, dhv, *, span):
    dhv[...] = jnp.zeros_like(dhv)
    dhv[0:1] = deb[0:1]
    per_sum = 4
    for t in range(hbuf.shape[0]):
        lanes = slice(t * 128, (t + 1) * 128)
        sums = [jnp.zeros((GROUP // 2, 128), F32) for _ in range(10)]
        for m in range(span // per_sum):
            parts = [None] * 10
            for col in range(per_sum * m, per_sum * (m + 1)):
                h = [
                    [hbuf[t, group(r * (span + 2) + col + d)] for d in range(3)]
                    for r in range(REDUCE + 2)
                ]
                for i in range(REDUCE):
                    gc = cbuf[t, group(i * (span + 2) + col + 1)]
                    terms = [gc] + [gc * h[i + a][c] for a in range(3) for c in range(3)]
                    parts = [
                        term if part is None else part + term for part, term in zip(parts, terms)
                    ]
            sums = [total + fold_rows(part.astype(F32)) for total, part in zip(sums, parts)]
        for n in range(10):
            dhv[1 + n : 2 + n, lanes] = row_sum(sums[n])


def output_body(abuf, stream_edge, stream_inner, vec, sw, out, acc, *, cols, slots):
    spans = GROUP // slots
    span = cols // spans
    line = span * GROUP
    for r in range(REDUCE):
        rows = slice(r * line, (r + 1) * line)
        acc[rows] = nn(abuf[rows], sw[...] * 0.5)
    for s in range(slots):
        for q in range(spans):
            for r in range(REDUCE):
                there = slice(r * cols + q * span, r * cols + (q + 1) * span)
                part = stream_edge if r in EDGE_ROWS else stream_inner
                at = (EDGE_ROWS if r in EDGE_ROWS else INNER_ROWS).index(r) * cols + q * span
                value = acc[group_places(r, s, q, cols, slots), :] + part[s, at : at + span]
                out[s, there] = (value + vec[SHRINK_BIAS : SHRINK_BIAS + 1]).astype(BF16)


def attend_back_body(*refs, pairs, cols, slots, rows):
    edge = rows == EDGE_ROWS
    (gn, stream_two, g, attended, probs, queries, normed, vec, ow, kv_all), refs = refs[:10], refs[10:]
    if edge:
        (up, down, dkv_in, dow_in, dqw_in, dvec_in), refs = refs[:6], refs[6:]
    (gst, gq, dow, dqw, dvec), refs = refs[:5], refs[5:]
    dkvs, (gpbuf, dsbuf, branch, gabuf) = refs[:-4], refs[-4:]
    grad = flat_rows(gn)
    if edge:
        lines = [part[s] for s in range(slots) for part in (up, down)]
        grad = grad + jnp.concatenate(lines, axis=0).astype(F32)
    hat, scale = norm_stats(flat_rows(stream_two), 1e-06)
    gi = pick_rows(g, rows, cols).astype(F32)
    value = norm_back(grad, hat, scale, vec[SECOND_GAIN : SECOND_GAIN + 1]) + gi
    gst[...] = value.reshape(gst.shape)
    low = value.astype(BF16)
    branch[...] = low
    gabuf[...] = nt(low, ow[...]).astype(BF16)
    count = len(rows) * cols
    keys = gpbuf.shape[2] // HEADS
    for s in range(slots):
        gpbuf[s] = nt(gabuf[s * count : (s + 1) * count], both_heads(kv_all, s, 128))
    for s in range(slots):
        for h in range(HEADS):
            span = slice(h * keys, (h + 1) * keys)
            p = probs[s, :, span].astype(F32)
            gp = gpbuf[s, :, span]
            inner = jnp.sum(gp * p, axis=-1, keepdims=True)
            dsbuf[s, :, span] = (p * (gp - inner)).astype(BF16)
    factor = (128 // HEADS) ** (-0.5)
    for s in range(slots):
        gq[s] = (nn(dsbuf[s], both_heads(kv_all, s, 0)) * factor).astype(BF16)

    def fold(both):
        return jnp.concatenate([both[:64, :keys], both[64:, keys:]], axis=0).T

    for s in range(slots):
        dk = fold(nn(queries[s].T, dsbuf[s])) * factor
        dv = fold(nn(gabuf[s * count : (s + 1) * count].T, probs[s]))
        dkv = jnp.concatenate([dk, dv], axis=1)
        if edge:
            dkv = (dkv + dkv_in[s]).astype(BF16)
            each = keys // pairs
            for n in range(pairs):
                dkvs[n][s] = dkv[n * each : (n + 1) * each]
        else:
            dkvs[0][s] = dkv
    dow[...] = tn(flat_rows(attended), branch[...])
    dqw[...] = tn(pick_rows(normed, rows, cols), flat_rows(gq))
    sums = {
        SECOND_GAIN: row_sum(grad * hat),
        SECOND_SHIFT: row_sum(grad),
        SHRINK_BIAS: row_sum(gi),
        OUTPUT_BIAS: row_sum(branch[...].astype(F32)),
        QUERY_BIAS: row_sum(flat_rows(gq).astype(F32)),
    }
    none = jnp.zeros((1, 128), F32)
    dvec[...] = jnp.concatenate([sums.get(n, none) for n in range(VECTORS)], axis=0)
    if edge:
        dow[...] += dow_in[...]
        dqw[...] += dqw_in[...]
        dvec[...] += dvec_in[...]


def reduce_back_body(*refs, parts, slots, tiles):
    arrived, refs = refs[:parts], refs[parts:]
    (meta, reduced, blocks, vec, rw, kw, vw, dexpand, dshrink, dhv, doutput, dquery, dvec_in) = refs[:13]
    gnb, dvec, keep, send = refs[13:]
    upper = core_place(meta, slots, tiles) == 1

    def place(chunk, first, second):
        rows = slice(chunk * 128, (chunk + 1) * 128)
        keep[rows] = jnp.where(upper, second, first)
        send[rows] = jnp.where(upper, first, second).astype(BF16)

    keys = reduced.shape[0] // slots
    dkv = arrived[-1][...].astype(F32)
    for part in arrived[:-1]:
        dkv = dkv + part[:, :keys].astype(F32)
    dkv = dkv.reshape(slots * keys, 256)
    dk, dv = dkv[:, :128], dkv[:, 128:]
    hat, scale = norm_stats(reduced[...], 1e-06)
    gain = vec[REDUCE_GAIN : REDUCE_GAIN + 1]
    rn = (hat * gain + vec[REDUCE_SHIFT : REDUCE_SHIFT + 1]).astype(BF16).astype(F32)
    dkw = tn(rn, dk, HIGHEST)
    dvw = tn(rn, dv, HIGHEST)
    grad = nt(dk, kw[...].astype(F32), HIGHEST) + nt(dv, vw[...].astype(F32), HIGHEST)
    low = norm_back(grad, hat, scale, gain).astype(BF16)
    gnb[...] = nt(low, rw[...])
    sums = {
        VALUE_BIAS: row_sum(dv),
        REDUCE_GAIN: row_sum(grad * hat),
        REDUCE_SHIFT: row_sum(grad),
        REDUCE_BIAS: row_sum(low.astype(F32)),
    }
    dvec[...] = jnp.concatenate(
        [sums.get(n, dvec_in[n : n + 1]) for n in range(VECTORS)], axis=0
    )
    spans = dexpand.shape[1] // 128
    second = [dexpand[:, t * 128 : (t + 1) * 128] for t in range(spans)]
    second += [dshrink[t * 128 : (t + 1) * 128] for t in range(spans)]
    second += [jnp.concatenate([dhv[:, t * 128 : (t + 1) * 128] for t in range(spans)], axis=0)]
    second += [doutput[...], dquery[...]]
    first = [tn(blocks[:, t * 128 : (t + 1) * 128], low) for t in range(REDUCE * REDUCE)]
    first += [dkw, dvw, jnp.zeros((128, 128), F32)]
    for chunk, (one, two) in enumerate(zip(first, second, strict=True)):
        place(chunk, one, two)


EARLY_ROWS = 19 * 128
LATE_ROWS = 3 * 128


def embed_back_body(
    meta, gnb, gq_edge, gq_inner, gst_edge, gst_inner, esum, vec, qw, dvec_in,
    ge, ge_first, dvec,
    gbuf, *, cols, slots, tiles,
):
    keys = cols // REDUCE
    cells = REDUCE * cols
    for s in range(slots):
        for a in range(REDUCE):
            for b in range(REDUCE):
                at = (a * REDUCE + b) * 128
                piece = gnb[s * keys : (s + 1) * keys, at : at + 128]
                gbuf[pl.ds(s * cells + a * cols + b, keys, REDUCE), :] = piece

    def joined(edge, inner):
        lines = []
        for s in range(slots):
            lines += [edge[s, :cols], inner[s], edge[s, cols:]]
        return jnp.concatenate(lines, axis=0)

    grad = gbuf[...] + nt(joined(gq_edge, gq_inner), qw[...])
    gain = vec[EMBED_GAIN : EMBED_GAIN + 1]
    hat, scale = norm_stats(flat_rows(esum), 1e-05)
    hat_one, scale_one = norm_stats(hat * gain + vec[EMBED_SHIFT : EMBED_SHIFT + 1], 1e-06)
    sums = {FIRST_GAIN: row_sum(grad * hat_one), FIRST_SHIFT: row_sum(grad)}
    grad = norm_back(grad, hat_one, scale_one, vec[FIRST_GAIN : FIRST_GAIN + 1])
    grad = grad + joined(gst_edge, gst_inner)
    sums[EMBED_GAIN] = row_sum(grad * hat)
    sums[EMBED_SHIFT] = row_sum(grad)
    low = norm_back(grad, hat, scale, gain).astype(BF16)
    wide = low.astype(F32)
    sums[EMBED_BIAS] = row_sum(wide)
    dvec[...] = jnp.concatenate(
        [sums.get(n, dvec_in[n : n + 1]) for n in range(VECTORS)], axis=0
    )
    for s, part in enumerate(by_slot(wide, slots)):
        _, same_up, _ = same_flags(meta, s, slots, tiles)
        ge_first[s] = (part[:cols] * same_up).astype(BF16)
    masks = [side_mask(meta, s, slots, tiles, cols, REDUCE, False) for s in range(slots)]
    mask = jnp.concatenate(masks, axis=0)
    shifted = (pltpu.roll(wide, slots * cells - 1, 0) * mask).astype(BF16)
    ge[:, :, :128] = low.reshape(slots, cells, 128)
    ge[:, :, 128:] = shifted.reshape(slots, cells, 128)


def embed_weight_body(meta, ge, pairs, top_pairs, dvec, keep, send, *, half, slots, tiles):
    upper = core_place(meta, slots, tiles) == 1
    all_ge = ge[...].reshape(-1, ge.shape[2])
    parts = []
    for a in range(3):
        lines = [(s, 2 * i + a - 1) for s in range(slots) for i in range(REDUCE)]
        lhs = [top_pairs[s] if n < 0 else pairs[s, n] for s, n in lines]
        part = nn(jnp.concatenate(lhs, axis=1), all_ge)
        parts += [part[half:, 128:], part[:, :128]]
    dew = jnp.concatenate(parts, axis=0)
    count = 9 * half // 2
    first, second = dew[:count], dew[count:]
    keep[:count] = jnp.where(upper, second, first)
    send[:count] = jnp.where(upper, first, second).astype(BF16)
    vectors = dvec[...]
    none = jnp.zeros_like(vectors)
    end = count + VECTORS
    keep[count:end] = jnp.where(upper, none, vectors)
    send[count:end] = jnp.where(upper, vectors, none).astype(BF16)
    keep[end:] = jnp.zeros((LATE_ROWS - end, 128), F32)
    send[end:] = jnp.zeros((LATE_ROWS - end, 128), BF16)


def spread_weights(ew, a):
    none = jnp.zeros_like(ew[0, 0])
    even = jnp.concatenate([ew[a, 1], none], axis=1)
    odd = jnp.concatenate([ew[a, 2], ew[a, 0]], axis=1)
    return jnp.concatenate([even, odd], axis=0)


def mixed_columns(lines, split, half, cols):
    lines = [jnp.concatenate([part[:half], part[half:]], axis=1) for part in lines]
    mixed = nt(jnp.concatenate(lines, axis=0), split[...])
    return mixed.reshape(len(lines), half, 2 * cols)


def input_back_body(s, ge, ew, gx, split, *, cols, half):
    @pl.when(s == 0)
    def _():
        split[...] = split_columns(2 * cols)

    own = ge[0]
    upper_rows = nt(spread_weights(ew, 1), own).astype(BF16)
    inner = nt(spread_weights(ew, 2), own[:-cols]) + nt(spread_weights(ew, 0), own[cols:])
    inner = inner.astype(BF16)
    lines = []
    for i in range(REDUCE):
        cells = slice(i * cols, (i + 1) * cols)
        lines.append(upper_rows[:, cells])
        lines.append(inner[:, cells] if i < REDUCE - 1 else jnp.zeros_like(upper_rows[:, cells]))
    gx[0] = mixed_columns(lines, split, half, cols)


def last_row_body(meta, ge, below, ew, done, gx, split, *, cols, half, slots, tiles):
    s = pl.program_id(0)
    same_sides, _, _ = same_flags(meta, s, slots, tiles)

    @pl.when(s == 0)
    def _():
        split[...] = split_columns(2 * cols)

    column = lax.broadcasted_iota(jnp.int32, (cols, 1), 0)
    mask = jnp.where(column == cols - 1, 0.0, jnp.where(column == cols // 2 - 1, same_sides, 1.0))
    shifted = (pltpu.roll(below[0].astype(F32), cols - 1, 0) * mask).astype(BF16)
    under = jnp.concatenate([below[0], shifted], axis=1)
    line = nt(spread_weights(ew, 2), ge[0]) + nt(spread_weights(ew, 0), under)
    gx[0] = mixed_columns([line.astype(BF16)], split, half, cols)


def unpack_body(meta, own, other, *outs, slots, tiles, half, middle):
    upper = core_place(meta, slots, tiles) == 1
    at = middle_place(meta, slots, tiles)
    early, late = EARLY_ROWS // middle, LATE_ROWS // middle

    def pick(start, count, base, size):
        step = math.gcd(size, 128)
        mine, theirs = [], []
        for row in range(start, start + count, step):
            chunk, offset = divmod(row, size)
            where = (chunk ^ at) * (early + late) + base + offset
            rows = pl.ds(pl.multiple_of(where, math.gcd(step, 16)), step)
            mine.append(own[rows])
            theirs.append(other[rows])
        mine = jnp.concatenate(mine, axis=0).astype(F32)[:count]
        theirs = jnp.concatenate(theirs, axis=0).astype(F32)[:count]
        return jnp.where(upper, theirs, mine), jnp.where(upper, mine, theirs)

    (embed, reduce, query, key, value, output, expand, shrink, *vectors) = outs
    spans = expand.shape[1] // 128
    taps = REDUCE * REDUCE
    for chunk in range(EARLY_ROWS // 128):
        first, second = pick(chunk * 128, 128, 0, early)
        if chunk < taps:
            reduce[chunk * 128 : (chunk + 1) * 128] = first
        elif chunk == taps:
            key[...] = first
        elif chunk == taps + 1:
            value[...] = first
        if chunk < spans:
            expand[:, chunk * 128 : (chunk + 1) * 128] = second
        elif chunk < 2 * spans:
            shrink[(chunk - spans) * 128 : (chunk - spans + 1) * 128] = second
        elif chunk == 2 * spans:
            hidden_vectors = second
        elif chunk == 2 * spans + 1:
            output[...] = second
        else:
            query[...] = second
    count = 9 * half // 2
    first, second = pick(0, count + VECTORS, early, late)
    embed[:count] = first[:count]
    embed[count:] = second[:count]
    *short, expand_bias, depth, depth_bias = vectors
    for n, out in enumerate(short):
        out[...] = first[count + n]
    for t in range(spans):
        lanes = slice(t * 128, (t + 1) * 128)
        at = t * HIDDEN_VECTORS
        expand_bias[lanes] = hidden_vectors[at]
        depth_bias[lanes] = hidden_vectors[at + 1]
        for a in range(3):
            depth[a, :, lanes] = hidden_vectors[at + 2 + 3 * a : at + 5 + 3 * a]


def turned_by(array, distance):
    count = lax.axis_size("tile")
    return lax.ppermute(array, "tile", [(i, (i + distance) % count) for i in range(count)])


def crossed(array, bits):
    count = lax.axis_size("tile")
    return lax.ppermute(array, "tile", [(i, i ^ bits) for i in range(count)])


def device_levels():
    batch_count, tile_count = lax.axis_size("batch"), lax.axis_size("tile")
    batch_at, tile_at = lax.axis_index("batch"), lax.axis_index("tile")

    def routes(size, target):
        return [
            [
                (b * tile_count + t, target(b, t, turn))
                for b in range(batch_count)
                for t in range(tile_count)
            ]
            for turn in range(1, size)
        ]

    def flat(batch, tile):
        return batch * tile_count + tile

    return (
        (2, batch_at % 2, routes(2, lambda b, t, turn: flat(b ^ turn, t))),
        (
            batch_count,
            (batch_at // 2) * 2 + tile_at % 2,
            routes(batch_count, lambda b, t, turn: flat(b ^ (turn // 2 * 2), t ^ (turn % 2))),
        ),
        (
            tile_count // 2,
            tile_at // 2,
            routes(tile_count // 2, lambda b, t, turn: flat(b, t ^ (2 * turn))),
        ),
    )


AXES = ("batch", "tile")


def scatter_level(parts, level):
    size, at, turns = level
    own = lax.dynamic_index_in_dim(parts, at, 0, keepdims=False)
    sent = [
        lax.ppermute(
            lax.dynamic_index_in_dim(parts, at ^ turn, 0, keepdims=False).astype(BF16),
            AXES,
            turns[turn - 1],
        )
        for turn in range(1, size)
    ]
    return own, sent


def added(own, sent):
    for part in sent:
        own = own + part.astype(F32)
    return own


def gather_level(low, level):
    size, _, turns = level
    return jnp.stack([low] + [lax.ppermute(low, AXES, turns[turn - 1]) for turn in range(1, size)])


def from_first(blocks, level):
    size, at, _ = level
    return jnp.stack(
        [lax.dynamic_index_in_dim(blocks, at ^ n, 0, keepdims=False) for n in range(size)]
    )


def shards(
    embed_input,
    piece_image,
    embed_weight,
    embed_bias,
    embed_gain,
    embed_shift,
    first_gain,
    first_shift,
    query_weight,
    query_bias,
    reduce_weight,
    reduce_bias,
    reduce_gain,
    reduce_shift,
    key_weight,
    value_weight,
    value_bias,
    output_weight,
    output_bias,
    second_gain,
    second_shift,
    expand_weight,
    expand_bias,
    depth_weight,
    depth_bias,
    shrink_weight,
    shrink_bias,
    cotangent,
):
    source = embed_input[0].swapaxes(2, 3)
    slots, _, channels, wide_cols = source.shape
    cols = wide_cols // 2
    cells = REDUCE * cols
    keys = cols // REDUCE
    model = embed_weight.shape[3]
    hidden = expand_weight.shape[1]
    tiles = lax.axis_size("tile")
    tile_at = lax.axis_index("tile")
    pieces = tiles
    core_level, middle_level, high_level = device_levels()

    top = turned_by(embed_input[0, :, 2 * REDUCE - 1].swapaxes(1, 2), 1)
    meta = jnp.concatenate(
        [piece_image.reshape(-1), jnp.stack([tile_at, core_level[1], middle_level[1]]).astype(jnp.int32)]
    )
    vec = jnp.stack(
        [
            embed_bias, embed_gain, embed_shift, first_gain, first_shift, query_bias, reduce_bias,
            reduce_gain, reduce_shift, value_bias, output_bias, second_gain, second_shift,
            shrink_bias, shrink_bias, shrink_bias,
        ]
    ).astype(F32)
    hv = jnp.stack([expand_bias, depth_bias]).astype(F32)

    kw = dict(cols=cols)
    place = dict(slots=slots, tiles=tiles)
    flat_reduce = reduce_weight.reshape(-1, model)
    pairs, partial_sum = slot_call(
        partial(embed_own_body, **kw, **place),
        slots,
        [(meta, "smem"), (source, "far slot"), (embed_weight, "far whole")],
        [
            ((slots, 2 * REDUCE, 2 * channels, cols), BF16, "far slot"),
            ((slots, cells, model), F32, "slot"),
        ],
        [pltpu.VMEM((wide_cols, wide_cols), BF16), pltpu.VMEM((cells, 2 * model), F32)],
        name="embed_own",
        lasts=4,
        looped=True,
    )
    top_pairs, esum, stream, normed, blocks, reduced, kv = vmem_call(
        partial(embed_body, **kw, **place),
        [meta, partial_sum, top, embed_weight, vec, flat_reduce, key_weight, value_weight],
        [
            ((slots, 2 * channels, cols), BF16),
            ((slots, cells, model), F32),
            ((slots, cells, model), F32),
            ((slots, cells, model), BF16),
            ((slots * keys, REDUCE * REDUCE * model), BF16),
            ((slots * keys, model), F32),
            ((slots * keys, 2 * model), BF16),
        ],
        [pltpu.VMEM((slots * cells, model), F32)],
        name="embed",
    )

    grad_out = cotangent[0].reshape(slots, cells, model)
    all_cells = slots * cells
    gp, g_t = pl.pallas_call(
        partial(grouped_body, cols=cols, slots=slots),
        out_shape=[
            jax.ShapeDtypeStruct((all_cells, model), BF16),
            jax.ShapeDtypeStruct((model, all_cells), BF16),
        ],
        scratch_shapes=[pltpu.VMEM((all_cells, model), F32)],
        compiler_params=pltpu.CompilerParams(vmem_limit_bytes=VMEM_BYTES),
        cost_estimate=cost(3),
        name="grouped",
    )(grad_out)

    kv = kv.reshape(slots, keys, 2 * model)
    crossing = {n: crossed(kv, n) for n in range(tiles - 1, 0, -1)}
    kvs = [kv] + [crossing[n] for n in range(1, tiles)]
    kvs, gp, g_t = lax.optimization_barrier((kvs, gp, g_t))

    all_keys = keys * tiles
    part_cells = cells // 2

    def attend(rows, sources, results):
        return vmem_call(
            partial(attend_body, pieces=pieces, rows=rows, **kw, **place),
            [meta, normed, stream, vec, query_weight, output_weight] + sources,
            [
                ((slots, part_cells, model), BF16),
                ((slots, part_cells, HEADS * all_keys), BF16),
                ((slots, part_cells, model), BF16),
                ((slots, part_cells, model), F32),
            ]
            + results,
            [pltpu.VMEM((slots, part_cells, HEADS * all_keys), F32)],
            name="attend",
        )

    *kept_edge, first_row, last_row, kv_all = attend(
        EDGE_ROWS,
        kvs,
        [
            ((slots, cols, model), BF16),
            ((slots, cols, model), BF16),
            ((slots, all_keys, 2 * model), BF16),
        ],
    )
    row_up = turned_by(last_row, 1)
    row_down = turned_by(first_row, -1)
    *kept_inner, normed_inner = attend(
        INNER_ROWS, [kv_all], [((slots, part_cells, model), BF16)]
    )
    row_up, row_down, normed_inner = lax.optimization_barrier((row_up, row_down, normed_inner))
    width = 256
    vmem = pl.BlockSpec(memory_space=pltpu.VMEM)
    ext_cells = slots * (cells + 2 * cols)
    lane_tiles = width // 128
    hidden_blocks = (hidden // width,)
    by_lanes = lambda shape: pl.BlockSpec((shape[0], width), lambda b: (0, b))
    by_tiles = lambda shape: pl.BlockSpec((lane_tiles,) + tuple(shape[1:]), lambda b: (b, 0, 0))
    hidden_shape = (hidden // 128, ext_cells + 2 * GROUP * (REDUCE + 2), 128)
    conv_shape = (hidden // 128, all_cells + 2 * GROUP * REDUCE, 128)
    (
        gn_edge, gn_inner, gn_up, gn_down, d_expand, d_shrink, d_expand_bias, active, hidden_cells, grad_conv,
    ) = pl.pallas_call(
        partial(feed_body, width=width, **kw, **place),
        in_specs=[smem()] + [vmem] * 11,
        out_specs=[vmem] * 7 + [pl.BlockSpec(memory_space=pltpu.HBM)] * 3,
        out_shape=[
            jax.ShapeDtypeStruct((slots, part_cells, model), F32),
            jax.ShapeDtypeStruct((slots, part_cells, model), F32),
            jax.ShapeDtypeStruct((slots, cols, model), BF16),
            jax.ShapeDtypeStruct((slots, cols, model), BF16),
            jax.ShapeDtypeStruct((model, hidden), F32),
            jax.ShapeDtypeStruct((hidden, model), F32),
            jax.ShapeDtypeStruct((8, hidden), F32),
            far((all_cells, hidden), BF16),
            far(hidden_shape, BF16),
            far(conv_shape, BF16),
        ],
        scratch_shapes=[pltpu.VMEM((all_cells, width), BF16)] * 2
        + [pltpu.VMEM((lane_tiles,) + hidden_shape[1:], BF16)] * 2
        + [pltpu.VMEM((lane_tiles,) + conv_shape[1:], BF16)] * 2
        + [
            pltpu.VMEM((ext_cells, width), BF16),
            pltpu.VMEM((all_cells, width), F32),
            pltpu.VMEM((ext_cells, model), F32),
            pltpu.VMEM((ext_cells, model), BF16),
            pltpu.VMEM((model + GROUP, ext_cells), BF16),
            pltpu.SemaphoreType.DMA((3, 2)),
        ],
        compiler_params=pltpu.CompilerParams(vmem_limit_bytes=VMEM_BYTES),
        cost_estimate=cost(18),
        name="feed_forward",
    )(
        meta, first_row, normed_inner, last_row, row_up, row_down, gp, g_t, hv, depth_weight,
        expand_weight, shrink_weight,
    )

    from_up = turned_by(gn_down, 1)
    from_down = turned_by(gn_up, -1)
    pairs_of_tiles = tiles // 2

    def attend_back(rows, grad, kept, sources, results):
        queries, probs, attended, stream_two = kept
        return vmem_call(
            partial(attend_back_body, pairs=pairs_of_tiles, rows=rows, slots=slots, **kw),
            [
                grad, stream_two, grad_out, attended, probs, queries, normed, vec, output_weight,
                kv_all,
            ]
            + sources,
            [
                ((slots, part_cells, model), F32),
                ((slots, part_cells, model), BF16),
                ((model, model), F32),
                ((model, model), F32),
                ((VECTORS, model), F32),
            ]
            + results,
            [
                pltpu.VMEM((slots, part_cells, HEADS * all_keys), F32),
                pltpu.VMEM((slots, part_cells, HEADS * all_keys), BF16),
                pltpu.VMEM((slots * part_cells, model), BF16),
                pltpu.VMEM((slots * part_cells, model), BF16),
            ],
            name="attend_back",
        )

    gst_inner, gq_inner, *sums, dkv_inner = attend_back(
        INNER_ROWS, gn_inner, kept_inner, [], [((slots, all_keys, 2 * model), F32)]
    )
    from_up, from_down, dkv_inner = lax.optimization_barrier((from_up, from_down, dkv_inner))
    gst_edge, gq_edge, d_output, d_query, dvec_a, *dkvs = attend_back(
        EDGE_ROWS,
        gn_edge,
        kept_edge,
        [from_up, from_down, dkv_inner] + sums,
        [((slots, 2 * keys, 2 * model), BF16)] * pairs_of_tiles,
    )
    crossing = {n: crossed(dkvs[n], 2 * n) for n in range(pairs_of_tiles - 1, 0, -1)}
    own_dkvs = [dkvs[0]] + [crossing[n] for n in range(1, pairs_of_tiles)]
    d_hv = pl.pallas_call(
        partial(depth_weight_body, span=cols * slots // GROUP),
        grid=hidden_blocks,
        in_specs=[by_tiles(hidden_shape), by_tiles(conv_shape), by_lanes((8, hidden))],
        out_specs=by_lanes((HIDDEN_VECTORS, hidden)),
        out_shape=jax.ShapeDtypeStruct((HIDDEN_VECTORS, hidden), F32),
        compiler_params=params(),
        cost_estimate=cost(6),
        name="depth_weights",
    )(from_far(hidden_cells), from_far(grad_conv), d_expand_bias)
    own_dkvs, d_hv = lax.optimization_barrier((own_dkvs, d_hv))
    for_mate = own_dkvs[0][:, keys:].astype(F32)
    for part in own_dkvs[1:]:
        for_mate = for_mate + part[:, keys:].astype(F32)
    own_dkvs.append(crossed(for_mate.astype(BF16), 1))

    gnb, dvec_b, keep, send = pl.pallas_call(
        partial(reduce_back_body, parts=len(own_dkvs), **place),
        in_specs=[vmem] * len(own_dkvs) + [smem()] + [vmem] * 12,
        out_specs=[vmem] * 4,
        out_shape=[
            jax.ShapeDtypeStruct((slots * keys, REDUCE * REDUCE * model), F32),
            jax.ShapeDtypeStruct((VECTORS, model), F32),
            jax.ShapeDtypeStruct((EARLY_ROWS, 128), F32),
            jax.ShapeDtypeStruct((EARLY_ROWS, 128), BF16),
        ],
        compiler_params=pltpu.CompilerParams(vmem_limit_bytes=VMEM_BYTES),
        cost_estimate=cost(3),
        name="reduce_back",
    )(
        *own_dkvs, meta, reduced, blocks, vec, flat_reduce, key_weight, value_weight,
        d_expand, d_shrink, d_hv, d_output, d_query, dvec_a,
    )
    got = lax.ppermute(send, AXES, core_level[2][0])

    ge, ge_first, dvec_c = vmem_call(
        partial(embed_back_body, **kw, **place),
        [
            meta, gnb, gq_edge, gq_inner, gst_edge, gst_inner, esum, vec, query_weight, dvec_b,
        ],
        [
            ((slots, cells, 2 * model), BF16),
            ((slots, cols, model), BF16),
            ((VECTORS, model), F32),
        ],
        [pltpu.VMEM((slots * cells, model), F32)],
        name="embed_back",
    )
    below = turned_by(ge_first, -1)
    late_keep, late_send = pl.pallas_call(
        partial(embed_weight_body, half=channels, **place),
        in_specs=[smem()] + [vmem] * 4,
        out_specs=[vmem] * 2,
        out_shape=[
            jax.ShapeDtypeStruct((LATE_ROWS, 128), F32),
            jax.ShapeDtypeStruct((LATE_ROWS, 128), BF16),
        ],
        compiler_params=pltpu.CompilerParams(vmem_limit_bytes=VMEM_BYTES),
        cost_estimate=cost(3),
        name="embed_weights",
    )(meta, ge, pairs, top_pairs, dvec_c)
    late_got = lax.ppermute(late_send, AXES, core_level[2][0])

    middle, high = middle_level[0], high_level[0]
    parts = jnp.concatenate(
        [
            (keep + got.astype(F32)).reshape(middle, -1, 128),
            (late_keep + late_got.astype(F32)).reshape(middle, -1, 128),
        ],
        axis=1,
    )
    (grad_input,) = slot_call(
        partial(input_back_body, half=channels, **kw),
        slots,
        [(ge, "slot"), (embed_weight, "whole")],
        [(source.shape, F32, "slot")],
        [pltpu.VMEM((wide_cols, wide_cols), BF16)],
        name="input_back",
    )
    own, sent = scatter_level(parts, middle_level)
    sent, grad_input = lax.optimization_barrier((sent, grad_input))
    own = added(own, sent)
    own, sent = scatter_level(own.reshape(high, -1, 128), high_level)
    last_line = pl.BlockSpec((1, 1, channels, wide_cols), lambda s: (s, 2 * REDUCE - 1, 0, 0))
    grad_input = pl.pallas_call(
        partial(last_row_body, half=channels, **kw, **place),
        grid=(slots,),
        in_specs=[
            smem(),
            pl.BlockSpec((1, cols, 2 * model), lambda s: (s, REDUCE - 1, 0)),
            per_slot(below.shape),
            whole(embed_weight.shape),
            pl.BlockSpec(memory_space=pl.ANY),
        ],
        out_specs=last_line,
        out_shape=jax.ShapeDtypeStruct(source.shape, F32),
        scratch_shapes=[pltpu.VMEM((wide_cols, wide_cols), BF16)],
        input_output_aliases={4: 0},
        compiler_params=params(),
        cost_estimate=cost(2),
        name="last_row",
    )(meta, ge, below, embed_weight, grad_input)
    sent, grad_input = lax.optimization_barrier((sent, grad_input))
    low = added(own, sent).astype(BF16)
    low = from_first(gather_level(low, high_level), high_level).reshape(-1, 128)
    out = pl.pallas_call(
        partial(output_body, cols=cols, slots=slots),
        out_shape=jax.ShapeDtypeStruct((slots, cells, model), BF16),
        scratch_shapes=[pltpu.VMEM((all_cells, model), F32)],
        compiler_params=pltpu.CompilerParams(vmem_limit_bytes=VMEM_BYTES),
        cost_estimate=cost(3),
        name="output",
    )(active, kept_edge[3], kept_inner[3], vec, shrink_weight)
    gathered = gather_level(low, middle_level)
    gathered, out = lax.optimization_barrier((gathered, out))
    low = gathered.reshape(-1, 128)
    other = lax.ppermute(low, AXES, core_level[2][0])

    shapes = [(9 * channels, model), (REDUCE * REDUCE * model, model)]
    shapes += [(model, model)] * 4 + [(model, hidden), (hidden, model)]
    shapes += [(model,)] * 14 + [(hidden,), (3, 3, hidden), (hidden,)]
    results = pl.pallas_call(
        partial(unpack_body, half=channels, middle=middle, **place),
        in_specs=[smem()] + [vmem] * 2,
        out_specs=[vmem] * len(shapes),
        out_shape=[jax.ShapeDtypeStruct(shape, F32) for shape in shapes],
        compiler_params=pltpu.CompilerParams(vmem_limit_bytes=VMEM_BYTES),
        cost_estimate=cost(3),
        name="unpack",
    )(meta, low, other)
    (s_embed, s_reduce, s_query, s_key, s_value, s_output, s_expand, s_shrink) = results[:8]
    vectors = results[8:22]
    s_expand_bias, s_depth, s_depth_bias = results[22:]
    return (
        out.reshape(cotangent.shape),
        grad_input.swapaxes(2, 3)[None],
        s_embed.reshape(embed_weight.shape),
        vectors[EMBED_BIAS],
        vectors[EMBED_GAIN],
        vectors[EMBED_SHIFT],
        vectors[FIRST_GAIN],
        vectors[FIRST_SHIFT],
        s_query,
        vectors[QUERY_BIAS],
        s_reduce.reshape(reduce_weight.shape),
        vectors[REDUCE_BIAS],
        vectors[REDUCE_GAIN],
        vectors[REDUCE_SHIFT],
        s_key,
        s_value,
        vectors[VALUE_BIAS],
        s_output,
        vectors[OUTPUT_BIAS],
        vectors[SECOND_GAIN],
        vectors[SECOND_SHIFT],
        s_expand,
        s_expand_bias,
        s_depth,
        s_depth_bias,
        s_shrink,
        vectors[SHRINK_BIAS],
    )


def solution(mesh):
    shard_rows = P("batch", None, "tile", None, None)
    in_specs = (shard_rows, P("batch", None, None, None)) + (P(),) * 25 + (shard_rows,)
    out_specs = (shard_rows, shard_rows) + (P(),) * 25
    return jax.shard_map(shards, mesh=mesh, in_specs=in_specs, out_specs=out_specs, check_vma=False)
```

```python
import math
from functools import partial

import jax
import jax.numpy as jnp
from jax import lax
from jax.experimental import pallas as pl
from jax.experimental.pallas import tpu as pltpu
from jax.sharding import PartitionSpec as P

HEADS = 2
REDUCE = 4
F32 = jnp.float32
BF16 = jnp.bfloat16
HIGHEST = lax.Precision.HIGHEST
LOG2E = math.log2(math.e)
VMEM_BYTES = 32 * 1024 * 1024

(
    EMBED_BIAS,
    EMBED_GAIN,
    EMBED_SHIFT,
    FIRST_GAIN,
    FIRST_SHIFT,
    QUERY_BIAS,
    REDUCE_BIAS,
    REDUCE_GAIN,
    REDUCE_SHIFT,
    VALUE_BIAS,
    OUTPUT_BIAS,
    SECOND_GAIN,
    SECOND_SHIFT,
    SHRINK_BIAS,
) = range(14)
VECTORS = 16
HIDDEN_VECTORS = 16


def nn(left, right, precision=None):
    return lax.dot_general(
        left, right, (((1,), (0,)), ((), ())), precision=precision, preferred_element_type=F32
    )


def nt(left, right, precision=None):
    return lax.dot_general(
        left, right, (((1,), (1,)), ((), ())), precision=precision, preferred_element_type=F32
    )


def tn(left, right, precision=None):
    return lax.dot_general(
        left, right, (((0,), (0,)), ((), ())), precision=precision, preferred_element_type=F32
    )


def norm_stats(values, epsilon):
    centered = values - jnp.mean(values, axis=-1, keepdims=True)
    scale = lax.rsqrt(jnp.mean(centered * centered, axis=-1, keepdims=True) + epsilon)
    return centered * scale, scale


def norm_back(grad, hat, scale, gain):
    grad_hat = grad * gain
    mean_grad = jnp.mean(grad_hat, axis=-1, keepdims=True)
    mean_dot = jnp.mean(grad_hat * hat, axis=-1, keepdims=True)
    return scale * (grad_hat - mean_grad - hat * mean_dot)


def row_sum(values):
    return jnp.sum(values, axis=0, keepdims=True)


def params(vmem=VMEM_BYTES, axes=1):
    return pltpu.CompilerParams(
        vmem_limit_bytes=vmem, dimension_semantics=("arbitrary",) * axes
    )


def whole(shape, slots=None):
    rank = len(shape)
    return pl.BlockSpec(tuple(shape), lambda *_: (0,) * rank)


def per_slot(shape, slots=None):
    rank = len(shape)
    return pl.BlockSpec((1,) + tuple(shape[1:]), lambda s: (s,) + (0,) * (rank - 1))


def per_slot_rows(shape, slots):
    return pl.BlockSpec((shape[0] // slots, shape[1]), lambda s: (s, 0))


def smem():
    return pl.BlockSpec(memory_space=pltpu.SMEM)


def far(shape, dtype):
    return pltpu.HBM(tuple(shape), dtype)


def from_far(array):
    return pltpu.with_memory_space_constraint(array, pltpu.HBM)


def cost(microseconds):
    return pl.CostEstimate(
        flops=int(microseconds * 1.0e9), bytes_accessed=int(microseconds * 3.0e6), transcendentals=0
    )


def slot_call(body, slots, inputs, outputs, scratch=(), name=None, lasts=5, looped=False):
    kinds = {"slot": per_slot, "whole": whole, "keys": per_slot_rows}
    arrays = [(a.shape, a.dtype, k) for a, k in inputs] + list(outputs)
    names = [k.removeprefix("far ") for *_, k in arrays]
    are_far = [k.startswith("far ") for *_, k in arrays]
    count_in = len(inputs)
    moved = [n for n, is_far in enumerate(are_far) if is_far and looped]

    def spec(shape, kind, is_far):
        if kind == "smem":
            return smem()
        if looped:
            return pl.BlockSpec(memory_space=pltpu.HBM if is_far else pltpu.VMEM)
        return kinds[kind](shape, slots)

    def grid_body(*refs):
        body(pl.program_id(0), *refs)

    def loop_body(*refs):
        refs = list(refs)
        extra = refs[len(names) :]
        if moved:
            sems, extra = extra[-1], extra[:-1]
            buffers, extra = extra[len(extra) - len(moved) :], extra[: len(extra) - len(moved)]

        def copy(m, s):
            n = moved[m]
            here, there = buffers[m], refs[n]
            if names[n] == "slot":
                here, there = here.at[pl.ds(s, 1)], there.at[pl.ds(s, 1)]
            source, target = (there, here) if n < count_in else (here, there)
            return pltpu.make_async_copy(source, target, sems.at[m, s])

        into = [m for m, n in enumerate(moved) if n < count_in]
        out_of = [m for m, n in enumerate(moved) if n >= count_in]
        whole_in = [m for m in into if names[moved[m]] == "whole"]
        slot_in = [m for m in into if names[moved[m]] == "slot"]
        slot_out = [m for m in out_of if names[moved[m]] == "slot"]
        whole_out = [m for m in out_of if names[moved[m]] == "whole"]
        for m in slot_in:
            copy(m, 0).start()
        for m in whole_in:
            copy(m, 0).start()
        for s in range(1, slots):
            for m in slot_in:
                copy(m, s).start()
        local = list(refs[: len(names)])
        for m, n in enumerate(moved):
            local[n] = buffers[m]
        for m in whole_in:
            copy(m, 0).wait()

        def step(s, carry):
            views = []
            for ref, kind, (shape, *_) in zip(local, names, arrays):
                if kind == "slot":
                    ref = ref.at[pl.ds(s, 1)]
                elif kind == "keys":
                    count = shape[0] // slots
                    ref = ref.at[pl.ds(pl.multiple_of(s * count, count), count)]
                views.append(ref)
            for m in slot_in:
                copy(m, s).wait()
            body(s, *views, *extra)
            for m in slot_out:
                copy(m, s).start()
            return carry

        lax.fori_loop(0, slots, step, 0)
        for m in whole_out:
            copy(m, 0).start()
        for s in range(slots):
            for m in slot_out:
                copy(m, s).wait()
        for m in whole_out:
            copy(m, 0).wait()

    specs = [spec(shape, kind, f) for (shape, *_), kind, f in zip(arrays, names, are_far)]
    scratch = list(scratch)
    if moved:
        scratch += [pltpu.VMEM(arrays[n][0], arrays[n][1]) for n in moved]
        scratch += [pltpu.SemaphoreType.DMA((len(moved), slots))]
    return pl.pallas_call(
        loop_body if looped else grid_body,
        grid=() if looped else (slots,),
        in_specs=specs[:count_in],
        out_specs=specs[count_in:],
        out_shape=[
            (far if k.startswith("far ") else jax.ShapeDtypeStruct)(s, d) for s, d, k in outputs
        ],
        scratch_shapes=scratch,
        compiler_params=pltpu.CompilerParams(vmem_limit_bytes=VMEM_BYTES) if looped else params(),
        cost_estimate=cost(lasts),
        name=name,
    )(*[from_far(a) if k.startswith("far ") else a for a, k in inputs])


def vmem_call(body, inputs, outputs, scratch=(), name=None, lasts=5):
    vmem = pl.BlockSpec(memory_space=pltpu.VMEM)
    return pl.pallas_call(
        body,
        in_specs=[smem() if a.dtype == jnp.int32 else vmem for a in inputs],
        out_specs=[vmem] * len(outputs),
        out_shape=[jax.ShapeDtypeStruct(shape, dtype) for shape, dtype in outputs],
        scratch_shapes=list(scratch),
        compiler_params=pltpu.CompilerParams(vmem_limit_bytes=VMEM_BYTES),
        cost_estimate=cost(lasts),
        name=name,
    )(*inputs)


def flat_rows(ref):
    return ref[...].reshape(-1, ref.shape[-1])


def by_slot(values, slots):
    count = values.shape[0] // slots
    return [values[s * count : (s + 1) * count] for s in range(slots)]


def tile_ids(meta, s, tile, tiles):
    at = (s * tiles + tile) * 2
    return meta[at], meta[at + 1]


def tile_place(meta, slots, tiles):
    return meta[slots * tiles * 2]


def core_place(meta, slots, tiles):
    return meta[slots * tiles * 2 + 1]


def middle_place(meta, slots, tiles):
    return meta[slots * tiles * 2 + 2]


def as_flag(condition):
    return jnp.where(condition, 1.0, 0.0).astype(F32)


def same_flags(meta, s, slots, tiles):
    at = tile_place(meta, slots, tiles)
    own = tile_ids(meta, s, at, tiles)
    up = tile_ids(meta, s, jnp.maximum(at - 1, 0), tiles)
    down = tile_ids(meta, s, jnp.minimum(at + 1, tiles - 1), tiles)
    return (
        as_flag(own[0] == own[1]),
        as_flag((own[0] == up[0]) & (at > 0)),
        as_flag((own[0] == down[0]) & (at < tiles - 1)),
    )


def split_columns(size):
    source = lax.broadcasted_iota(jnp.int32, (size, size), 0)
    target = lax.broadcasted_iota(jnp.int32, (size, size), 1)
    wanted = jnp.where(target < size // 2, 2 * target, 2 * target - size + 1)
    return jnp.where(source == wanted, 1.0, 0.0).astype(BF16)


def embed_weights(ew):
    half = ew.shape[2]
    none = jnp.zeros_like(ew[0, 0])
    weights = []
    for a in range(3):
        main = ew[a, 1:3].reshape(2 * half, 128)
        side = jnp.concatenate([none, ew[a, 0]], axis=0)
        weights.append(jnp.concatenate([main, side], axis=1))
    return jnp.concatenate(weights, axis=0)


def embed_own_body(s, meta, x, ew, pairs, partial_sum, split, zbuf, *, cols, slots, tiles):
    half = x.shape[2]

    @pl.when(s == 0)
    def _():
        split[...] = split_columns(2 * cols)

    own = nn(x[0].reshape(2 * REDUCE * half, 2 * cols), split[...])
    for r in range(2 * REDUCE):
        row = own[r * half : (r + 1) * half].astype(BF16)
        pairs[0, r, :half] = row[:, :cols]
        pairs[0, r, half:] = row[:, cols:]
    weights = embed_weights(ew)
    for i in range(REDUCE):
        first = max(2 * i - 1, 0)
        lines = pairs[0, first : 2 * i + 2]
        lines = lines.reshape(lines.shape[0] * 128, cols)
        zbuf[i * cols : (i + 1) * cols] = tn(lines, weights[-lines.shape[0] :])
    mask = side_mask(meta, s, slots, tiles, cols, REDUCE, True)
    partial_sum[0] = zbuf[:, :128] + pltpu.roll(zbuf[:, 128:], 1, 0) * mask


def side_mask(meta, s, slots, tiles, cols, rows, forward):
    column = lax.broadcasted_iota(jnp.int32, (rows * cols, 1), 0) % cols
    outside = 0 if forward else cols - 1
    border = cols // 2 if forward else cols // 2 - 1
    same_sides, _, _ = same_flags(meta, s, slots, tiles)
    return jnp.where(column == outside, 0.0, jnp.where(column == border, same_sides, 1.0))


def embed_body(
    meta, partial_sum, top, ew, vec, rw, kw, vw,
    top_pairs, esum, stream, normed, blocks, reduced, kv,
    nbuf, *, cols, slots, tiles,
):
    keys = cols // REDUCE
    cells = REDUCE * cols
    half = top.shape[1]
    above = by_slot(nn(flat_rows(top), split_columns(2 * cols)), slots)
    weights = embed_weights(ew)[:128]
    lines = []
    for s in range(slots):
        _, same_up, _ = same_flags(meta, s, slots, tiles)
        row = (above[s] * same_up).astype(BF16)
        top_pairs[s, :half] = row[:, :cols]
        top_pairs[s, half:] = row[:, cols:]
        z = tn(top_pairs[s], weights)
        mask = side_mask(meta, s, slots, tiles, cols, 1, True)
        first = partial_sum[s, :cols] + z[:, :128] + pltpu.roll(z[:, 128:], 1, 0) * mask
        lines += [first, partial_sum[s, cols:]]
    value = jnp.concatenate(lines, axis=0) + vec[EMBED_BIAS : EMBED_BIAS + 1]
    esum[...] = value.reshape(esum.shape)
    hat, _ = norm_stats(value, 1e-05)
    st = hat * vec[EMBED_GAIN : EMBED_GAIN + 1] + vec[EMBED_SHIFT : EMBED_SHIFT + 1]
    stream[...] = st.reshape(stream.shape)
    hat, _ = norm_stats(st, 1e-06)
    nm = hat * vec[FIRST_GAIN : FIRST_GAIN + 1] + vec[FIRST_SHIFT : FIRST_SHIFT + 1]
    low = nm.astype(BF16)
    normed[...] = low.reshape(normed.shape)
    nbuf[...] = low.astype(F32)
    for s in range(slots):
        for a in range(REDUCE):
            for b in range(REDUCE):
                at = (a * REDUCE + b) * 128
                piece = nbuf[pl.ds(s * cells + a * cols + b, keys, REDUCE), :]
                blocks[s * keys : (s + 1) * keys, at : at + 128] = piece.astype(BF16)
    value = nn(blocks[...], rw[...]) + vec[REDUCE_BIAS : REDUCE_BIAS + 1]
    reduced[...] = value
    hat, _ = norm_stats(value, 1e-06)
    rn = (hat * vec[REDUCE_GAIN : REDUCE_GAIN + 1] + vec[REDUCE_SHIFT : REDUCE_SHIFT + 1]).astype(BF16)
    kv[:, :128] = nn(rn, kw[...]).astype(BF16)
    kv[:, 128:] = (nn(rn, vw[...]) + vec[VALUE_BIAS : VALUE_BIAS + 1]).astype(BF16)


def both_heads(kv, s, at):
    rows = kv[s, :, at : at + 128]
    lane = lax.broadcasted_iota(jnp.int32, rows.shape, 1)
    zero = jnp.zeros_like(rows)
    return jnp.concatenate(
        [jnp.where(lane < 64, rows, zero), jnp.where(lane < 64, zero, rows)], axis=0
    )


def key_bias(meta, s, slots, tiles, keys):
    at = tile_place(meta, slots, tiles)
    own = tile_ids(meta, s, at, tiles)
    part = keys // (2 * tiles)
    entry = lax.broadcasted_iota(jnp.int32, (1, keys), 1) // part
    rows = [jnp.zeros((1, keys), F32) for _ in range(2)]
    for n in range(tiles):
        ids = tile_ids(meta, s, at ^ n, tiles)
        for side in range(2):
            for query in range(2):
                value = jnp.where(ids[side] == own[query], 0.0, -1e30).astype(F32)
                rows[query] = jnp.where(entry == 2 * n + side, value, rows[query])
    return rows


EDGE_ROWS = (0, REDUCE - 1)
INNER_ROWS = tuple(range(1, REDUCE - 1))


def pick_rows(ref, rows, cols):
    lines = [ref[s, i * cols : (i + 1) * cols] for s in range(ref.shape[0]) for i in rows]
    return jnp.concatenate(lines, axis=0)


def attend_body(*refs, pieces, cols, slots, tiles, rows):
    edge = rows == EDGE_ROWS
    (meta, normed, stream, vec, qw, ow), refs = refs[:6], refs[6:]
    if edge:
        kvs, refs = refs[:pieces], refs[pieces:]
        queries, probs, attended, stream_two, first_row, last_row, kv_all, sbuf = refs
        for s in range(slots):
            kv_all[s] = jnp.concatenate([p[s] for p in kvs], axis=0)
    else:
        kv_all, queries, probs, attended, stream_two, normed_two, sbuf = refs
    q = nn(pick_rows(normed, rows, cols), qw[...]) + vec[QUERY_BIAS : QUERY_BIAS + 1]
    queries[...] = q.astype(BF16).reshape(queries.shape)
    for s in range(slots):
        sbuf[s] = nt(queries[s], both_heads(kv_all, s, 0))
    keys = sbuf.shape[2] // HEADS
    factor = LOG2E * (128 // HEADS) ** (-0.5)
    column = lax.broadcasted_iota(jnp.int32, (len(rows) * cols, 1), 0) % cols
    for s in range(slots):
        left, right = key_bias(meta, s, slots, tiles, keys)
        bias = jnp.where(column < cols // 2, left, right)
        for h in range(HEADS):
            span = slice(h * keys, (h + 1) * keys)
            score = sbuf[s, :, span] * factor + bias
            e = jnp.exp2(score - jnp.max(score, axis=-1, keepdims=True))
            p = e * (1.0 / jnp.sum(e, axis=-1, keepdims=True))
            probs[s, :, span] = p.astype(BF16)
    for s in range(slots):
        attended[s] = nn(probs[s], both_heads(kv_all, s, 128)).astype(BF16)
    value = pick_rows(stream, rows, cols) + nn(flat_rows(attended), ow[...])
    value = value + vec[OUTPUT_BIAS : OUTPUT_BIAS + 1]
    stream_two[...] = value.reshape(stream_two.shape)
    hat, _ = norm_stats(value, 1e-06)
    low = (hat * vec[SECOND_GAIN : SECOND_GAIN + 1] + vec[SECOND_SHIFT : SECOND_SHIFT + 1]).astype(BF16)
    if edge:
        for s, part in enumerate(by_slot(low, slots)):
            first_row[s] = part[:cols]
            last_row[s] = part[cols:]
    else:
        normed_two[...] = low.reshape(normed_two.shape)


DENSITY = 1.0 / math.sqrt(2.0 * math.pi)


def gelu_pair(x):
    twice_cdf = 1.0 + lax.erf(x * math.sqrt(0.5))
    e = jnp.exp2((x * x) * (-0.5 * LOG2E))
    return x * twice_cdf, twice_cdf + x * (e * (2.0 * DENSITY))


GROUP = 16


def fold_rows(values):
    return values[: GROUP // 2] + values[GROUP // 2 :]


def group(n):
    return slice(n * GROUP, (n + 1) * GROUP)


def group_places(r, s, q, cols, slots):
    spans = GROUP // slots
    span = cols // spans
    return pl.ds(r * span * GROUP + s * spans + q, span, GROUP)


def grouped_body(g, gp, g_t, buf, *, cols, slots):
    spans = GROUP // slots
    span = cols // spans
    line = span * GROUP
    for s in range(slots):
        for q in range(spans):
            for r in range(REDUCE):
                row = g[s, r * cols + q * span : r * cols + (q + 1) * span]
                buf[group_places(r, s, q, cols, slots), :] = row.astype(F32)
    for r in range(REDUCE):
        rows = slice(r * line, (r + 1) * line)
        gp[rows] = buf[rows].astype(BF16)
        g_t[:, rows] = gp[rows].T


def feed_body(
    meta, nt_first, nt_inner, nt_last, nt_up, nt_down, gp, g_t, hv, dw, ew, sw,
    gn_edge, gn_inner, gn_up, gn_down, dew, dsw, deb, a_out, h_out, c_out,
    abuf0, abuf1, hbuf0, hbuf1, cbuf0, cbuf1, ghbuf, gabuf, gnacc, ext, ext_t, sems,
    *, cols, slots, tiles, width,
):
    abufs, hbufs, cbufs = (abuf0, abuf1), (hbuf0, hbuf1), (cbuf0, cbuf1)
    model = ew.shape[0]
    blocks = ew.shape[1] // width
    spans = GROUP // slots
    span = cols // spans
    line = span * GROUP
    padded = line + 2 * GROUP
    rows_in = REDUCE + 2
    lane_tiles = width // 128

    def copies(b, side):
        lanes = pl.ds(pl.multiple_of(b * width, width), width)
        tiles_at = pl.ds(b * lane_tiles, lane_tiles)
        pairs = (
            (abufs, a_out.at[:, lanes]), (hbufs, h_out.at[tiles_at]), (cbufs, c_out.at[tiles_at]),
        )
        return [
            pltpu.make_async_copy(bufs[side], there, sems.at[n, side])
            for n, (bufs, there) in enumerate(pairs)
        ]

    sub = lax.broadcasted_iota(jnp.int32, (GROUP, 1), 0)
    at_slot, at_span = sub // spans, sub % spans
    same = [jnp.zeros((GROUP, 1), F32) for _ in range(3)]
    for s in range(slots):
        flags = same_flags(meta, s, slots, tiles)
        same = [jnp.where(at_slot == s, flag, mask) for flag, mask in zip(flags, same)]
    sides, same_up, same_down = same
    from_left = jnp.where(at_span == 0, 0.0, jnp.where(at_span == spans // 2, sides, 1.0))
    from_right = jnp.where(
        at_span == spans - 1, 0.0, jnp.where(at_span == spans // 2 - 1, sides, 1.0)
    )
    low_up = jnp.broadcast_to(same_up, (GROUP, 128)).astype(BF16)
    low_down = jnp.broadcast_to(same_down, (GROUP, 128)).astype(BF16)

    for s in range(slots):
        for q in range(spans):
            for r in range(rows_in):
                if 2 <= r < rows_in - 2:
                    at = (r - 2) * cols + q * span
                    row = nt_inner[s, at : at + span]
                else:
                    lines = {0: nt_up, 1: nt_first, rows_in - 2: nt_last, rows_in - 1: nt_down}
                    row = lines[r][s, q * span : (q + 1) * span]
                gnacc[group_places(r, s, q, cols, slots), :] = row.astype(F32)
    for r in range(rows_in):
        rows = slice(r * line, (r + 1) * line)
        ext[rows] = gnacc[rows].astype(BF16)
        ext_t[:model, rows] = ext[rows].T
    ext_t[model:] = jnp.ones_like(ext_t[model:])
    gnacc[...] = jnp.zeros_like(gnacc)

    def ghosts(buf, rows):
        for t in range(lane_tiles):
            for r in range(rows):
                base = r * padded
                first = buf[t, base + GROUP : base + 2 * GROUP].astype(F32)
                last = buf[t, base + line : base + line + GROUP].astype(F32)
                left = pltpu.roll(last, 1, 0) * from_left
                right = pltpu.roll(first, GROUP - 1, 0) * from_right
                buf[t, base : base + GROUP] = left.astype(BF16)
                buf[t, base + line + GROUP : base + padded] = right.astype(BF16)

    def taps_of(lanes):
        return [
            [jnp.broadcast_to(dw[a, c : c + 1, lanes], (GROUP, 128)) for c in range(3)]
            for a in range(3)
        ]

    def block(b, side):
        abuf, hbuf, cbuf = abufs[side], hbufs[side], cbufs[side]
        to_a, to_h, to_c = copies(b, side)
        at = pl.multiple_of(b * width, width)
        ewb = ew[:, pl.ds(at, width)]
        half_sw = sw[pl.ds(at, width), :] * 0.5
        bias = hv[0:1, pl.ds(at, width)]
        for r in range(rows_in):
            hid = nn(ext[r * line : (r + 1) * line], ewb) + bias
            if r == 0 or r == rows_in - 1:
                mask = same_up if r == 0 else same_down
                hid = (hid.reshape(span, GROUP, width) * mask[None]).reshape(line, width)
            for t in range(lane_tiles):
                base = r * padded + GROUP
                hbuf[t, base : base + line] = hid[:, t * 128 : (t + 1) * 128].astype(BF16)
        ghosts(hbuf, rows_in)
        to_h.start()
        for r in range(REDUCE):
            rows = slice(r * line, (r + 1) * line)
            gabuf[rows] = nt(gp[rows], half_sw)
        for t in range(lane_tiles):
            lanes = slice(t * 128, (t + 1) * 128)
            spot = pl.ds(pl.multiple_of(at + t * 128, 128), 128)
            taps = taps_of(spot)
            depth_bias = hv[1:2, spot]
            for col in range(span):
                h = [
                    [hbuf[t, group(r * (span + 2) + col + d)] for d in range(3)]
                    for r in range(rows_in)
                ]
                for i in range(REDUCE):
                    conv = None
                    for a in range(3):
                        for c in range(3):
                            term = h[i + a][c] * taps[a][c]
                            conv = term if conv is None else conv + term
                    act, slope = gelu_pair(conv.astype(F32) + depth_bias)
                    rows = group(i * span + col)
                    abuf[rows, lanes] = act.astype(BF16)
                    grad = gabuf[rows, lanes] * slope
                    cbuf[t, group(i * (span + 2) + col + 1)] = grad.astype(BF16)
        to_a.start()
        ghosts(cbuf, REDUCE)
        to_c.start()
        for t in range(lane_tiles):
            lanes = slice(t * 128, (t + 1) * 128)
            taps = taps_of(pl.ds(pl.multiple_of(at + t * 128, 128), 128))
            for col in range(span):
                gc = [
                    [cbuf[t, group(i * (span + 2) + col + d)] for d in range(3)]
                    for i in range(REDUCE)
                ]
                for r in range(rows_in):
                    gh = None
                    for a in range(3):
                        if not 0 <= r - a < REDUCE:
                            continue
                        for c in range(3):
                            term = gc[r - a][2 - c] * taps[a][c]
                            gh = term if gh is None else gh + term
                    if r == 0:
                        gh = gh * low_up
                    if r == rows_in - 1:
                        gh = gh * low_down
                    ghbuf[group(r * span + col), lanes] = gh
        for r in range(rows_in):
            rows = slice(r * line, (r + 1) * line)
            gnacc[rows] += nt(ghbuf[rows], ewb)
        grad = nn(ext_t[...], ghbuf[...])
        dew[:, pl.ds(at, width)] = grad[:model]
        deb[:, pl.ds(at, width)] = grad[model : model + 8]
        dsw[pl.ds(at, width), :] = nn(g_t[...], abuf[...]).T * 0.5

    def two_blocks(k, carry):
        for side in range(2):
            b = 2 * k + side

            @pl.when(k > 0)
            def _():
                for copy in copies(b - 2, side):
                    copy.wait()

            block(b, side)
        return carry

    lax.fori_loop(0, blocks // 2, two_blocks, 0)
    for s in range(slots):
        for q in range(spans):
            there = slice(q * span, (q + 1) * span)
            for r in range(rows_in):
                grad = gnacc[group_places(r, s, q, cols, slots), :]
                if r == 0:
                    gn_up[s, there] = grad.astype(BF16)
                elif r == rows_in - 1:
                    gn_down[s, there] = grad.astype(BF16)
                elif r in (1, rows_in - 2):
                    at = (0 if r == 1 else cols) + q * span
                    gn_edge[s, at : at + span] = grad
                else:
                    at = (r - 2) * cols + q * span
                    gn_inner[s, at : at + span] = grad
    for side in range(2):
        for copy in copies(blocks - 2 + side, side):
            copy.wait()


def depth_weight_body(hbuf, cbuf, deb, dhv, *, span):
    dhv[...] = jnp.zeros_like(dhv)
    dhv[0:1] = deb[0:1]
    per_sum = 4
    for t in range(hbuf.shape[0]):
        lanes = slice(t * 128, (t + 1) * 128)
        sums = [jnp.zeros((GROUP // 2, 128), F32) for _ in range(10)]
        for m in range(span // per_sum):
            parts = [None] * 10
            for col in range(per_sum * m, per_sum * (m + 1)):
                h = [
                    [hbuf[t, group(r * (span + 2) + col + d)] for d in range(3)]
                    for r in range(REDUCE + 2)
                ]
                for i in range(REDUCE):
                    gc = cbuf[t, group(i * (span + 2) + col + 1)]
                    terms = [gc] + [gc * h[i + a][c] for a in range(3) for c in range(3)]
                    parts = [
                        term if part is None else part + term for part, term in zip(parts, terms)
                    ]
            sums = [total + fold_rows(part.astype(F32)) for total, part in zip(sums, parts)]
        for n in range(10):
            dhv[1 + n : 2 + n, lanes] = row_sum(sums[n])


def output_body(abuf, stream_edge, stream_inner, vec, sw, out, acc, *, cols, slots):
    spans = GROUP // slots
    span = cols // spans
    line = span * GROUP
    for r in range(REDUCE):
        rows = slice(r * line, (r + 1) * line)
        acc[rows] = nn(abuf[rows], sw[...] * 0.5)
    for s in range(slots):
        for q in range(spans):
            for r in range(REDUCE):
                there = slice(r * cols + q * span, r * cols + (q + 1) * span)
                part = stream_edge if r in EDGE_ROWS else stream_inner
                at = (EDGE_ROWS if r in EDGE_ROWS else INNER_ROWS).index(r) * cols + q * span
                value = acc[group_places(r, s, q, cols, slots), :] + part[s, at : at + span]
                out[s, there] = (value + vec[SHRINK_BIAS : SHRINK_BIAS + 1]).astype(BF16)


def attend_back_body(*refs, pairs, cols, slots, rows):
    edge = rows == EDGE_ROWS
    (gn, stream_two, g, attended, probs, queries, normed, vec, ow, kv_all), refs = refs[:10], refs[10:]
    if edge:
        (up, down, dkv_in, dow_in, dqw_in, dvec_in), refs = refs[:6], refs[6:]
    (gst, gq, dow, dqw, dvec), refs = refs[:5], refs[5:]
    dkvs, (gpbuf, dsbuf, branch, gabuf) = refs[:-4], refs[-4:]
    grad = flat_rows(gn)
    if edge:
        lines = [part[s] for s in range(slots) for part in (up, down)]
        grad = grad + jnp.concatenate(lines, axis=0).astype(F32)
    hat, scale = norm_stats(flat_rows(stream_two), 1e-06)
    gi = pick_rows(g, rows, cols).astype(F32)
    value = norm_back(grad, hat, scale, vec[SECOND_GAIN : SECOND_GAIN + 1]) + gi
    gst[...] = value.reshape(gst.shape)
    low = value.astype(BF16)
    branch[...] = low
    gabuf[...] = nt(low, ow[...]).astype(BF16)
    count = len(rows) * cols
    keys = gpbuf.shape[2] // HEADS
    for s in range(slots):
        gpbuf[s] = nt(gabuf[s * count : (s + 1) * count], both_heads(kv_all, s, 128))
    for s in range(slots):
        for h in range(HEADS):
            span = slice(h * keys, (h + 1) * keys)
            p = probs[s, :, span].astype(F32)
            gp = gpbuf[s, :, span]
            inner = jnp.sum(gp * p, axis=-1, keepdims=True)
            dsbuf[s, :, span] = (p * (gp - inner)).astype(BF16)
    factor = (128 // HEADS) ** (-0.5)
    for s in range(slots):
        gq[s] = (nn(dsbuf[s], both_heads(kv_all, s, 0)) * factor).astype(BF16)

    def fold(both):
        return jnp.concatenate([both[:64, :keys], both[64:, keys:]], axis=0).T

    for s in range(slots):
        dk = fold(nn(queries[s].T, dsbuf[s])) * factor
        dv = fold(nn(gabuf[s * count : (s + 1) * count].T, probs[s]))
        dkv = jnp.concatenate([dk, dv], axis=1)
        if edge:
            dkv = (dkv + dkv_in[s]).astype(BF16)
            each = keys // pairs
            for n in range(pairs):
                dkvs[n][s] = dkv[n * each : (n + 1) * each]
        else:
            dkvs[0][s] = dkv
    dow[...] = tn(flat_rows(attended), branch[...])
    dqw[...] = tn(pick_rows(normed, rows, cols), flat_rows(gq))
    sums = {
        SECOND_GAIN: row_sum(grad * hat),
        SECOND_SHIFT: row_sum(grad),
        SHRINK_BIAS: row_sum(gi),
        OUTPUT_BIAS: row_sum(branch[...].astype(F32)),
        QUERY_BIAS: row_sum(flat_rows(gq).astype(F32)),
    }
    none = jnp.zeros((1, 128), F32)
    dvec[...] = jnp.concatenate([sums.get(n, none) for n in range(VECTORS)], axis=0)
    if edge:
        dow[...] += dow_in[...]
        dqw[...] += dqw_in[...]
        dvec[...] += dvec_in[...]


def reduce_back_body(*refs, parts, slots, tiles):
    arrived, refs = refs[:parts], refs[parts:]
    (meta, reduced, blocks, vec, rw, kw, vw, dexpand, dshrink, dhv, doutput, dquery, dvec_in) = refs[:13]
    gnb, dvec, keep, send = refs[13:]
    upper = core_place(meta, slots, tiles) == 1

    def place(chunk, first, second):
        rows = slice(chunk * 128, (chunk + 1) * 128)
        keep[rows] = jnp.where(upper, second, first)
        send[rows] = jnp.where(upper, first, second).astype(BF16)

    keys = reduced.shape[0] // slots
    dkv = arrived[-1][...].astype(F32)
    for part in arrived[:-1]:
        dkv = dkv + part[:, :keys].astype(F32)
    dkv = dkv.reshape(slots * keys, 256)
    dk, dv = dkv[:, :128], dkv[:, 128:]
    hat, scale = norm_stats(reduced[...], 1e-06)
    gain = vec[REDUCE_GAIN : REDUCE_GAIN + 1]
    rn = (hat * gain + vec[REDUCE_SHIFT : REDUCE_SHIFT + 1]).astype(BF16).astype(F32)
    dkw = tn(rn, dk, HIGHEST)
    dvw = tn(rn, dv, HIGHEST)
    grad = nt(dk, kw[...].astype(F32), HIGHEST) + nt(dv, vw[...].astype(F32), HIGHEST)
    low = norm_back(grad, hat, scale, gain).astype(BF16)
    gnb[...] = nt(low, rw[...])
    sums = {
        VALUE_BIAS: row_sum(dv),
        REDUCE_GAIN: row_sum(grad * hat),
        REDUCE_SHIFT: row_sum(grad),
        REDUCE_BIAS: row_sum(low.astype(F32)),
    }
    dvec[...] = jnp.concatenate(
        [sums.get(n, dvec_in[n : n + 1]) for n in range(VECTORS)], axis=0
    )
    spans = dexpand.shape[1] // 128
    second = [dexpand[:, t * 128 : (t + 1) * 128] for t in range(spans)]
    second += [dshrink[t * 128 : (t + 1) * 128] for t in range(spans)]
    second += [jnp.concatenate([dhv[:, t * 128 : (t + 1) * 128] for t in range(spans)], axis=0)]
    second += [doutput[...], dquery[...]]
    first = [tn(blocks[:, t * 128 : (t + 1) * 128], low) for t in range(REDUCE * REDUCE)]
    first += [dkw, dvw, jnp.zeros((128, 128), F32)]
    for chunk, (one, two) in enumerate(zip(first, second, strict=True)):
        place(chunk, one, two)


EARLY_ROWS = 19 * 128
LATE_ROWS = 3 * 128


def joined_rows(edge, inner, cols):
    lines = []
    for s in range(edge.shape[0]):
        lines += [edge[s, :cols], inner[s], edge[s, cols:]]
    return jnp.concatenate(lines, axis=0)


def embed_stats_body(
    gq_edge, gq_inner, esum, vec, qw, hat, hat_one, scale, scale_one, from_queries, *, cols
):
    gain = vec[EMBED_GAIN : EMBED_GAIN + 1]
    value, scale[...] = norm_stats(flat_rows(esum), 1e-05)
    hat[...] = value
    hat_one[...], scale_one[...] = norm_stats(
        value * gain + vec[EMBED_SHIFT : EMBED_SHIFT + 1], 1e-06
    )
    from_queries[...] = nt(joined_rows(gq_edge, gq_inner, cols), qw[...])


def embed_back_body(
    meta, gnb, from_queries, gst_edge, gst_inner, hat_in, hat_one_in, scale_in, scale_one_in, vec,
    dvec_in, ge, ge_first, dvec,
    gbuf, *, cols, slots, tiles,
):
    keys = cols // REDUCE
    cells = REDUCE * cols
    for s in range(slots):
        for a in range(REDUCE):
            for b in range(REDUCE):
                at = (a * REDUCE + b) * 128
                piece = gnb[s * keys : (s + 1) * keys, at : at + 128]
                gbuf[pl.ds(s * cells + a * cols + b, keys, REDUCE), :] = piece
    grad = gbuf[...] + from_queries[...]
    gain = vec[EMBED_GAIN : EMBED_GAIN + 1]
    hat, scale = hat_in[...], scale_in[...]
    hat_one, scale_one = hat_one_in[...], scale_one_in[...]
    sums = {FIRST_GAIN: row_sum(grad * hat_one), FIRST_SHIFT: row_sum(grad)}
    grad = norm_back(grad, hat_one, scale_one, vec[FIRST_GAIN : FIRST_GAIN + 1])
    grad = grad + joined_rows(gst_edge, gst_inner, cols)
    sums[EMBED_GAIN] = row_sum(grad * hat)
    sums[EMBED_SHIFT] = row_sum(grad)
    low = norm_back(grad, hat, scale, gain).astype(BF16)
    wide = low.astype(F32)
    sums[EMBED_BIAS] = row_sum(wide)
    dvec[...] = jnp.concatenate(
        [sums.get(n, dvec_in[n : n + 1]) for n in range(VECTORS)], axis=0
    )
    for s, part in enumerate(by_slot(wide, slots)):
        _, same_up, _ = same_flags(meta, s, slots, tiles)
        ge_first[s] = (part[:cols] * same_up).astype(BF16)
    masks = [side_mask(meta, s, slots, tiles, cols, REDUCE, False) for s in range(slots)]
    mask = jnp.concatenate(masks, axis=0)
    shifted = (pltpu.roll(wide, slots * cells - 1, 0) * mask).astype(BF16)
    ge[:, :, :128] = low.reshape(slots, cells, 128)
    ge[:, :, 128:] = shifted.reshape(slots, cells, 128)


def embed_weight_body(meta, ge, pairs, top_pairs, dvec, keep, send, *, half, slots, tiles):
    upper = core_place(meta, slots, tiles) == 1
    all_ge = ge[...].reshape(-1, ge.shape[2])
    parts = []
    for a in range(3):
        lines = [(s, 2 * i + a - 1) for s in range(slots) for i in range(REDUCE)]
        lhs = [top_pairs[s] if n < 0 else pairs[s, n] for s, n in lines]
        part = nn(jnp.concatenate(lhs, axis=1), all_ge)
        parts += [part[half:, 128:], part[:, :128]]
    dew = jnp.concatenate(parts, axis=0)
    count = 9 * half // 2
    first, second = dew[:count], dew[count:]
    keep[:count] = jnp.where(upper, second, first)
    send[:count] = jnp.where(upper, first, second).astype(BF16)
    vectors = dvec[...]
    none = jnp.zeros_like(vectors)
    end = count + VECTORS
    keep[count:end] = jnp.where(upper, none, vectors)
    send[count:end] = jnp.where(upper, vectors, none).astype(BF16)
    keep[end:] = jnp.zeros((LATE_ROWS - end, 128), F32)
    send[end:] = jnp.zeros((LATE_ROWS - end, 128), BF16)


def spread_weights(ew, a):
    none = jnp.zeros_like(ew[0, 0])
    even = jnp.concatenate([ew[a, 1], none], axis=1)
    odd = jnp.concatenate([ew[a, 2], ew[a, 0]], axis=1)
    return jnp.concatenate([even, odd], axis=0)


def mixed_columns(lines, split, half, cols):
    lines = [jnp.concatenate([part[:half], part[half:]], axis=1) for part in lines]
    mixed = nt(jnp.concatenate(lines, axis=0), split[...])
    return mixed.reshape(len(lines), half, 2 * cols)


def input_back_body(s, ge, ew, gx, split, *, cols, half):
    @pl.when(s == 0)
    def _():
        split[...] = split_columns(2 * cols)

    own = ge[0]
    upper_rows = nt(spread_weights(ew, 1), own).astype(BF16)
    inner = nt(spread_weights(ew, 2), own[:-cols]) + nt(spread_weights(ew, 0), own[cols:])
    inner = inner.astype(BF16)
    lines = []
    for i in range(REDUCE):
        cells = slice(i * cols, (i + 1) * cols)
        lines.append(upper_rows[:, cells])
        lines.append(inner[:, cells] if i < REDUCE - 1 else jnp.zeros_like(upper_rows[:, cells]))
    gx[0] = mixed_columns(lines, split, half, cols)


def last_row_body(meta, ge, below, ew, done, gx, split, *, cols, half, slots, tiles):
    s = pl.program_id(0)
    same_sides, _, _ = same_flags(meta, s, slots, tiles)

    @pl.when(s == 0)
    def _():
        split[...] = split_columns(2 * cols)

    column = lax.broadcasted_iota(jnp.int32, (cols, 1), 0)
    mask = jnp.where(column == cols - 1, 0.0, jnp.where(column == cols // 2 - 1, same_sides, 1.0))
    shifted = (pltpu.roll(below[0].astype(F32), cols - 1, 0) * mask).astype(BF16)
    under = jnp.concatenate([below[0], shifted], axis=1)
    line = nt(spread_weights(ew, 2), ge[0]) + nt(spread_weights(ew, 0), under)
    gx[0] = mixed_columns([line.astype(BF16)], split, half, cols)


def unpack_body(meta, own, other, *outs, slots, tiles, half, middle):
    upper = core_place(meta, slots, tiles) == 1
    at = middle_place(meta, slots, tiles)
    early, late = EARLY_ROWS // middle, LATE_ROWS // middle

    def pick(start, count, base, size):
        step = math.gcd(size, 128)
        mine, theirs = [], []
        for row in range(start, start + count, step):
            chunk, offset = divmod(row, size)
            where = (chunk ^ at) * (early + late) + base + offset
            rows = pl.ds(pl.multiple_of(where, math.gcd(step, 16)), step)
            mine.append(own[rows])
            theirs.append(other[rows])
        mine = jnp.concatenate(mine, axis=0).astype(F32)[:count]
        theirs = jnp.concatenate(theirs, axis=0).astype(F32)[:count]
        return jnp.where(upper, theirs, mine), jnp.where(upper, mine, theirs)

    (embed, reduce, query, key, value, output, expand, shrink, *vectors) = outs
    spans = expand.shape[1] // 128
    taps = REDUCE * REDUCE
    for chunk in range(EARLY_ROWS // 128):
        first, second = pick(chunk * 128, 128, 0, early)
        if chunk < taps:
            reduce[chunk * 128 : (chunk + 1) * 128] = first
        elif chunk == taps:
            key[...] = first
        elif chunk == taps + 1:
            value[...] = first
        if chunk < spans:
            expand[:, chunk * 128 : (chunk + 1) * 128] = second
        elif chunk < 2 * spans:
            shrink[(chunk - spans) * 128 : (chunk - spans + 1) * 128] = second
        elif chunk == 2 * spans:
            hidden_vectors = second
        elif chunk == 2 * spans + 1:
            output[...] = second
        else:
            query[...] = second
    count = 9 * half // 2
    first, second = pick(0, count + VECTORS, early, late)
    embed[:count] = first[:count]
    embed[count:] = second[:count]
    *short, expand_bias, depth, depth_bias = vectors
    for n, out in enumerate(short):
        out[...] = first[count + n]
    for t in range(spans):
        lanes = slice(t * 128, (t + 1) * 128)
        at = t * HIDDEN_VECTORS
        expand_bias[lanes] = hidden_vectors[at]
        depth_bias[lanes] = hidden_vectors[at + 1]
        for a in range(3):
            depth[a, :, lanes] = hidden_vectors[at + 2 + 3 * a : at + 5 + 3 * a]


def turned_by(array, distance):
    count = lax.axis_size("tile")
    return lax.ppermute(array, "tile", [(i, (i + distance) % count) for i in range(count)])


def crossed(array, bits):
    count = lax.axis_size("tile")
    return lax.ppermute(array, "tile", [(i, i ^ bits) for i in range(count)])


def device_levels():
    batch_count, tile_count = lax.axis_size("batch"), lax.axis_size("tile")
    batch_at, tile_at = lax.axis_index("batch"), lax.axis_index("tile")

    def routes(size, target):
        return [
            [
                (b * tile_count + t, target(b, t, turn))
                for b in range(batch_count)
                for t in range(tile_count)
            ]
            for turn in range(1, size)
        ]

    def flat(batch, tile):
        return batch * tile_count + tile

    return (
        (2, batch_at % 2, routes(2, lambda b, t, turn: flat(b ^ turn, t))),
        (
            batch_count,
            (batch_at // 2) * 2 + tile_at % 2,
            routes(batch_count, lambda b, t, turn: flat(b ^ (turn // 2 * 2), t ^ (turn % 2))),
        ),
        (
            tile_count // 2,
            tile_at // 2,
            routes(tile_count // 2, lambda b, t, turn: flat(b, t ^ (2 * turn))),
        ),
    )


AXES = ("batch", "tile")


def scatter_level(parts, level):
    size, at, turns = level
    own = lax.dynamic_index_in_dim(parts, at, 0, keepdims=False)
    sent = [
        lax.ppermute(
            lax.dynamic_index_in_dim(parts, at ^ turn, 0, keepdims=False).astype(BF16),
            AXES,
            turns[turn - 1],
        )
        for turn in range(1, size)
    ]
    return own, sent


def added(own, sent):
    for part in sent:
        own = own + part.astype(F32)
    return own


def gather_level(low, level):
    size, _, turns = level
    return jnp.stack([low] + [lax.ppermute(low, AXES, turns[turn - 1]) for turn in range(1, size)])


def from_first(blocks, level):
    size, at, _ = level
    return jnp.stack(
        [lax.dynamic_index_in_dim(blocks, at ^ n, 0, keepdims=False) for n in range(size)]
    )


def shards(
    embed_input,
    piece_image,
    embed_weight,
    embed_bias,
    embed_gain,
    embed_shift,
    first_gain,
    first_shift,
    query_weight,
    query_bias,
    reduce_weight,
    reduce_bias,
    reduce_gain,
    reduce_shift,
    key_weight,
    value_weight,
    value_bias,
    output_weight,
    output_bias,
    second_gain,
    second_shift,
    expand_weight,
    expand_bias,
    depth_weight,
    depth_bias,
    shrink_weight,
    shrink_bias,
    cotangent,
):
    source = embed_input[0].swapaxes(2, 3)
    slots, _, channels, wide_cols = source.shape
    cols = wide_cols // 2
    cells = REDUCE * cols
    keys = cols // REDUCE
    model = embed_weight.shape[3]
    hidden = expand_weight.shape[1]
    tiles = lax.axis_size("tile")
    tile_at = lax.axis_index("tile")
    pieces = tiles
    core_level, middle_level, high_level = device_levels()

    top = turned_by(embed_input[0, :, 2 * REDUCE - 1].swapaxes(1, 2), 1)
    meta = jnp.concatenate(
        [piece_image.reshape(-1), jnp.stack([tile_at, core_level[1], middle_level[1]]).astype(jnp.int32)]
    )
    vec = jnp.stack(
        [
            embed_bias, embed_gain, embed_shift, first_gain, first_shift, query_bias, reduce_bias,
            reduce_gain, reduce_shift, value_bias, output_bias, second_gain, second_shift,
            shrink_bias, shrink_bias, shrink_bias,
        ]
    ).astype(F32)
    hv = jnp.stack([expand_bias, depth_bias]).astype(F32)

    kw = dict(cols=cols)
    place = dict(slots=slots, tiles=tiles)
    flat_reduce = reduce_weight.reshape(-1, model)
    pairs, partial_sum = slot_call(
        partial(embed_own_body, **kw, **place),
        slots,
        [(meta, "smem"), (source, "far slot"), (embed_weight, "far whole")],
        [
            ((slots, 2 * REDUCE, 2 * channels, cols), BF16, "far slot"),
            ((slots, cells, model), F32, "slot"),
        ],
        [pltpu.VMEM((wide_cols, wide_cols), BF16), pltpu.VMEM((cells, 2 * model), F32)],
        name="embed_own",
        lasts=4,
        looped=True,
    )
    top_pairs, esum, stream, normed, blocks, reduced, kv = vmem_call(
        partial(embed_body, **kw, **place),
        [meta, partial_sum, top, embed_weight, vec, flat_reduce, key_weight, value_weight],
        [
            ((slots, 2 * channels, cols), BF16),
            ((slots, cells, model), F32),
            ((slots, cells, model), F32),
            ((slots, cells, model), BF16),
            ((slots * keys, REDUCE * REDUCE * model), BF16),
            ((slots * keys, model), F32),
            ((slots * keys, 2 * model), BF16),
        ],
        [pltpu.VMEM((slots * cells, model), F32)],
        name="embed",
    )

    grad_out = cotangent[0].reshape(slots, cells, model)
    all_cells = slots * cells
    gp, g_t = pl.pallas_call(
        partial(grouped_body, cols=cols, slots=slots),
        out_shape=[
            jax.ShapeDtypeStruct((all_cells, model), BF16),
            jax.ShapeDtypeStruct((model, all_cells), BF16),
        ],
        scratch_shapes=[pltpu.VMEM((all_cells, model), F32)],
        compiler_params=pltpu.CompilerParams(vmem_limit_bytes=VMEM_BYTES),
        cost_estimate=cost(3),
        name="grouped",
    )(grad_out)

    kv = kv.reshape(slots, keys, 2 * model)
    crossing = {n: crossed(kv, n) for n in range(tiles - 1, 0, -1)}
    kvs = [kv] + [crossing[n] for n in range(1, tiles)]
    kvs, gp, g_t = lax.optimization_barrier((kvs, gp, g_t))

    all_keys = keys * tiles
    part_cells = cells // 2

    def attend(rows, sources, results):
        return vmem_call(
            partial(attend_body, pieces=pieces, rows=rows, **kw, **place),
            [meta, normed, stream, vec, query_weight, output_weight] + sources,
            [
                ((slots, part_cells, model), BF16),
                ((slots, part_cells, HEADS * all_keys), BF16),
                ((slots, part_cells, model), BF16),
                ((slots, part_cells, model), F32),
            ]
            + results,
            [pltpu.VMEM((slots, part_cells, HEADS * all_keys), F32)],
            name="attend",
        )

    *kept_edge, first_row, last_row, kv_all = attend(
        EDGE_ROWS,
        kvs,
        [
            ((slots, cols, model), BF16),
            ((slots, cols, model), BF16),
            ((slots, all_keys, 2 * model), BF16),
        ],
    )
    row_up = turned_by(last_row, 1)
    row_down = turned_by(first_row, -1)
    *kept_inner, normed_inner = attend(
        INNER_ROWS, [kv_all], [((slots, part_cells, model), BF16)]
    )
    row_up, row_down, normed_inner = lax.optimization_barrier((row_up, row_down, normed_inner))
    width = 256
    vmem = pl.BlockSpec(memory_space=pltpu.VMEM)
    ext_cells = slots * (cells + 2 * cols)
    lane_tiles = width // 128
    hidden_blocks = (hidden // width,)
    by_lanes = lambda shape: pl.BlockSpec((shape[0], width), lambda b: (0, b))
    by_tiles = lambda shape: pl.BlockSpec((lane_tiles,) + tuple(shape[1:]), lambda b: (b, 0, 0))
    hidden_shape = (hidden // 128, ext_cells + 2 * GROUP * (REDUCE + 2), 128)
    conv_shape = (hidden // 128, all_cells + 2 * GROUP * REDUCE, 128)
    (
        gn_edge, gn_inner, gn_up, gn_down, d_expand, d_shrink, d_expand_bias, active, hidden_cells, grad_conv,
    ) = pl.pallas_call(
        partial(feed_body, width=width, **kw, **place),
        in_specs=[smem()] + [vmem] * 11,
        out_specs=[vmem] * 7 + [pl.BlockSpec(memory_space=pltpu.HBM)] * 3,
        out_shape=[
            jax.ShapeDtypeStruct((slots, part_cells, model), F32),
            jax.ShapeDtypeStruct((slots, part_cells, model), F32),
            jax.ShapeDtypeStruct((slots, cols, model), BF16),
            jax.ShapeDtypeStruct((slots, cols, model), BF16),
            jax.ShapeDtypeStruct((model, hidden), F32),
            jax.ShapeDtypeStruct((hidden, model), F32),
            jax.ShapeDtypeStruct((8, hidden), F32),
            far((all_cells, hidden), BF16),
            far(hidden_shape, BF16),
            far(conv_shape, BF16),
        ],
        scratch_shapes=[pltpu.VMEM((all_cells, width), BF16)] * 2
        + [pltpu.VMEM((lane_tiles,) + hidden_shape[1:], BF16)] * 2
        + [pltpu.VMEM((lane_tiles,) + conv_shape[1:], BF16)] * 2
        + [
            pltpu.VMEM((ext_cells, width), BF16),
            pltpu.VMEM((all_cells, width), F32),
            pltpu.VMEM((ext_cells, model), F32),
            pltpu.VMEM((ext_cells, model), BF16),
            pltpu.VMEM((model + GROUP, ext_cells), BF16),
            pltpu.SemaphoreType.DMA((3, 2)),
        ],
        compiler_params=pltpu.CompilerParams(vmem_limit_bytes=VMEM_BYTES),
        cost_estimate=cost(18),
        name="feed_forward",
    )(
        meta, first_row, normed_inner, last_row, row_up, row_down, gp, g_t, hv, depth_weight,
        expand_weight, shrink_weight,
    )

    from_up = turned_by(gn_down, 1)
    from_down = turned_by(gn_up, -1)
    pairs_of_tiles = tiles // 2

    def attend_back(rows, grad, kept, sources, results):
        queries, probs, attended, stream_two = kept
        return vmem_call(
            partial(attend_back_body, pairs=pairs_of_tiles, rows=rows, slots=slots, **kw),
            [
                grad, stream_two, grad_out, attended, probs, queries, normed, vec, output_weight,
                kv_all,
            ]
            + sources,
            [
                ((slots, part_cells, model), F32),
                ((slots, part_cells, model), BF16),
                ((model, model), F32),
                ((model, model), F32),
                ((VECTORS, model), F32),
            ]
            + results,
            [
                pltpu.VMEM((slots, part_cells, HEADS * all_keys), F32),
                pltpu.VMEM((slots, part_cells, HEADS * all_keys), BF16),
                pltpu.VMEM((slots * part_cells, model), BF16),
                pltpu.VMEM((slots * part_cells, model), BF16),
            ],
            name="attend_back",
        )

    gst_inner, gq_inner, *sums, dkv_inner = attend_back(
        INNER_ROWS, gn_inner, kept_inner, [], [((slots, all_keys, 2 * model), F32)]
    )
    from_up, from_down, dkv_inner = lax.optimization_barrier((from_up, from_down, dkv_inner))
    gst_edge, gq_edge, d_output, d_query, dvec_a, *dkvs = attend_back(
        EDGE_ROWS,
        gn_edge,
        kept_edge,
        [from_up, from_down, dkv_inner] + sums,
        [((slots, 2 * keys, 2 * model), BF16)] * pairs_of_tiles,
    )
    crossing = {n: crossed(dkvs[n], 2 * n) for n in range(pairs_of_tiles - 1, 0, -1)}
    own_dkvs = [dkvs[0]] + [crossing[n] for n in range(1, pairs_of_tiles)]
    d_hv = pl.pallas_call(
        partial(depth_weight_body, span=cols * slots // GROUP),
        grid=hidden_blocks,
        in_specs=[by_tiles(hidden_shape), by_tiles(conv_shape), by_lanes((8, hidden))],
        out_specs=by_lanes((HIDDEN_VECTORS, hidden)),
        out_shape=jax.ShapeDtypeStruct((HIDDEN_VECTORS, hidden), F32),
        compiler_params=params(),
        cost_estimate=cost(6),
        name="depth_weights",
    )(from_far(hidden_cells), from_far(grad_conv), d_expand_bias)
    own_dkvs, d_hv = lax.optimization_barrier((own_dkvs, d_hv))
    for_mate = own_dkvs[0][:, keys:].astype(F32)
    for part in own_dkvs[1:]:
        for_mate = for_mate + part[:, keys:].astype(F32)
    from_mate = crossed(for_mate.astype(BF16), 1)
    stats = vmem_call(
        partial(embed_stats_body, **kw),
        [gq_edge, gq_inner, esum, vec, query_weight],
        [
            ((all_cells, model), F32),
            ((all_cells, model), F32),
            ((all_cells, 1), F32),
            ((all_cells, 1), F32),
            ((all_cells, model), F32),
        ],
        name="embed_stats",
        lasts=3,
    )
    from_mate, stats = lax.optimization_barrier((from_mate, stats))
    own_dkvs.append(from_mate)

    gnb, dvec_b, keep, send = pl.pallas_call(
        partial(reduce_back_body, parts=len(own_dkvs), **place),
        in_specs=[vmem] * len(own_dkvs) + [smem()] + [vmem] * 12,
        out_specs=[vmem] * 4,
        out_shape=[
            jax.ShapeDtypeStruct((slots * keys, REDUCE * REDUCE * model), F32),
            jax.ShapeDtypeStruct((VECTORS, model), F32),
            jax.ShapeDtypeStruct((EARLY_ROWS, 128), F32),
            jax.ShapeDtypeStruct((EARLY_ROWS, 128), BF16),
        ],
        compiler_params=pltpu.CompilerParams(vmem_limit_bytes=VMEM_BYTES),
        cost_estimate=cost(3),
        name="reduce_back",
    )(
        *own_dkvs, meta, reduced, blocks, vec, flat_reduce, key_weight, value_weight,
        d_expand, d_shrink, d_hv, d_output, d_query, dvec_a,
    )
    got = lax.ppermute(send, AXES, core_level[2][0])

    ge, ge_first, dvec_c = vmem_call(
        partial(embed_back_body, **kw, **place),
        [
            meta, gnb, stats[4], gst_edge, gst_inner, *stats[:4], vec, dvec_b,
        ],
        [
            ((slots, cells, 2 * model), BF16),
            ((slots, cols, model), BF16),
            ((VECTORS, model), F32),
        ],
        [pltpu.VMEM((slots * cells, model), F32)],
        name="embed_back",
    )
    below = turned_by(ge_first, -1)
    late_keep, late_send = pl.pallas_call(
        partial(embed_weight_body, half=channels, **place),
        in_specs=[smem()] + [vmem] * 4,
        out_specs=[vmem] * 2,
        out_shape=[
            jax.ShapeDtypeStruct((LATE_ROWS, 128), F32),
            jax.ShapeDtypeStruct((LATE_ROWS, 128), BF16),
        ],
        compiler_params=pltpu.CompilerParams(vmem_limit_bytes=VMEM_BYTES),
        cost_estimate=cost(3),
        name="embed_weights",
    )(meta, ge, pairs, top_pairs, dvec_c)
    late_got = lax.ppermute(late_send, AXES, core_level[2][0])

    middle, high = middle_level[0], high_level[0]
    parts = jnp.concatenate(
        [
            (keep + got.astype(F32)).reshape(middle, -1, 128),
            (late_keep + late_got.astype(F32)).reshape(middle, -1, 128),
        ],
        axis=1,
    )
    (grad_input,) = slot_call(
        partial(input_back_body, half=channels, **kw),
        slots,
        [(ge, "slot"), (embed_weight, "whole")],
        [(source.shape, F32, "slot")],
        [pltpu.VMEM((wide_cols, wide_cols), BF16)],
        name="input_back",
    )
    own, sent = scatter_level(parts, middle_level)
    sent, grad_input = lax.optimization_barrier((sent, grad_input))
    own = added(own, sent)
    own, sent = scatter_level(own.reshape(high, -1, 128), high_level)
    last_line = pl.BlockSpec((1, 1, channels, wide_cols), lambda s: (s, 2 * REDUCE - 1, 0, 0))
    grad_input = pl.pallas_call(
        partial(last_row_body, half=channels, **kw, **place),
        grid=(slots,),
        in_specs=[
            smem(),
            pl.BlockSpec((1, cols, 2 * model), lambda s: (s, REDUCE - 1, 0)),
            per_slot(below.shape),
            whole(embed_weight.shape),
            pl.BlockSpec(memory_space=pl.ANY),
        ],
        out_specs=last_line,
        out_shape=jax.ShapeDtypeStruct(source.shape, F32),
        scratch_shapes=[pltpu.VMEM((wide_cols, wide_cols), BF16)],
        input_output_aliases={4: 0},
        compiler_params=params(),
        cost_estimate=cost(2),
        name="last_row",
    )(meta, ge, below, embed_weight, grad_input)
    sent, grad_input = lax.optimization_barrier((sent, grad_input))
    low = added(own, sent).astype(BF16)
    low = from_first(gather_level(low, high_level), high_level).reshape(-1, 128)
    out = pl.pallas_call(
        partial(output_body, cols=cols, slots=slots),
        out_shape=jax.ShapeDtypeStruct((slots, cells, model), BF16),
        scratch_shapes=[pltpu.VMEM((all_cells, model), F32)],
        compiler_params=pltpu.CompilerParams(vmem_limit_bytes=VMEM_BYTES),
        cost_estimate=cost(3),
        name="output",
    )(active, kept_edge[3], kept_inner[3], vec, shrink_weight)
    gathered = gather_level(low, middle_level)
    gathered, out = lax.optimization_barrier((gathered, out))
    low = gathered.reshape(-1, 128)
    other = lax.ppermute(low, AXES, core_level[2][0])

    shapes = [(9 * channels, model), (REDUCE * REDUCE * model, model)]
    shapes += [(model, model)] * 4 + [(model, hidden), (hidden, model)]
    shapes += [(model,)] * 14 + [(hidden,), (3, 3, hidden), (hidden,)]
    results = pl.pallas_call(
        partial(unpack_body, half=channels, middle=middle, **place),
        in_specs=[smem()] + [vmem] * 2,
        out_specs=[vmem] * len(shapes),
        out_shape=[jax.ShapeDtypeStruct(shape, F32) for shape in shapes],
        compiler_params=pltpu.CompilerParams(vmem_limit_bytes=VMEM_BYTES),
        cost_estimate=cost(3),
        name="unpack",
    )(meta, low, other)
    (s_embed, s_reduce, s_query, s_key, s_value, s_output, s_expand, s_shrink) = results[:8]
    vectors = results[8:22]
    s_expand_bias, s_depth, s_depth_bias = results[22:]
    return (
        out.reshape(cotangent.shape),
        grad_input.swapaxes(2, 3)[None],
        s_embed.reshape(embed_weight.shape),
        vectors[EMBED_BIAS],
        vectors[EMBED_GAIN],
        vectors[EMBED_SHIFT],
        vectors[FIRST_GAIN],
        vectors[FIRST_SHIFT],
        s_query,
        vectors[QUERY_BIAS],
        s_reduce.reshape(reduce_weight.shape),
        vectors[REDUCE_BIAS],
        vectors[REDUCE_GAIN],
        vectors[REDUCE_SHIFT],
        s_key,
        s_value,
        vectors[VALUE_BIAS],
        s_output,
        vectors[OUTPUT_BIAS],
        vectors[SECOND_GAIN],
        vectors[SECOND_SHIFT],
        s_expand,
        s_expand_bias,
        s_depth,
        s_depth_bias,
        s_shrink,
        vectors[SHRINK_BIAS],
    )


def solution(mesh):
    shard_rows = P("batch", None, "tile", None, None)
    in_specs = (shard_rows, P("batch", None, None, None)) + (P(),) * 25 + (shard_rows,)
    out_specs = (shard_rows, shard_rows) + (P(),) * 25
    return jax.shard_map(shards, mesh=mesh, in_specs=in_specs, out_specs=out_specs, check_vma=False)
```
